32 devices in a mesh: tm: 4 (over z), space: 8 (over y, x, core).
Axes of the slice: x: 2, y: 2, z: 4, core: 2. Of those that a mesh axis runs over, the one named last changes fastest.
Arguments:
- initial: float32 [32, 128, 512], P('space'), may hold values from -6 to 6
- prior: float32 [4, 32, 128, 512], P('tm', 'space'), may hold values from -6 to 6
- conductivity: float32 [32, 128, 512], P('space'), may hold values from 0.1 to 1
Outputs:
- update: float32 [4, 32, 128, 512], P('tm', 'space')
- coarse_end: float32 [4, 16, 64, 256], P('tm', 'space')
The draws below stay inside these ranges and needn't reach their ends.
All inputs are finite; a program needn't handle non-finite values.
Results may differ from the reference program's by a relative error of at most 0.00002.
Values sent between devices are 32-bit elements; how exact they have to be, the bound alone decides.
No kernel may reach another device: no remote copies, remote signals or barrier semaphores. Data moves between devices by JAX's collectives and lax.ppermute only.
A program may use at most 64 MiB of HBM per device.

```python
import math
import jax
import jax.numpy as jnp
from jax import lax

NY = 128
NZ = 512
FINE_STEPS = 4
COARSE_STEPS = 2
N_INTERVALS = 4
NX = 32


def block_levels(rng, shape, cuts, smallest, top_value):
    gain = 1.0
    for dim, shards_of in cuts:
        steps = jax.random.uniform(jax.random.fold_in(jax.random.fold_in(rng, 6), dim), (shards_of,), jnp.float32, smallest / len(cuts), top_value / len(cuts))
        gain = gain * jnp.repeat(jnp.exp(steps), shape[dim] // shards_of).reshape((-1,) + (1,) * (len(shape) - 1 - dim))
    return gain


def scatter_about(stream_key, extent, scale, reach, shards=(), kind=jnp.bfloat16):
    values = jax.random.normal(stream_key, extent, jnp.float32) * scale
    if len(shards) > 0:
        values = block_levels(stream_key, extent, shards, -0.22, 0.18) * values
    return jnp.clip(values, min=-reach, max=reach).astype(kind)


def setup_inputs(seed: int = 0) -> dict:
    splits = jax.random.split(jax.random.key(seed), 4)
    initial = scatter_about(splits[0], (NX, NY, NZ), 1.0, 6.0, ((0, 8),), jnp.float32)
    prior = scatter_about(splits[1], (N_INTERVALS, NX, NY, NZ), 1.0, 6.0, ((0, 4), (1, 8)), jnp.float32)
    conductivity = jnp.clip(jnp.exp(math.log(1.0) - 2.3025851 * jax.random.uniform(splits[2], (NX, NY, NZ), jnp.float32) ** block_levels(splits[2], (NX, NY, NZ), ((0, 8),), -0.2, 0.2)), 0.1, 1.0)
    return dict(initial=initial, prior=prior, conductivity=conductivity)


fine_rate = 0.16


def neighbour(field, dim, forward):
    count = field.shape[dim]
    edge_shape = list(field.shape)
    edge_shape[dim] = 1
    zeros = jnp.zeros(edge_shape, field.dtype)
    if forward:
        return jnp.concatenate([lax.slice_in_dim(field, 1, count, axis=dim), zeros], axis=dim)
    return jnp.concatenate([zeros, lax.slice_in_dim(field, 0, count - 1, axis=dim)], axis=dim)


def face_terms(padded_cond):
    center = padded_cond[1:-1]
    return (0.5 * (center + padded_cond[2:]), 0.5 * (center + padded_cond[:-2]),
            0.5 * (center + neighbour(center, 1, True)), 0.5 * (center + neighbour(center, 1, False)),
            0.5 * (center + neighbour(center, 2, True)), 0.5 * (center + neighbour(center, 2, False)))


def local_step(padded_state, faces, factor):
    center = padded_state[1:-1]
    flux_sum = faces[0] * (padded_state[2:] - center)
    flux_sum = flux_sum + faces[1] * (padded_state[:-2] - center)
    flux_sum = flux_sum + faces[2] * (neighbour(center, 1, True) - center)
    flux_sum = flux_sum + faces[3] * (neighbour(center, 1, False) - center)
    flux_sum = flux_sum + faces[4] * (neighbour(center, 2, True) - center)
    flux_sum = flux_sum + faces[5] * (neighbour(center, 2, False) - center)
    return center + factor * flux_sum


def pad_rows(field):
    return jnp.pad(field, ((1, 1), (0, 0), (0, 0)))


def restrict(field):
    paired = field[0::2] + field[1::2]
    paired = paired[:, 0::2] + paired[:, 1::2]
    paired = paired[:, :, 0::2] + paired[:, :, 1::2]
    return paired * 0.125


def prolong(field):
    return jnp.repeat(jnp.repeat(jnp.repeat(field, 2, axis=0), 2, axis=1), 2, axis=2)


def reference(initial, prior, conductivity):
    fine_faces = face_terms(pad_rows(conductivity))
    coarse_faces = face_terms(pad_rows(restrict(conductivity)))

    def coarse(state):
        for step in range(COARSE_STEPS):
            state = local_step(pad_rows(state), coarse_faces, fine_rate * 0.5)
        return state

    current = restrict(initial)
    updates = []
    tails = []
    for section in range(N_INTERVALS):
        opening = initial if section == 0 else prior[section - 1]
        fine_state = opening
        for step in range(FINE_STEPS):
            fine_state = local_step(pad_rows(fine_state), fine_faces, fine_rate)
        predicted = coarse(restrict(opening))
        delta = fine_state - prolong(predicted)
        reduced = restrict(delta)
        propagated = coarse(current)
        coarse_tail = propagated + reduced
        updates.append((prolong(propagated) + delta) - prior[section])
        tails.append(coarse_tail)
        current = coarse_tail
    return jnp.stack(updates), jnp.stack(tails)
```

```python
import jax
import jax.numpy as jnp
from jax import lax
from jax.experimental import pallas as pl
from jax.experimental.pallas import tpu as pltpu
from jax.sharding import PartitionSpec as P

FINE_STEPS = 4
COARSE_STEPS = 2
FINE_RATE = 0.16
HALF_FINE = 0.5 * FINE_RATE
HALF_COARSE = 0.25 * FINE_RATE
TILE = 16
LANES = 128

VMEM = pl.BlockSpec(memory_space=pltpu.VMEM)
SMEM = pl.BlockSpec(memory_space=pltpu.SMEM)
F32 = jnp.float32


def call(body, out_shapes, operands, specs=None, scratch=(), flops=0):
    operands = list(operands)
    specs = specs or [VMEM] * len(operands)
    return pl.pallas_call(
        body,
        out_shape=[jax.ShapeDtypeStruct(s, F32) for s in out_shapes],
        in_specs=specs,
        out_specs=[VMEM] * len(out_shapes),
        scratch_shapes=list(scratch),
        compiler_params=pltpu.CompilerParams(vmem_limit_bytes=32 * 1024 * 1024),
    )(*operands)


def lane_scratch(rows, columns):
    return pltpu.VMEM((columns // LANES, rows, LANES), F32)


def split3(x):
    hi = x.astype(jnp.bfloat16)
    rest = x - hi.astype(F32)
    mid = rest.astype(jnp.bfloat16)
    low = (rest - mid.astype(F32)).astype(jnp.bfloat16)
    return hi, mid, low


def dot3(x, m):
    parts = [jnp.dot(p, m, preferred_element_type=F32) for p in split3(x)]
    return parts[0] + (parts[1] + parts[2])


def pair_matrix(fine, coarse, value):
    rows = lax.broadcasted_iota(jnp.int32, (fine, coarse), 0)
    cols = lax.broadcasted_iota(jnp.int32, (fine, coarse), 1)
    return jnp.where((rows >> 1) == cols, value, 0.0).astype(jnp.bfloat16)


def repeat_matrix(coarse, fine):
    rows = lax.broadcasted_iota(jnp.int32, (coarse, fine), 0)
    cols = lax.broadcasted_iota(jnp.int32, (coarse, fine), 1)
    return jnp.where(rows == (cols >> 1), 1.0, 0.0).astype(jnp.bfloat16)


def restrict_planes(first, second, scratch, matrix):
    blocks, ny, _ = scratch.shape
    sums = dot3(first + second, matrix)
    parts = []
    for b in range(blocks):
        scratch[b] = sums[:, b * LANES:(b + 1) * LANES]
        parts.append(scratch[b, pl.ds(0, ny // 2, 2), :] + scratch[b, pl.ds(1, ny // 2, 2), :])
    return jnp.concatenate(parts, axis=1)


def rows_above(ref, index, a, size):
    if a == 0:
        return pltpu.roll(ref[index + (slice(0, size),)], 1, 0)
    return ref[index + (slice(a - 1, a + size - 1),)]


def rows_below(ref, index, a, size, ny):
    if a + size == ny:
        return pltpu.roll(ref[index + (slice(a, a + size),)], size - 1, 0)
    return ref[index + (slice(a + 1, a + size + 1),)]


def face_coefficients(k, above, below, half, a, size, ny, nz):
    row = lax.broadcasted_iota(jnp.int32, (size, nz), 0) + a
    col = lax.broadcasted_iota(jnp.int32, (size, nz), 1)
    up_face = half * (k + jnp.where(row == 0, 0.0, above))
    down_face = half * (k + jnp.where(row == ny - 1, 0.0, below))
    right = pltpu.roll(k, nz - 1, 1)
    left = pltpu.roll(k, 1, 1)
    right_face = half * (k + jnp.where(col == nz - 1, 0.0, right))
    left_face = half * (k + jnp.where(col == 0, 0.0, left))
    total = (up_face + down_face) + (right_face + left_face)
    return (
        jnp.where(row == 0, 0.0, up_face),
        jnp.where(row == ny - 1, 0.0, down_face),
        jnp.where(col == nz - 1, 0.0, right_face),
        total,
    )


def prepare_fine(cond):
    nx, ny, nz = cond.shape

    def body(k_ref, kx, up, down, right, diag, coarse, scratch):
        for p in range(nx):
            for a in range(0, ny, TILE):
                s = slice(a, a + TILE)
                k = k_ref[p, s]
                u, d, r, total = face_coefficients(
                    k, rows_above(k_ref, (p,), a, TILE), rows_below(k_ref, (p,), a, TILE, ny),
                    HALF_FINE, a, TILE, ny, nz)
                up[p, s], down[p, s], right[p, s] = u, d, r
                if p > 0:
                    total = total + kx[p - 1, s]
                if p < nx - 1:
                    face = HALF_FINE * (k + k_ref[p + 1, s])
                    kx[p, s] = face
                    total = total + face
                diag[p, s] = 1.0 - total
        matrix = pair_matrix(nz, nz // 2, 0.125)
        for q in range(nx // 2):
            coarse[q] = restrict_planes(k_ref[2 * q], k_ref[2 * q + 1], scratch, matrix)

    full = (nx, ny, nz)
    return call(
        body,
        [(nx - 1, ny, nz), full, full, full, full, (nx // 2, ny // 2, nz // 2)],
        [cond],
        scratch=[lane_scratch(ny, nz // 2)],
    )


def restricted(field):
    nx, ny, nz = field.shape

    def body(f_ref, out, scratch):
        matrix = pair_matrix(nz, nz // 2, 0.125)
        for q in range(nx // 2):
            out[q] = restrict_planes(f_ref[2 * q], f_ref[2 * q + 1], scratch, matrix)

    return call(
        body, [(nx // 2, ny // 2, nz // 2)], [field], scratch=[lane_scratch(ny, nz // 2)]
    )[0]


def fine_step(ends, planes, before, after, cond, cond_before, cond_after, coefficients, last_prior=None):
    nx = len(planes)
    ny, nz = planes[0].shape
    final = last_prior is not None

    def body(*refs):
        ends_ref = refs[0]
        v = refs[1:1 + nx]
        lo, hi, k_ref, k_lo, k_hi, kx, up, down, right, diag = refs[1 + nx:11 + nx]
        rest = refs[11 + nx:]
        has_lo, has_hi = ends_ref[0] > 0, ends_ref[1] > 0
        if final:
            prior_ref, out_ref, jump_ref, scratch = rest
            out = [out_ref.at[p] for p in range(nx)]
        else:
            out = rest
        for p in range(nx):
            for a in range(0, ny, TILE):
                s = slice(a, a + TILE)
                c = v[p][s]
                total = diag[p, s] * c
                total = total + up[p, s] * rows_above(v[p], (), a, TILE)
                total = total + down[p, s] * rows_below(v[p], (), a, TILE, ny)
                r = right[p, s]
                total = total + r * pltpu.roll(c, nz - 1, 1)
                total = total + pltpu.roll(r * c, 1, 1)
                if p > 0:
                    total = total + kx[p - 1, s] * v[p - 1][s]
                else:
                    face = HALF_FINE * (k_ref[p, s] + jnp.where(has_lo, k_lo[0, s], 0.0))
                    total = total + face * (jnp.where(has_lo, lo[s], 0.0) - c)
                if p < nx - 1:
                    total = total + kx[p, s] * v[p + 1][s]
                else:
                    face = HALF_FINE * (k_ref[p, s] + jnp.where(has_hi, k_hi[0, s], 0.0))
                    total = total + face * (jnp.where(has_hi, hi[s], 0.0) - c)
                out[p][s] = total
        if final:
            matrix = pair_matrix(nz, nz // 2, 0.125)
            for q in range(nx // 2):
                jump_ref[q] = restrict_planes(out[2 * q][...], out[2 * q + 1][...], scratch, matrix) - prior_ref[q]

    operands = [ends, *planes, before, after, cond, cond_before, cond_after, *coefficients]
    if final:
        operands.append(last_prior)
        shapes = [(nx, ny, nz), (nx // 2, ny // 2, nz // 2)]
        scratch = [lane_scratch(ny, nz // 2)]
    else:
        shapes = [(ny, nz)] * nx
        scratch = []
    return call(body, shapes, operands, [SMEM] + [VMEM] * (len(operands) - 1), scratch)


def coarse_coefficients(ends, own, before, after):
    nx, ny, nz = own.shape
    planes = nx + 2

    def body(ends_ref, k_own, k_lo, k_hi, kx, up, down, right, diag):
        has_lo, has_hi = ends_ref[0] > 0, ends_ref[1] > 0

        def plane(i):
            if i < 2:
                return jnp.where(has_lo, k_lo[nx - 2 + i], 0.0)
            if i < nx + 2:
                return k_own[i - 2]
            return jnp.where(has_hi, k_hi[i - nx - 2], 0.0)

        for i in range(planes + 1):
            kx[i] = HALF_COARSE * (plane(i) + plane(i + 1))
        for p in range(planes):
            k = plane(p + 1)
            u, d, r, total = face_coefficients(
                k, pltpu.roll(k, 1, 0), pltpu.roll(k, ny - 1, 0), HALF_COARSE, 0, ny, ny, nz)
            up[p], down[p], right[p] = u, d, r
            diag[p] = 1.0 - (total + kx[p] + kx[p + 1])

    full = (planes, ny, nz)
    return call(
        body, [(planes + 1, ny, nz)] + [full] * 4, [ends, own, before, after], [SMEM] + [VMEM] * 3
    )


def coarse_sweep_step(ends, own, before, after, coefficients, jump=None):
    nx, ny, nz = own.shape

    def body(ends_ref, d_own, d_lo, d_hi, kx, up, down, right, diag, *rest):
        has_lo, has_hi = ends_ref[0] > 0, ends_ref[1] > 0

        def step(v, i):
            c = v[1]
            total = diag[i] * c + kx[i] * v[0] + kx[i + 1] * v[2]
            total = total + up[i] * pltpu.roll(c, 1, 0) + down[i] * pltpu.roll(c, ny - 1, 0)
            return total + right[i] * pltpu.roll(c, nz - 1, 1) + pltpu.roll(right[i] * c, 1, 1)

        lo = [jnp.where(has_lo, d_lo[nx - 2 + i], 0.0) for i in range(2)]
        hi = [jnp.where(has_hi, d_hi[i], 0.0) for i in range(2)]
        v = lo + [d_own[i] for i in range(nx)] + hi
        w = [step(v[i:i + 3], i) for i in range(nx + 2)]
        w[0] = jnp.where(has_lo, w[0], 0.0)
        w[-1] = jnp.where(has_hi, w[-1], 0.0)
        for i in range(nx):
            e = step(w[i:i + 3], i + 1)
            rest[-1 if jump is None else -2][i] = e
            if jump is not None:
                rest[-1][i] = e + rest[0][i]

    operands = [ends, own, before, after, *coefficients]
    shapes = [own.shape]
    if jump is not None:
        operands.append(jump)
        shapes.append(own.shape)
    return call(body, shapes, operands, [SMEM] + [VMEM] * (len(operands) - 1))


def finish(fine, prior, correction):
    nx, ny, nz = fine.shape

    def body(f_ref, p_ref, e_ref, update, tail, scratch, wide):
        matrix = pair_matrix(nz, nz // 2, 0.125)
        spread = repeat_matrix(nz // 2, nz)
        for q in range(nx // 2):
            e = e_ref[q]
            tail[q] = e + restrict_planes(f_ref[2 * q], f_ref[2 * q + 1], scratch, matrix)
            row = dot3(e, spread)
            for b in range(nz // LANES):
                s = slice(b * LANES, (b + 1) * LANES)
                wide[b, pl.ds(0, ny // 2, 2), :] = row[:, s]
                wide[b, pl.ds(1, ny // 2, 2), :] = row[:, s]
                for p in (2 * q, 2 * q + 1):
                    update[p, :, s] = (f_ref[p, :, s] + wide[b]) - p_ref[p, :, s]

    return call(
        body,
        [(nx, ny, nz), (nx // 2, ny // 2, nz // 2)],
        [fine, prior, correction],
        scratch=[lane_scratch(ny, nz // 2), lane_scratch(ny, nz)],
    )


def ring(block, axis, distance):
    size = lax.axis_size(axis)
    return lax.ppermute(block, axis, [(i, (i + distance) % size) for i in range(size)])


def from_sides(last, first):
    return ring(last, "space", 1), ring(first, "space", -1)


def shards(initial, prior, conductivity):
    t, times = lax.axis_index("tm"), lax.axis_size("tm")
    s, blocks = lax.axis_index("space"), lax.axis_size("space")
    ends = jnp.stack([s > 0, s < blocks - 1]).astype(jnp.int32)
    own_prior = prior[0]
    nx = initial.shape[0]
    home = times - 1

    opening = jnp.where(t == home, initial, own_prior)
    planes = [opening[p] for p in range(nx)]
    cond_before, cond_after = from_sides(conductivity[nx - 1:], conductivity[:1])

    *coefficients, coarse_cond = prepare_fine(conductivity)
    next_prior = ring(restricted(own_prior), "tm", -1)
    coarse_before, coarse_after = from_sides(coarse_cond, coarse_cond)
    coarse_coef = coarse_coefficients(ends, coarse_cond, coarse_before, coarse_after)

    for step in range(FINE_STEPS):
        before, after = from_sides(planes[-1], planes[0])
        planes = fine_step(
            ends, planes, before, after, conductivity, cond_before, cond_after, coefficients,
            next_prior if step == FINE_STEPS - 1 else None)
    fine, jump = planes

    jumps = [jump] + [
        lax.ppermute(jump, "tm", [(n - 1, home)]) for n in range(1, times - 1)
    ]
    own_fine = ring(fine, "tm", 1)
    state = jump
    correction = jnp.zeros_like(jump)
    for n in range(1, times):
        before, after = from_sides(state, state)
        swept = coarse_sweep_step(
            ends, state, before, after, coarse_coef, jumps[n] if n < home else None)
        if n < home:
            e, state = swept
            arrived = lax.ppermute(e, "tm", [(home, n)])
        else:
            arrived = swept[0]
        correction = jnp.where(t == n, arrived, correction)
    update, tail = finish(own_fine, own_prior, correction)
    return update[None], tail[None]


def solution(mesh):
    return jax.shard_map(
        shards,
        mesh=mesh,
        in_specs=(P("space", None, None), P("tm", "space", None, None), P("space", None, None)),
        out_specs=(P("tm", "space", None, None), P("tm", "space", None, None)),
        check_vma=False,
    )
```

```python
import jax
import jax.numpy as jnp
from jax import lax
from jax.experimental import pallas as pl
from jax.experimental.pallas import tpu as pltpu
from jax.sharding import PartitionSpec as P

FINE_RATE = 0.16
HALF_FINE = 0.5 * FINE_RATE
HALF_COARSE = 0.25 * FINE_RATE
TILE = 16
LANES = 128

VMEM = pl.BlockSpec(memory_space=pltpu.VMEM)
SMEM = pl.BlockSpec(memory_space=pltpu.SMEM)
F32 = jnp.float32


def call(body, out_shapes, operands, specs=None, scratch=(), flops=0):
    operands = list(operands)
    specs = specs or [VMEM] * len(operands)
    return pl.pallas_call(
        body,
        out_shape=[jax.ShapeDtypeStruct(s, F32) for s in out_shapes],
        in_specs=specs,
        out_specs=[VMEM] * len(out_shapes),
        scratch_shapes=list(scratch),
        compiler_params=pltpu.CompilerParams(vmem_limit_bytes=8 * 1024 * 1024),
    )(*operands)


def lane_scratch(rows, columns):
    return pltpu.VMEM((columns // LANES, rows, LANES), F32)


def split3(x):
    hi = x.astype(jnp.bfloat16)
    rest = x - hi.astype(F32)
    mid = rest.astype(jnp.bfloat16)
    low = (rest - mid.astype(F32)).astype(jnp.bfloat16)
    return hi, mid, low


def dot3(x, m):
    parts = [jnp.dot(p, m, preferred_element_type=F32) for p in split3(x)]
    return parts[0] + (parts[1] + parts[2])


def pair_matrix(fine, coarse, value):
    rows = lax.broadcasted_iota(jnp.int32, (fine, coarse), 0)
    cols = lax.broadcasted_iota(jnp.int32, (fine, coarse), 1)
    return jnp.where((rows >> 1) == cols, value, 0.0).astype(jnp.bfloat16)


def repeat_matrix(coarse, fine):
    rows = lax.broadcasted_iota(jnp.int32, (coarse, fine), 0)
    cols = lax.broadcasted_iota(jnp.int32, (coarse, fine), 1)
    return jnp.where(rows == (cols >> 1), 1.0, 0.0).astype(jnp.bfloat16)


def restrict_planes(first, second, scratch, matrix):
    blocks, ny, _ = scratch.shape
    sums = dot3(first + second, matrix)
    parts = []
    for b in range(blocks):
        scratch[b] = sums[:, b * LANES:(b + 1) * LANES]
        parts.append(scratch[b, pl.ds(0, ny // 2, 2), :] + scratch[b, pl.ds(1, ny // 2, 2), :])
    return jnp.concatenate(parts, axis=1)


def rows_above(ref, index, a, size):
    if a == 0:
        return pltpu.roll(ref[index + (slice(0, size),)], 1, 0)
    return ref[index + (slice(a - 1, a + size - 1),)]


def rows_below(ref, index, a, size, ny):
    if a + size == ny:
        return pltpu.roll(ref[index + (slice(a, a + size),)], size - 1, 0)
    return ref[index + (slice(a + 1, a + size + 1),)]


def face_coefficients(k, above, below, half, a, size, ny, nz):
    row = lax.broadcasted_iota(jnp.int32, (size, nz), 0) + a
    col = lax.broadcasted_iota(jnp.int32, (size, nz), 1)
    up_face = half * (k + jnp.where(row == 0, 0.0, above))
    down_face = half * (k + jnp.where(row == ny - 1, 0.0, below))
    right = pltpu.roll(k, nz - 1, 1)
    left = pltpu.roll(k, 1, 1)
    right_face = half * (k + jnp.where(col == nz - 1, 0.0, right))
    left_face = half * (k + jnp.where(col == 0, 0.0, left))
    total = (up_face + down_face) + (right_face + left_face)
    return (
        jnp.where(row == 0, 0.0, up_face),
        jnp.where(row == ny - 1, 0.0, down_face),
        jnp.where(col == nz - 1, 0.0, right_face),
        total,
    )


def prepare_fine(cond):
    nx, ny, nz = cond.shape

    def body(k_ref, kx, up, down, right, diag, coarse, scratch):
        for p in range(nx):
            for a in range(0, ny, TILE):
                s = slice(a, a + TILE)
                k = k_ref[p, s]
                u, d, r, total = face_coefficients(
                    k, rows_above(k_ref, (p,), a, TILE), rows_below(k_ref, (p,), a, TILE, ny),
                    HALF_FINE, a, TILE, ny, nz)
                up[p, s], down[p, s], right[p, s] = u, d, r
                if p > 0:
                    total = total + kx[p - 1, s]
                if p < nx - 1:
                    face = HALF_FINE * (k + k_ref[p + 1, s])
                    kx[p, s] = face
                    total = total + face
                diag[p, s] = 1.0 - total
        matrix = pair_matrix(nz, nz // 2, 0.125)
        for q in range(nx // 2):
            coarse[q] = restrict_planes(k_ref[2 * q], k_ref[2 * q + 1], scratch, matrix)

    full = (nx, ny, nz)
    return call(
        body,
        [(nx - 1, ny, nz), full, full, full, full, (nx // 2, ny // 2, nz // 2)],
        [cond],
        scratch=[lane_scratch(ny, nz // 2)],
    )


def restricted(field):
    nx, ny, nz = field.shape

    def body(f_ref, out, scratch):
        matrix = pair_matrix(nz, nz // 2, 0.125)
        for q in range(nx // 2):
            out[q] = restrict_planes(f_ref[2 * q], f_ref[2 * q + 1], scratch, matrix)

    return call(
        body, [(nx // 2, ny // 2, nz // 2)], [field], scratch=[lane_scratch(ny, nz // 2)]
    )[0]


def gather_openings(place, initial, prior, cond, slots):
    nx, ny, nz = initial.shape
    half, rows = nx // 2, ny // slots

    def body(place_ref, i_ref, p_ref, k_ref, low, high, on, off, sems):
        even = place_ref[2]
        own, far = even * half, (1 - even) * half
        start = pl.multiple_of(place_ref[3] * rows, rows)

        def opening(ref):
            copies = [
                pltpu.make_async_copy(ref.at[pl.ds(0, half)], low, sems.at[0]),
                pltpu.make_async_copy(ref.at[pl.ds(half, half)], high, sems.at[1]),
                pltpu.make_async_copy(k_ref.at[pl.ds(own, half)], on, sems.at[2]),
                pltpu.make_async_copy(
                    k_ref.at[pl.ds(far, half), pl.ds(start, rows)], off, sems.at[3]),
            ]
            for c in copies:
                c.start()
            for c in copies:
                c.wait()

        pl.when(place_ref[4] > 0)(lambda: opening(i_ref))
        pl.when(place_ref[4] == 0)(lambda: opening(p_ref))

    plane = (half, ny, nz)
    return call(
        body, [plane, plane, plane, (half, rows, nz)], [place, initial, prior, cond],
        [SMEM] + [pl.BlockSpec(memory_space=pl.ANY)] * 3, [pltpu.SemaphoreType.DMA((4,))])


def ghost_coefficients(place, cond, on, quarters):
    nx, ny, nz = cond.shape
    half, rows, _ = quarters[0].shape
    slots = len(quarters)

    def body(place_ref, k_ref, on_ref, *refs):
        parts = refs[:slots]
        kx, up, down, right, diag, far, sides = refs[slots:]
        even = place_ref[2] > 0
        has_lo, has_hi = place_ref[0] > 0, place_ref[1] > 0
        for j in range(slots):
            slot = lax.rem(place_ref[3] + (slots - j), slots)
            far[:, pl.ds(pl.multiple_of(slot * rows, rows), rows)] = parts[j][...]
        for p in range(half):
            for a in range(0, ny, TILE):
                s = slice(a, a + TILE)
                x, y = far[p, s], on_ref[p, s]
                sides[p, s] = jnp.where(has_lo, jnp.where(even, x, y), 0.0)
                sides[half + p, s] = jnp.where(has_hi, jnp.where(even, y, x), 0.0)
        for side, near, next_, inner in ((0, half - 1, half - 2, 0), (1, half, half + 1, nx - 1)):
            for a in range(0, ny, TILE):
                s = slice(a, a + TILE)
                k = sides[near, s]
                u, d, r, total = face_coefficients(
                    k, rows_above(sides, (near,), a, TILE), rows_below(sides, (near,), a, TILE, ny),
                    HALF_FINE, a, TILE, ny, nz)
                outer = HALF_FINE * (k + sides[next_, s])
                face = HALF_FINE * (k + k_ref[inner, s])
                kx[2 * side, s], kx[2 * side + 1, s] = outer, face
                up[side, s], down[side, s], right[side, s] = u, d, r
                diag[side, s] = 1.0 - ((total + outer) + face)

    two = (2, ny, nz)
    return call(
        body, [(4, ny, nz), two, two, two, two], [place, cond, on, *quarters],
        [SMEM] + [VMEM] * (2 + slots),
        [pltpu.VMEM((half, ny, nz), F32), pltpu.VMEM((2 * half, ny, nz), F32)])


def row_step(v, up, down, right, diag, a, ny, nz):
    ref, index = v
    s = slice(a, a + TILE)
    c = ref[index + (s,)]
    total = diag * c
    total = total + up * rows_above(ref, index, a, TILE)
    total = total + down * rows_below(ref, index, a, TILE, ny)
    total = total + right * pltpu.roll(c, nz - 1, 1)
    return c, total + pltpu.roll(right * c, 1, 1)


def half_step(low, high, coefficients):
    half, ny, nz = low.shape
    nx = 2 * half

    def body(low_ref, high_ref, kx, up, down, right, diag, out):
        planes = [(low_ref, (p,)) for p in range(half)] + [(high_ref, (p,)) for p in range(half)]
        for p in range(nx):
            for a in range(0, ny, TILE):
                s = slice(a, a + TILE)
                c, total = row_step(planes[p], up[p, s], down[p, s], right[p, s], diag[p, s], a, ny, nz)
                if p > 0:
                    ref, index = planes[p - 1]
                    total = total + kx[p - 1, s] * ref[index + (s,)]
                if p < nx - 1:
                    ref, index = planes[p + 1]
                    total = total + kx[p, s] * ref[index + (s,)]
                out[p, s] = total

    return call(body, [(nx, ny, nz)], [low, high, *coefficients])[0]


def two_steps(place, low, high, before, after, started, coefficients, ghosts, last_prior=None, extra=()):
    half, ny, nz = low.shape
    nx = 2 * half
    final = last_prior is not None

    def body(place_ref, low_ref, high_ref, lo, hi, part, kx, up, down, right, diag, gx, gup, gdown, gright, gdiag, *rest):
        has_lo, has_hi = place_ref[0] > 0, place_ref[1] > 0
        rest = rest[len(extra):]
        if final:
            prior_ref, out_ref, jump_ref, mid, scratch = rest
            out = [out_ref.at[p] for p in range(nx)]
        else:
            low_out, high_out, mid = rest
            out = [low_out.at[p] for p in range(half)] + [high_out.at[p] for p in range(half)]
        for a in range(0, ny, TILE):
            s = slice(a, a + TILE)
            for side, ref, near, far, inner, has, own, place_in in (
                (0, lo, half - 1, half - 2, low_ref[0, s], has_lo, 0, 0),
                (1, hi, 0, 1, high_ref[half - 1, s], has_hi, nx - 1, nx + 1),
            ):
                c, total = row_step(
                    (ref, (near,)), gup[side, s], gdown[side, s], gright[side, s], gdiag[side, s], a, ny, nz)
                total = total + gx[2 * side, s] * ref[far, s] + gx[2 * side + 1, s] * inner
                mid[place_in, s] = jnp.where(has, total, 0.0)
                mid[own + 1, s] = part[own, s] + gx[2 * side + 1, s] * (jnp.where(has, c, 0.0) - inner)
            for p in range(1, nx - 1):
                mid[p + 1, s] = part[p, s]
        for p in range(nx):
            for a in range(0, ny, TILE):
                s = slice(a, a + TILE)
                c, total = row_step(
                    (mid, (p + 1,)), up[p, s], down[p, s], right[p, s], diag[p, s], a, ny, nz)
                if p > 0:
                    total = total + kx[p - 1, s] * mid[p, s]
                else:
                    total = total + gx[1, s] * (mid[p, s] - c)
                if p < nx - 1:
                    total = total + kx[p, s] * mid[p + 2, s]
                else:
                    total = total + gx[3, s] * (mid[p + 2, s] - c)
                out[p][s] = total
        if final:
            matrix = pair_matrix(nz, nz // 2, 0.125)
            for q in range(half):
                jump_ref[q] = restrict_planes(out[2 * q][...], out[2 * q + 1][...], scratch, matrix) - prior_ref[q]

    operands = [place, low, high, before, after, started, *coefficients, *ghosts, *extra]
    scratch = [pltpu.VMEM((nx + 2, ny, nz), F32)]
    if final:
        operands.append(last_prior)
        shapes = [(nx, ny, nz), (half, ny // 2, nz // 2)]
        scratch.append(lane_scratch(ny, nz // 2))
    else:
        shapes = [low.shape, high.shape]
    return call(body, shapes, operands, [SMEM] + [VMEM] * (len(operands) - 1), scratch)


def coarse_coefficients(ends, own, before, after):
    nx, ny, nz = own.shape
    planes = nx + 2

    def body(ends_ref, k_own, k_lo, k_hi, kx, up, down, right, diag):
        has_lo, has_hi = ends_ref[0] > 0, ends_ref[1] > 0

        def plane(i):
            if i < 2:
                return jnp.where(has_lo, k_lo[nx - 2 + i], 0.0)
            if i < nx + 2:
                return k_own[i - 2]
            return jnp.where(has_hi, k_hi[i - nx - 2], 0.0)

        for i in range(planes + 1):
            kx[i] = HALF_COARSE * (plane(i) + plane(i + 1))
        for p in range(planes):
            k = plane(p + 1)
            u, d, r, total = face_coefficients(
                k, pltpu.roll(k, 1, 0), pltpu.roll(k, ny - 1, 0), HALF_COARSE, 0, ny, ny, nz)
            up[p], down[p], right[p] = u, d, r
            diag[p] = 1.0 - (total + kx[p] + kx[p + 1])

    full = (planes, ny, nz)
    return call(
        body, [(planes + 1, ny, nz)] + [full] * 4, [ends, own, before, after], [SMEM] + [VMEM] * 3
    )


def coarse_sweep_step(ends, own, before, after, coefficients, jump=None):
    nx, ny, nz = own.shape

    def body(ends_ref, d_own, d_lo, d_hi, kx, up, down, right, diag, *rest):
        has_lo, has_hi = ends_ref[0] > 0, ends_ref[1] > 0

        def step(v, i):
            c = v[1]
            total = diag[i] * c + kx[i] * v[0] + kx[i + 1] * v[2]
            total = total + up[i] * pltpu.roll(c, 1, 0) + down[i] * pltpu.roll(c, ny - 1, 0)
            return total + right[i] * pltpu.roll(c, nz - 1, 1) + pltpu.roll(right[i] * c, 1, 1)

        lo = [jnp.where(has_lo, d_lo[nx - 2 + i], 0.0) for i in range(2)]
        hi = [jnp.where(has_hi, d_hi[i], 0.0) for i in range(2)]
        v = lo + [d_own[i] for i in range(nx)] + hi
        w = [step(v[i:i + 3], i) for i in range(nx + 2)]
        w[0] = jnp.where(has_lo, w[0], 0.0)
        w[-1] = jnp.where(has_hi, w[-1], 0.0)
        for i in range(nx):
            e = step(w[i:i + 3], i + 1)
            rest[-1 if jump is None else -2][i] = e
            if jump is not None:
                rest[-1][i] = e + rest[0][i]

    operands = [ends, own, before, after, *coefficients]
    shapes = [own.shape]
    if jump is not None:
        operands.append(jump)
        shapes.append(own.shape)
    return call(body, shapes, operands, [SMEM] + [VMEM] * (len(operands) - 1))


def finish(fine, prior, correction):
    nx, ny, nz = fine.shape

    def body(f_ref, p_ref, e_ref, update, tail, scratch, wide):
        matrix = pair_matrix(nz, nz // 2, 0.125)
        spread = repeat_matrix(nz // 2, nz)
        for q in range(nx // 2):
            e = e_ref[q]
            tail[q] = e + restrict_planes(f_ref[2 * q], f_ref[2 * q + 1], scratch, matrix)
            row = dot3(e, spread)
            for b in range(nz // LANES):
                s = slice(b * LANES, (b + 1) * LANES)
                wide[b, pl.ds(0, ny // 2, 2), :] = row[:, s]
                wide[b, pl.ds(1, ny // 2, 2), :] = row[:, s]
                for p in (2 * q, 2 * q + 1):
                    update[p, :, s] = (f_ref[p, :, s] + wide[b]) - p_ref[p, :, s]

    return call(
        body,
        [(nx, ny, nz), (nx // 2, ny // 2, nz // 2)],
        [fine, prior, correction],
        scratch=[lane_scratch(ny, nz // 2), lane_scratch(ny, nz)],
    )


def ring(block, axis, distance):
    size = lax.axis_size(axis)
    return lax.ppermute(block, axis, [(i, (i + distance) % size) for i in range(size)])


def from_sides(last, first):
    return ring(last, "space", 1), ring(first, "space", -1)


def swapped(block, axis, offset):
    size = lax.axis_size(axis)
    pairs = [(i % size, (i + 1) % size) for i in range(offset, size + offset, 2)]
    return lax.ppermute(block, axis, pairs + [(j, i) for i, j in pairs])


def shards(initial, prior, conductivity):
    t, times = lax.axis_index("tm"), lax.axis_size("tm")
    s, blocks = lax.axis_index("space"), lax.axis_size("space")
    own_prior = prior[0]
    home = times - 1
    place = jnp.stack([s > 0, s < blocks - 1, s % 2 == 0, t, t == home]).astype(jnp.int32)

    low, high, on, off = gather_openings(place, initial, own_prior, conductivity, times)
    off = swapped(off, "space", 1)
    before, after = from_sides(high, low)
    on = swapped(on, "space", 0)
    quarters = [off] + [ring(off, "tm", j) for j in range(1, times)]

    *coefficients, coarse_cond = prepare_fine(conductivity)
    started = half_step(low, high, coefficients)
    next_prior = ring(restricted(own_prior), "tm", -1)
    coarse_before, coarse_after = from_sides(coarse_cond, coarse_cond)
    ghosts = ghost_coefficients(place, conductivity, on, quarters)
    low, high = two_steps(place, low, high, before, after, started, coefficients, ghosts)

    before, after = from_sides(high, low)
    started = half_step(low, high, coefficients)
    coarse_coef = coarse_coefficients(place, coarse_cond, coarse_before, coarse_after)
    fine, jump = two_steps(
        place, low, high, before, after, started, coefficients, ghosts, next_prior, coarse_coef[:1])

    jumps = [jump] + [
        lax.ppermute(jump, "tm", [(n - 1, home)]) for n in range(1, times - 1)
    ]
    own_fine = ring(fine, "tm", 1)
    state = jump
    correction = jnp.zeros_like(jump)
    for n in range(1, times):
        before, after = from_sides(state, state)
        swept = coarse_sweep_step(
            place, state, before, after, coarse_coef, jumps[n] if n < home else None)
        if n < home:
            e, state = swept
            arrived = lax.ppermute(e, "tm", [(home, n)])
        else:
            arrived = swept[0]
        correction = jnp.where(t == n, arrived, correction)
    update, tail = finish(own_fine, own_prior, correction)
    return update[None], tail[None]


def solution(mesh):
    return jax.shard_map(
        shards,
        mesh=mesh,
        in_specs=(P("space", None, None), P("tm", "space", None, None), P("space", None, None)),
        out_specs=(P("tm", "space", None, None), P("tm", "space", None, None)),
        check_vma=False,
    )
```

```python
import jax
import jax.numpy as jnp
from jax import lax
from jax.experimental import pallas as pl
from jax.experimental.pallas import tpu as pltpu
from jax.sharding import PartitionSpec as P

FINE_RATE = 0.16
HALF_FINE = 0.5 * FINE_RATE
HALF_COARSE = 0.25 * FINE_RATE
TILE = 8
OVERLAP = 8
LANES = 128

VMEM = pl.BlockSpec(memory_space=pltpu.VMEM)
SMEM = pl.BlockSpec(memory_space=pltpu.SMEM)
HBM = pl.BlockSpec(memory_space=pltpu.HBM)
F32 = jnp.float32


def call(body, out_shapes, operands, specs=None, scratch=()):
    operands = list(operands)
    specs = specs or [VMEM] * len(operands)
    operands = [
        pltpu.with_memory_space_constraint(x, pltpu.HBM) if spec is HBM else x for x, spec in zip(operands, specs)
    ]
    return pl.pallas_call(
        body,
        out_shape=[jax.ShapeDtypeStruct(s, F32) for s in out_shapes],
        in_specs=specs,
        out_specs=[VMEM] * len(out_shapes),
        scratch_shapes=list(scratch),
        compiler_params=pltpu.CompilerParams(vmem_limit_bytes=8 * 1024 * 1024),
    )(*operands)


def lane_scratch(rows, columns):
    return pltpu.VMEM((columns // LANES, rows, LANES), F32)


def split3(x):
    hi = x.astype(jnp.bfloat16)
    rest = x - hi.astype(F32)
    mid = rest.astype(jnp.bfloat16)
    low = (rest - mid.astype(F32)).astype(jnp.bfloat16)
    return hi, mid, low


def dot3(x, m):
    parts = [jnp.dot(p, m, preferred_element_type=F32) for p in split3(x)]
    return parts[0] + (parts[1] + parts[2])


def pair_matrix(fine, coarse, value):
    rows = lax.broadcasted_iota(jnp.int32, (fine, coarse), 0)
    cols = lax.broadcasted_iota(jnp.int32, (fine, coarse), 1)
    return jnp.where((rows >> 1) == cols, value, 0.0).astype(jnp.bfloat16)


def repeat_matrix(coarse, fine):
    rows = lax.broadcasted_iota(jnp.int32, (coarse, fine), 0)
    cols = lax.broadcasted_iota(jnp.int32, (coarse, fine), 1)
    return jnp.where(rows == (cols >> 1), 1.0, 0.0).astype(jnp.bfloat16)


def restrict_planes(first, second, scratch, matrix):
    blocks, ny, _ = scratch.shape
    sums = dot3(first + second, matrix)
    parts = []
    for b in range(blocks):
        scratch[b] = sums[:, b * LANES:(b + 1) * LANES]
        parts.append(scratch[b, pl.ds(0, ny // 2, 2), :] + scratch[b, pl.ds(1, ny // 2, 2), :])
    return jnp.concatenate(parts, axis=1)


class Field:
    def __init__(self, pieces, ny):
        self.pieces, self.ny = pieces, ny

    def find(self, row):
        for piece in self.pieces:
            if piece[0] <= row < piece[1]:
                return piece
        return None

    def rows(self, a, size):
        first, end, ref, index, base = self.find(a)
        return ref[index + (slice(a - base, a - base + size),)]

    def tile(self, a):
        return self.rows(a, TILE)

    def edge(self, a, row, shift, at):
        moved = pltpu.roll(self.tile(a), shift, 0)
        if self.find(row) is None:
            return moved
        place = lax.broadcasted_iota(jnp.int32, moved.shape, 0)
        return jnp.where(place == at, self.rows(row, 1), moved)

    def above(self, a):
        if self.find(a - 1) == self.find(a):
            return self.rows(a - 1, TILE)
        return self.edge(a, a - 1, 1, 0)

    def below(self, a):
        if self.find(a + TILE) == self.find(a):
            return self.rows(a + 1, TILE)
        return self.edge(a, a + TILE, TILE - 1, TILE - 1)


def plane(ref, index, ny):
    return Field([(0, ny, ref, index, 0)], ny)


def face_coefficients(k, above, below, half, a, size, ny, nz):
    row = lax.broadcasted_iota(jnp.int32, (size, nz), 0) + a
    col = lax.broadcasted_iota(jnp.int32, (size, nz), 1)
    up_face = half * (k + jnp.where(row == 0, 0.0, above))
    down_face = half * (k + jnp.where(row == ny - 1, 0.0, below))
    right = pltpu.roll(k, nz - 1, 1)
    left = pltpu.roll(k, 1, 1)
    right_face = half * (k + jnp.where(col == nz - 1, 0.0, right))
    left_face = half * (k + jnp.where(col == 0, 0.0, left))
    total = (up_face + down_face) + (right_face + left_face)
    return (
        jnp.where(row == 0, 0.0, up_face),
        jnp.where(row == ny - 1, 0.0, down_face),
        jnp.where(col == nz - 1, 0.0, right_face),
        total,
    )


def prepare_fine(cond):
    nx, ny, nz = cond.shape

    def body(k_ref, kx, up, down, right, diag):
        for p in range(nx):
            for a in range(0, ny, TILE):
                s = slice(a, a + TILE)
                k = k_ref[p, s]
                u, d, r, total = face_coefficients(
                    k, plane(k_ref, (p,), ny).above(a), plane(k_ref, (p,), ny).below(a),
                    HALF_FINE, a, TILE, ny, nz)
                up[p, s], down[p, s], right[p, s] = u, d, r
                if p > 0:
                    total = total + kx[p - 1, s]
                if p < nx - 1:
                    face = HALF_FINE * (k + k_ref[p + 1, s])
                    kx[p, s] = face
                    total = total + face
                diag[p, s] = 1.0 - total
    full = (nx, ny, nz)
    return call(body, [(nx - 1, ny, nz), full, full, full, full], [cond])


def restricted(field):
    nx, ny, nz = field.shape

    def body(f_ref, out, scratch):
        matrix = pair_matrix(nz, nz // 2, 0.125)
        for q in range(nx // 2):
            out[q] = restrict_planes(f_ref[2 * q], f_ref[2 * q + 1], scratch, matrix)

    return call(
        body, [(nx // 2, ny // 2, nz // 2)], [field], scratch=[lane_scratch(ny, nz // 2)]
    )[0]


def packed(half, nz, at, count):
    step = count // (2 * half)
    return [
        (slice(i * step, (i + 1) * step),
         (i // 2, slice(at, at + step), slice(i % 2 * nz // 2, (i % 2 + 1) * nz // 2)))
        for i in range(2 * half)
    ]


def row_copies(source, out, base, rows, at, sems, first_sem):
    start, end = rows
    return [
        pltpu.make_async_copy(
            source.at[base + p, pl.ds(start, end - start)], out.at[p, pl.ds(at, end - start)], sems.at[first_sem + p])
        for p in range(out.shape[0])
    ]


def run(copies):
    for c in copies:
        c.start()
    for c in copies:
        c.wait()


def chosen(flag, body, this, other):
    pl.when(flag > 0)(lambda: body(this))
    pl.when(flag == 0)(lambda: body(other))


def first_messages(place, initial, prior, cond, end):
    nx, ny, nz = cond.shape
    half = nx // 2

    def body(place_ref, i_ref, p_ref, k_ref, down, up, sems):
        def copy(ref):
            copies = []
            for out, base in ((down, 0), (up, half)):
                for source, at in ((k_ref, 0), (ref, end)):
                    copies += row_copies(source, out, base, (0, end), at, sems, len(copies))
            run(copies)

        chosen(place_ref[3], copy, i_ref, p_ref)

    return call(
        body, [(half, 2 * end, nz)] * 2, [place, initial, prior, cond], [SMEM, HBM, HBM, HBM],
        [pltpu.SemaphoreType.DMA((4 * half,))])


def second_messages(cond, end, after):
    nx, ny, nz = cond.shape
    half, rows = nx // 2, ny - end
    extra = ny // 2 // (2 * half)

    def body(k_ref, after_ref, down, up, cond_out, coarse, scratch, sems):
        whole = [pltpu.make_async_copy(k_ref.at[p], cond_out.at[p], sems.at[p]) for p in range(nx)]
        run(whole)
        matrix = pair_matrix(nz, nz // 2, 0.125)
        for q in range(half):
            coarse[q] = restrict_planes(cond_out[2 * q], cond_out[2 * q + 1], scratch, matrix)
            down[q, :rows] = cond_out[q, end:]
            up[q, :rows] = cond_out[half + q, end:]
        for source, to in packed(half, nz, rows, ny // 2):
            down[to] = coarse[half - 1, source]
            up[to] = coarse[0, source]

    return call(
        body, [(half, rows + extra, nz)] * 2 + [(nx, ny, nz), (half, ny // 2, nz // 2)],
        [cond, after], [HBM, VMEM], [lane_scratch(ny, nz // 2), pltpu.SemaphoreType.DMA((nx,))])


def rows_from(field, start, after):
    nx, ny, nz = field.shape

    def body(ref, after_ref, out, sems):
        run(row_copies(ref, out, 0, (start, ny), 0, sems, 0))

    return call(body, [(nx, ny - start, nz)], [field, after], [HBM, VMEM], [pltpu.SemaphoreType.DMA((nx,))])[0]


def third_messages(place, initial, received, start):
    nx, ny, nz = initial.shape
    half = nx // 2

    def body(place_ref, i_ref, r_ref, down, up, sems):
        def copy(rows_of):
            ref, rows = rows_of
            run(row_copies(ref, down, 0, rows, 0, sems, 0) + row_copies(ref, up, half, rows, 0, sems, half))

        chosen(place_ref[4], copy, (i_ref, (start, ny)), (r_ref, (0, ny - start)))

    return call(
        body, [(half, ny - start, nz)] * 2, [place, initial, received], [SMEM, HBM, VMEM],
        [pltpu.SemaphoreType.DMA((nx,))])


def ghost_coefficients(place, cond, before, after, spans, window):
    nx, ny, nz = cond.shape
    half, count = nx // 2, len(spans)
    w0, w1 = window

    def body(place_ref, k_ref, *refs):
        lo = fields(spans, refs[:count], half, ny)
        hi = fields(spans, refs[count:2 * count], half, ny)
        kx, up, down, right, diag = refs[2 * count:]
        for side, near, far, inner, has in (
            (0, lo[half - 1], lo[half - 2], 0, place_ref[0] > 0),
            (1, hi[0], hi[1], nx - 1, place_ref[1] > 0),
        ):
            for a in range(w0, w1, TILE):
                s, d = slice(a, a + TILE), slice(a - w0, a - w0 + TILE)
                k = jnp.where(has, near.tile(a), 0.0)
                above, below = (jnp.where(has, x, 0.0) for x in (near.above(a), near.below(a)))
                u, v, r, total = face_coefficients(k, above, below, HALF_FINE, a, TILE, ny, nz)
                outer = HALF_FINE * (k + jnp.where(has, far.tile(a), 0.0))
                face = HALF_FINE * (k + k_ref[inner, s])
                kx[2 * side, d], kx[2 * side + 1, d] = outer, face
                up[side, d], down[side, d], right[side, d] = u, v, r
                diag[side, d] = 1.0 - ((total + outer) + face)

    rows = w1 - w0
    return call(
        body, [(4, rows, nz)] + [(2, rows, nz)] * 4, [place, cond, *before, *after],
        [SMEM] + [VMEM] * (1 + 2 * count))


def row_step(v, up, down, right, diag, a):
    c = v.tile(a)
    nz = c.shape[1]
    total = diag * c
    total = total + up * v.above(a)
    total = total + down * v.below(a)
    total = total + right * pltpu.roll(c, nz - 1, 1)
    return c, total + pltpu.roll(right * c, 1, 1)


def fields(spans, refs, half, ny):
    return [
        Field([(a, b, ref, (p,), base) for (a, b, base), ref in zip(spans, refs)], ny)
        for p in range(half)
    ]


def half_step(low, high, spans, window, coefficients):
    half, nz = low[0].shape[0], low[0].shape[2]
    nx, ny, count = 2 * half, coefficients[1].shape[1], len(spans)
    w0, w1 = window

    def body(*refs):
        kx, up, down, right, diag, out = refs[2 * count:]
        v = fields(spans, refs[:count], half, ny) + fields(spans, refs[count:2 * count], half, ny)
        for p in range(nx):
            for a in range(w0, w1, TILE):
                s = slice(a, a + TILE)
                _, total = row_step(v[p], up[p, s], down[p, s], right[p, s], diag[p, s], a)
                if p > 0:
                    total = total + kx[p - 1, s] * v[p - 1].tile(a)
                if p < nx - 1:
                    total = total + kx[p, s] * v[p + 1].tile(a)
                out[p, a - w0:a - w0 + TILE] = total

    return call(body, [(nx, w1 - w0, nz)], [*low, *high, *coefficients])[0]


def two_steps(place, low, high, spans, before, after, side_spans, started, window, result, coefficients, ghosts, final=False):
    half, nz = low[0].shape[0], low[0].shape[2]
    nx, ny = 2 * half, coefficients[1].shape[1]
    n, m = len(spans), len(side_spans)
    (w0, w1), (r0, r1) = window, result
    counts = [n, n, m, m]

    def body(place_ref, *refs):
        groups, at = [], 0
        for c in counts:
            groups.append(refs[at:at + c])
            at += c
        part, kx, up, down, right, diag, gx, gup, gdown, gright, gdiag, *rest = refs[at:]
        v = fields(spans, groups[0], half, ny) + fields(spans, groups[1], half, ny)
        lo = fields(side_spans, groups[2], half, ny)
        hi = fields(side_spans, groups[3], half, ny)
        has_lo, has_hi = place_ref[0] > 0, place_ref[1] > 0
        if final:
            out_ref, coarse_out, mid, scratch = rest
            out = [out_ref.at[p] for p in range(nx)]
        else:
            low_out, high_out, mid = rest
            out = [low_out.at[p] for p in range(half)] + [high_out.at[p] for p in range(half)]
        for a in range(w0, w1, TILE):
            s, d = slice(a, a + TILE), slice(a - w0, a - w0 + TILE)
            for side, near, far, has, own, ghost in (
                (0, lo[half - 1], lo[half - 2], has_lo, 0, 0),
                (1, hi[0], hi[1], has_hi, nx - 1, nx + 1),
            ):
                inner = v[own].tile(a)
                c, total = row_step(near, gup[side, d], gdown[side, d], gright[side, d], gdiag[side, d], a)
                total = total + gx[2 * side, d] * far.tile(a) + gx[2 * side + 1, d] * inner
                mid[ghost, d] = jnp.where(has, total, 0.0)
                mid[own + 1, d] = part[own, d] + gx[2 * side + 1, d] * (jnp.where(has, c, 0.0) - inner)
            for p in range(1, nx - 1):
                mid[p + 1, d] = part[p, d]
        w = [Field([(w0, w1, mid, (p,), w0)], ny) for p in range(nx + 2)]
        for p in range(nx):
            for a in range(r0, r1, TILE):
                s, d = slice(a, a + TILE), slice(a - w0, a - w0 + TILE)
                c, total = row_step(w[p + 1], up[p, s], down[p, s], right[p, s], diag[p, s], a)
                if p > 0:
                    total = total + kx[p - 1, s] * w[p].tile(a)
                else:
                    total = total + gx[1, d] * (w[p].tile(a) - c)
                if p < nx - 1:
                    total = total + kx[p, s] * w[p + 2].tile(a)
                else:
                    total = total + gx[3, d] * (w[p + 2].tile(a) - c)
                out[p][a - r0:a - r0 + TILE] = total
        if final:
            matrix = pair_matrix(nz, nz // 2, 0.125)
            for q in range(half):
                coarse_out[q] = restrict_planes(out[2 * q][...], out[2 * q + 1][...], scratch, matrix)

    operands = [place, *low, *high, *before, *after, started, *coefficients, *ghosts]
    scratch = [pltpu.VMEM((nx + 2, w1 - w0, nz), F32)]
    shapes = [(half, r1 - r0, nz)] * 2
    if final:
        scratch.append(lane_scratch(r1 - r0, nz // 2))
        shapes = [(nx, r1 - r0, nz), (half, (r1 - r0) // 2, nz // 2)]
    return call(body, shapes, operands, [SMEM] + [VMEM] * (len(operands) - 1), scratch)


def coarse_coefficients(place, own, before, after, spans):
    nx, ny, nz = own.shape
    planes, count = nx + 2, len(spans)

    def body(place_ref, k_own, *refs):
        sides = refs[:count], refs[count:2 * count]
        kx, up, down, right, diag, k_near, k_far, total, scratch = refs[2 * count:]
        matrix = pair_matrix(2 * nz, nz, 0.125)
        for i, (side, has) in enumerate(zip(sides, (place_ref[0] > 0, place_ref[1] > 0))):
            for (a, b, base), ref in zip(spans, side):
                total[a:b] = ref[0, a - base:b - base] + ref[1, a - base:b - base]
            near = restrict_planes(total[...], 0.0, scratch, matrix)
            k_near[i] = jnp.where(has, near, 0.0)
            last = side[-1]
            for rows, at in packed(nx, 2 * nz, last.shape[1] - ny // (2 * nx), ny):
                k_far[i, rows] = jnp.where(has, last[at], 0.0)

        def plane(i):
            if i == 0:
                return k_far[0]
            if i == 1:
                return k_near[0]
            if i < nx + 2:
                return k_own[i - 2]
            return k_near[1] if i == nx + 2 else k_far[1]

        for i in range(planes + 1):
            kx[i] = HALF_COARSE * (plane(i) + plane(i + 1))
        for p in range(planes):
            k = plane(p + 1)
            u, d, r, total = face_coefficients(
                k, pltpu.roll(k, 1, 0), pltpu.roll(k, ny - 1, 0), HALF_COARSE, 0, ny, ny, nz)
            up[p], down[p], right[p] = u, d, r
            diag[p] = 1.0 - (total + kx[p] + kx[p + 1])

    full = (planes, ny, nz)
    return call(
        body, [(planes + 1, ny, nz)] + [full] * 4, [place, own, *before, *after],
        [SMEM] + [VMEM] * (1 + 2 * count),
        [pltpu.VMEM((2, ny, nz), F32), pltpu.VMEM((2, ny, nz), F32),
         pltpu.VMEM((2 * ny, 2 * nz), F32), lane_scratch(2 * ny, nz)])


def sweep_step(place, own, before, after, coefficients, first, jumps=(), later=0):
    nx, ny, nz = own.shape

    def body(place_ref, d_own, d_lo, d_hi, kx, up, down, right, diag, *rest):
        live = place_ref[3] > 0 if first else True
        has_lo = jnp.logical_and(place_ref[0] > 0, live)
        has_hi = jnp.logical_and(place_ref[1] > 0, live)

        def step(v, i):
            c = v[1]
            total = diag[i] * c + kx[i] * v[0] + kx[i + 1] * v[2]
            total = total + up[i] * pltpu.roll(c, 1, 0) + down[i] * pltpu.roll(c, ny - 1, 0)
            return total + right[i] * pltpu.roll(c, nz - 1, 1) + pltpu.roll(right[i] * c, 1, 1)

        lo = [jnp.where(has_lo, d_lo[nx - 2 + i], 0.0) for i in range(2)]
        hi = [jnp.where(has_hi, d_hi[i], 0.0) for i in range(2)]
        block = [jnp.where(live, d_own[i], 0.0) if first else d_own[i] for i in range(nx)]
        v = lo + block + hi
        w = [step(v[i:i + 3], i) for i in range(nx + 2)]
        w[0] = jnp.where(has_lo, w[0], 0.0)
        w[-1] = jnp.where(has_hi, w[-1], 0.0)
        for i in range(nx):
            e = step(w[i:i + 3], i + 1)
            if jumps:
                e = e + jnp.where(place_ref[2] >= later, joined(rest[0][i], rest[1][i]), 0.0)
            rest[-1][i] = e

    operands = [place, own, before, after, *coefficients]
    operands += jumps
    return call(body, [own.shape], operands, [SMEM] + [VMEM] * (len(operands) - 1))[0]


def jumps_of(moved, own, next_prior, own_prior):
    nx, rows, nz = moved.shape

    def body(a_ref, b_ref, next_ref, own_ref, out):
        for p in range(nx):
            out[p, :rows] = a_ref[p] - next_ref[p, :rows]
            out[p, rows:] = b_ref[p] - own_ref[p, rows:]

    return call(body, [own_prior.shape], [moved, own, next_prior, own_prior])[0]


def joined(upper, lower):
    rows = upper.shape[-2]
    row = lax.broadcasted_iota(jnp.int32, upper.shape, upper.ndim - 2)
    return jnp.where(row < rows // 2, upper, lower)


def finish(moved, own, prior, correction):
    nx, ny, nz = prior.shape
    rows = moved.shape[1]

    def body(moved_ref, own_ref, p_ref, e_ref, update, tail, scratch, wide):
        matrix = pair_matrix(nz, nz // 2, 0.125)
        spread = repeat_matrix(nz // 2, nz)
        for i, ref in enumerate((own_ref, moved_ref)):
            r0 = rows * (1 - i)
            r, c = slice(r0, r0 + rows), slice(r0 // 2, (r0 + rows) // 2)
            for q in range(nx // 2):
                e = e_ref[q, c]
                tail[q, c] = e + restrict_planes(ref[2 * q], ref[2 * q + 1], scratch, matrix)
                row = dot3(e, spread)
                for b in range(nz // LANES):
                    s = slice(b * LANES, (b + 1) * LANES)
                    wide[b, pl.ds(0, rows // 2, 2), :] = row[:, s]
                    wide[b, pl.ds(1, rows // 2, 2), :] = row[:, s]
                    for p in (2 * q, 2 * q + 1):
                        update[p, r, s] = (ref[p, :, s] + wide[b]) - p_ref[p, r, s]

    return call(
        body,
        [(nx, ny, nz), (nx // 2, ny // 2, nz // 2)],
        [moved, own, prior, correction],
        scratch=[lane_scratch(rows, nz // 2), lane_scratch(rows, nz)],
    )


def ring(block, axis, distance):
    size = lax.axis_size(axis)
    return lax.ppermute(block, axis, [(i, (i + distance) % size) for i in range(size)])


def from_sides(last, first):
    return ring(last, "space", 1), ring(first, "space", -1)


def shards(initial, prior, conductivity):
    t, times = lax.axis_index("tm"), lax.axis_size("tm")
    s, blocks = lax.axis_index("space"), lax.axis_size("space")
    own_prior = prior[0]
    home = times - 1
    place = jnp.stack([s > 0, s < blocks - 1, t, t == home, t == 0]).astype(jnp.int32)
    ny = initial.shape[1]
    cut, wide = ny // 2, ny // 2 + OVERLAP
    windows = [(0, wide), (cut - OVERLAP, ny)]
    results = [(0, cut), (cut, ny)]

    down, up = first_messages(place, initial, own_prior, conductivity, wide)
    before, after = ([x] for x in from_sides(up, down))
    received = ring(rows_from(own_prior, windows[1][0], up), "tm", 1)
    down_2, up_2, cond, coarse_cond = second_messages(conductivity, wide, up)
    before_2, after_2 = from_sides(up_2, down_2)
    down_3, up_3 = third_messages(place, initial, received, windows[1][0])
    before_3, after_3 = from_sides(up_3, down_3)

    coefficients = prepare_fine(cond)
    cond_spans = [(0, wide, 0), (wide, ny, wide)]
    cond_before, cond_after = (before[0], before_2), (after[0], after_2)
    low, high = [[down], [down_3]], [[up], [up_3]]
    before, after = [before, [before_3]], [after, [after_3]]
    spans = [[(0, wide, -wide)], [(*windows[1], windows[1][0])]]
    started = [half_step(low[i], high[i], spans[i], windows[i], coefficients) for i in range(2)]
    own_coarse = restricted(own_prior)
    next_coarse = ring(own_coarse, "tm", -1)

    ghosts, middle = [], []
    for i in range(2):
        there = slice(0, i + 1)
        ghosts.append(ghost_coefficients(
            place, cond, cond_before[there], cond_after[there], cond_spans[there], windows[i]))
        middle.append(two_steps(
            place, low[i], high[i], spans[i], before[i], after[i], spans[i],
            started[i], windows[i], windows[i], coefficients, ghosts[i]))
    coarse_coef = coarse_coefficients(place, coarse_cond, cond_before, cond_after, cond_spans)
    sides = [from_sides(b, a) for a, b in middle]
    spans = [[(*w, w[0])] for w in windows]
    ended = []
    for i in range(2):
        a, b = middle[i]
        part = half_step([a], [b], spans[i], windows[i], coefficients)
        ended.append(two_steps(
            place, [a], [b], spans[i], [sides[i][0]], [sides[i][1]], spans[i],
            part, windows[i], results[i], coefficients, ghosts[i], True))
    (moved, moved_coarse), (own_fine, fine_coarse) = ended

    jump = jumps_of(moved_coarse, fine_coarse, next_coarse, own_coarse)
    shifted = [jump] + [ring(jump, "tm", -j) for j in range(1, times)]
    state = joined(shifted[0], shifted[1])
    for j in range(home):
        before, after = from_sides(state, state)
        if j == 0:
            before, after, moved, *shifted[2:] = lax.optimization_barrier((before, after, moved, *shifted[2:]))
            moved = ring(moved, "tm", 1)
        more = (shifted[j + 1:j + 3], home - j - 1) if j < home - 1 else ()
        state = sweep_step(place, state, before, after, coarse_coef, j == 0, *more)
    update, tail = finish(moved, own_fine, own_prior, state)
    return update[None], tail[None]


def solution(mesh):
    return jax.shard_map(
        shards,
        mesh=mesh,
        in_specs=(P("space", None, None), P("tm", "space", None, None), P("space", None, None)),
        out_specs=(P("tm", "space", None, None), P("tm", "space", None, None)),
        check_vma=False,
    )
```

```python
import jax
import jax.numpy as jnp
from jax import lax
from jax.experimental import pallas as pl
from jax.experimental.pallas import tpu as pltpu
from jax.sharding import PartitionSpec as P

FINE_RATE = 0.16
HALF_FINE = 0.5 * FINE_RATE
HALF_COARSE = 0.25 * FINE_RATE
TILE = 8
OVERLAP = 8
LANES = 128

VMEM = pl.BlockSpec(memory_space=pltpu.VMEM)
SMEM = pl.BlockSpec(memory_space=pltpu.SMEM)
HBM = pl.BlockSpec(memory_space=pltpu.HBM)
F32 = jnp.float32


def call(body, out_shapes, operands, specs=None, scratch=(), out_specs=None):
    operands = list(operands)
    specs = specs or [VMEM] * len(operands)
    operands = [
        pltpu.with_memory_space_constraint(x, pltpu.HBM) if spec is HBM else x for x, spec in zip(operands, specs)
    ]
    return pl.pallas_call(
        body,
        out_shape=[jax.ShapeDtypeStruct(s, F32) for s in out_shapes],
        in_specs=specs,
        out_specs=out_specs or [VMEM] * len(out_shapes),
        scratch_shapes=list(scratch),
        compiler_params=pltpu.CompilerParams(vmem_limit_bytes=8 * 1024 * 1024),
    )(*operands)


def lane_scratch(rows, columns):
    return pltpu.VMEM((columns // LANES, rows, LANES), F32)


def split3(x):
    hi = x.astype(jnp.bfloat16)
    rest = x - hi.astype(F32)
    mid = rest.astype(jnp.bfloat16)
    low = (rest - mid.astype(F32)).astype(jnp.bfloat16)
    return hi, mid, low


def dot3(x, m):
    parts = [jnp.dot(p, m, preferred_element_type=F32) for p in split3(x)]
    return parts[0] + (parts[1] + parts[2])


def pair_matrix(fine, coarse, value):
    rows = lax.broadcasted_iota(jnp.int32, (fine, coarse), 0)
    cols = lax.broadcasted_iota(jnp.int32, (fine, coarse), 1)
    return jnp.where((rows >> 1) == cols, value, 0.0).astype(jnp.bfloat16)


def repeat_matrix(coarse, fine):
    rows = lax.broadcasted_iota(jnp.int32, (coarse, fine), 0)
    cols = lax.broadcasted_iota(jnp.int32, (coarse, fine), 1)
    return jnp.where(rows == (cols >> 1), 1.0, 0.0).astype(jnp.bfloat16)


def restrict_planes(first, second, scratch, matrix):
    blocks, ny, _ = scratch.shape
    sums = dot3(first + second, matrix)
    parts = []
    for b in range(blocks):
        scratch[b] = sums[:, b * LANES:(b + 1) * LANES]
        parts.append(scratch[b, pl.ds(0, ny // 2, 2), :] + scratch[b, pl.ds(1, ny // 2, 2), :])
    return jnp.concatenate(parts, axis=1)


class Field:
    def __init__(self, pieces, ny):
        self.pieces, self.ny = pieces, ny

    def find(self, row):
        for piece in self.pieces:
            if piece[0] <= row < piece[1]:
                return piece
        return None

    def rows(self, a, size):
        first, end, ref, index, base = self.find(a)
        return ref[index + (slice(a - base, a - base + size),)]

    def tile(self, a):
        return self.rows(a, TILE)

    def edge(self, a, row, shift, at):
        moved = pltpu.roll(self.tile(a), shift, 0)
        if self.find(row) is None:
            return moved
        place = lax.broadcasted_iota(jnp.int32, moved.shape, 0)
        return jnp.where(place == at, self.rows(row, 1), moved)

    def above(self, a):
        if self.find(a - 1) == self.find(a):
            return self.rows(a - 1, TILE)
        return self.edge(a, a - 1, 1, 0)

    def below(self, a):
        if self.find(a + TILE) == self.find(a):
            return self.rows(a + 1, TILE)
        return self.edge(a, a + TILE, TILE - 1, TILE - 1)


def plane(ref, index, ny):
    return Field([(0, ny, ref, index, 0)], ny)


def face_coefficients(k, above, below, half, a, size, ny, nz):
    row = lax.broadcasted_iota(jnp.int32, (size, nz), 0) + a
    col = lax.broadcasted_iota(jnp.int32, (size, nz), 1)
    up_face = half * (k + jnp.where(row == 0, 0.0, above))
    down_face = half * (k + jnp.where(row == ny - 1, 0.0, below))
    right = pltpu.roll(k, nz - 1, 1)
    left = pltpu.roll(k, 1, 1)
    right_face = half * (k + jnp.where(col == nz - 1, 0.0, right))
    left_face = half * (k + jnp.where(col == 0, 0.0, left))
    total = (up_face + down_face) + (right_face + left_face)
    return (
        jnp.where(row == 0, 0.0, up_face),
        jnp.where(row == ny - 1, 0.0, down_face),
        jnp.where(col == nz - 1, 0.0, right_face),
        total,
    )


def prepare_fine(cond):
    nx, ny, nz = cond.shape

    def body(k_ref, kx, up, down, right, diag):
        for p in range(nx):
            for a in range(0, ny, TILE):
                s = slice(a, a + TILE)
                k = k_ref[p, s]
                u, d, r, total = face_coefficients(
                    k, plane(k_ref, (p,), ny).above(a), plane(k_ref, (p,), ny).below(a),
                    HALF_FINE, a, TILE, ny, nz)
                up[p, s], down[p, s], right[p, s] = u, d, r
                if p > 0:
                    total = total + kx[p - 1, s]
                if p < nx - 1:
                    face = HALF_FINE * (k + k_ref[p + 1, s])
                    kx[p, s] = face
                    total = total + face
                diag[p, s] = 1.0 - total
    full = (nx, ny, nz)
    return call(body, [(nx - 1, ny, nz), full, full, full, full], [cond])


def restricted(field):
    nx, ny, nz = field.shape

    def body(f_ref, out, scratch):
        matrix = pair_matrix(nz, nz // 2, 0.125)
        for q in range(nx // 2):
            out[q] = restrict_planes(f_ref[2 * q], f_ref[2 * q + 1], scratch, matrix)

    return call(
        body, [(nx // 2, ny // 2, nz // 2)], [field], scratch=[lane_scratch(ny, nz // 2)]
    )[0]


def packed(half, nz, at, count):
    step = count // (2 * half)
    return [
        (slice(i * step, (i + 1) * step),
         (i // 2, slice(at, at + step), slice(i % 2 * nz // 2, (i % 2 + 1) * nz // 2)))
        for i in range(2 * half)
    ]


def row_copies(source, out, base, rows, at, sems, first_sem):
    start, end = rows
    return [
        pltpu.make_async_copy(
            source.at[base + p, pl.ds(start, end - start)], out.at[p, pl.ds(at, end - start)], sems.at[first_sem + p])
        for p in range(out.shape[0])
    ]


def run(copies):
    for c in copies:
        c.start()
    for c in copies:
        c.wait()


def chosen(flag, body, this, other):
    pl.when(flag > 0)(lambda: body(this))
    pl.when(flag == 0)(lambda: body(other))


def first_messages(place, initial, prior, cond, end, start):
    nx, ny, nz = cond.shape
    half = nx // 2

    def body(place_ref, i_ref, p_ref, k_ref, down, up, rows, sems):
        def copy(ref):
            copies = []
            for out, base in ((down, 0), (up, half)):
                for source, at in ((k_ref, 0), (ref, end)):
                    copies += row_copies(source, out, base, (0, end), at, sems, len(copies))
            run(copies + row_copies(p_ref, rows, 0, (start, ny), 0, sems, len(copies)))

        chosen(place_ref[3], copy, i_ref, p_ref)

    return call(
        body, [(half, 2 * end, nz)] * 2 + [(nx, ny - start, nz)], [place, initial, prior, cond], [SMEM, HBM, HBM, HBM],
        [pltpu.SemaphoreType.DMA((4 * half + nx,))])


def second_messages(cond, end, after):
    nx, ny, nz = cond.shape
    half, rows = nx // 2, ny - end
    extra = ny // 2 // (2 * half)

    def body(k_ref, after_ref, down, up, cond_out, coarse, scratch, sems):
        whole = [pltpu.make_async_copy(k_ref.at[p], cond_out.at[p], sems.at[p]) for p in range(nx)]
        run(whole)
        matrix = pair_matrix(nz, nz // 2, 0.125)
        for q in range(half):
            coarse[q] = restrict_planes(cond_out[2 * q], cond_out[2 * q + 1], scratch, matrix)
            down[q, :rows] = cond_out[q, end:]
            up[q, :rows] = cond_out[half + q, end:]
        for source, to in packed(half, nz, rows, ny // 2):
            down[to] = coarse[half - 1, source]
            up[to] = coarse[0, source]

    return call(
        body, [(half, rows + extra, nz)] * 2 + [(nx, ny, nz), (half, ny // 2, nz // 2)],
        [cond, after], [HBM, VMEM], [lane_scratch(ny, nz // 2), pltpu.SemaphoreType.DMA((nx,))])


def third_messages(place, initial, received, start):
    nx, ny, nz = initial.shape
    half = nx // 2

    def body(place_ref, i_ref, r_ref, down, up, sems):
        def copy(rows_of):
            ref, rows = rows_of
            run(row_copies(ref, down, 0, rows, 0, sems, 0) + row_copies(ref, up, half, rows, 0, sems, half))

        chosen(place_ref[4], copy, (i_ref, (start, ny)), (r_ref, (0, ny - start)))

    return call(
        body, [(half, ny - start, nz)] * 2, [place, initial, received], [SMEM, HBM, VMEM],
        [pltpu.SemaphoreType.DMA((nx,))])


def ghost_coefficients(place, cond, before, after, spans, window):
    nx, ny, nz = cond.shape
    half, count = nx // 2, len(spans)
    w0, w1 = window

    def body(place_ref, k_ref, *refs):
        lo = fields(spans, refs[:count], half, ny)
        hi = fields(spans, refs[count:2 * count], half, ny)
        kx, up, down, right, diag = refs[2 * count:]
        for side, near, far, inner, has in (
            (0, lo[half - 1], lo[half - 2], 0, place_ref[0] > 0),
            (1, hi[0], hi[1], nx - 1, place_ref[1] > 0),
        ):
            for a in range(w0, w1, TILE):
                s, d = slice(a, a + TILE), slice(a - w0, a - w0 + TILE)
                k = jnp.where(has, near.tile(a), 0.0)
                above, below = (jnp.where(has, x, 0.0) for x in (near.above(a), near.below(a)))
                u, v, r, total = face_coefficients(k, above, below, HALF_FINE, a, TILE, ny, nz)
                outer = HALF_FINE * (k + jnp.where(has, far.tile(a), 0.0))
                face = HALF_FINE * (k + k_ref[inner, s])
                kx[2 * side, d], kx[2 * side + 1, d] = outer, face
                up[side, d], down[side, d], right[side, d] = u, v, r
                diag[side, d] = 1.0 - ((total + outer) + face)

    rows = w1 - w0
    return call(
        body, [(4, rows, nz)] + [(2, rows, nz)] * 4, [place, cond, *before, *after],
        [SMEM] + [VMEM] * (1 + 2 * count))


def row_step(v, up, down, right, diag, a):
    c = v.tile(a)
    nz = c.shape[1]
    total = diag * c
    total = total + up * v.above(a)
    total = total + down * v.below(a)
    total = total + right * pltpu.roll(c, nz - 1, 1)
    return c, total + pltpu.roll(right * c, 1, 1)


def fields(spans, refs, half, ny):
    return [
        Field([(a, b, ref, (p,), base) for (a, b, base), ref in zip(spans, refs)], ny)
        for p in range(half)
    ]


def half_step(low, high, spans, window, coefficients, ahead=()):
    half, nz = low[0].shape[0], low[0].shape[2]
    nx, ny, count = 2 * half, coefficients[1].shape[1], len(spans)
    w0, w1 = window

    def body(*refs):
        kx, up, down, right, diag = refs[2 * count:2 * count + 5]
        out = refs[-1]
        v = fields(spans, refs[:count], half, ny) + fields(spans, refs[count:2 * count], half, ny)
        for p in range(nx):
            for a in range(w0, w1, TILE):
                s = slice(a, a + TILE)
                _, total = row_step(v[p], up[p, s], down[p, s], right[p, s], diag[p, s], a)
                if p > 0:
                    total = total + kx[p - 1, s] * v[p - 1].tile(a)
                if p < nx - 1:
                    total = total + kx[p, s] * v[p + 1].tile(a)
                out[p, a - w0:a - w0 + TILE] = total

    return call(body, [(nx, w1 - w0, nz)], [*low, *high, *coefficients, *ahead])[0]


def two_steps(place, low, high, spans, before, after, side_spans, started, window, result, coefficients, ghosts, final=False):
    half, nz = low[0].shape[0], low[0].shape[2]
    nx, ny = 2 * half, coefficients[1].shape[1]
    n, m = len(spans), len(side_spans)
    (w0, w1), (r0, r1) = window, result
    counts = [n, n, m, m]

    def body(place_ref, *refs):
        groups, at = [], 0
        for c in counts:
            groups.append(refs[at:at + c])
            at += c
        part, kx, up, down, right, diag, gx, gup, gdown, gright, gdiag, *rest = refs[at:]
        v = fields(spans, groups[0], half, ny) + fields(spans, groups[1], half, ny)
        lo = fields(side_spans, groups[2], half, ny)
        hi = fields(side_spans, groups[3], half, ny)
        has_lo, has_hi = place_ref[0] > 0, place_ref[1] > 0
        if final:
            out_ref, coarse_out, mid, scratch = rest
            out = [out_ref.at[p] for p in range(nx)]
        else:
            low_out, high_out, mid = rest
            out = [low_out.at[p] for p in range(half)] + [high_out.at[p] for p in range(half)]
        for a in range(w0, w1, TILE):
            s, d = slice(a, a + TILE), slice(a - w0, a - w0 + TILE)
            for side, near, far, has, own, ghost in (
                (0, lo[half - 1], lo[half - 2], has_lo, 0, 0),
                (1, hi[0], hi[1], has_hi, nx - 1, nx + 1),
            ):
                inner = v[own].tile(a)
                c, total = row_step(near, gup[side, d], gdown[side, d], gright[side, d], gdiag[side, d], a)
                total = total + gx[2 * side, d] * far.tile(a) + gx[2 * side + 1, d] * inner
                mid[ghost, d] = jnp.where(has, total, 0.0)
                mid[own + 1, d] = part[own, d] + gx[2 * side + 1, d] * (jnp.where(has, c, 0.0) - inner)
            for p in range(1, nx - 1):
                mid[p + 1, d] = part[p, d]
        w = [Field([(w0, w1, mid, (p,), w0)], ny) for p in range(nx + 2)]
        for p in range(nx):
            for a in range(r0, r1, TILE):
                s, d = slice(a, a + TILE), slice(a - w0, a - w0 + TILE)
                c, total = row_step(w[p + 1], up[p, s], down[p, s], right[p, s], diag[p, s], a)
                if p > 0:
                    total = total + kx[p - 1, s] * w[p].tile(a)
                else:
                    total = total + gx[1, d] * (w[p].tile(a) - c)
                if p < nx - 1:
                    total = total + kx[p, s] * w[p + 2].tile(a)
                else:
                    total = total + gx[3, d] * (w[p + 2].tile(a) - c)
                out[p][a - r0:a - r0 + TILE] = total
        if final:
            matrix = pair_matrix(nz, nz // 2, 0.125)
            for q in range(half):
                coarse_out[q] = restrict_planes(out[2 * q][...], out[2 * q + 1][...], scratch, matrix)

    operands = [place, *low, *high, *before, *after, started, *coefficients, *ghosts]
    scratch = [pltpu.VMEM((nx + 2, w1 - w0, nz), F32)]
    shapes = [(half, r1 - r0, nz)] * 2
    if final:
        scratch.append(lane_scratch(r1 - r0, nz // 2))
        shapes = [(nx, r1 - r0, nz), (half, (r1 - r0) // 2, nz // 2)]
    return call(body, shapes, operands, [SMEM] + [VMEM] * (len(operands) - 1), scratch)


def coarse_coefficients(place, own, before, after, spans):
    nx, ny, nz = own.shape
    planes, count = nx + 2, len(spans)

    def body(place_ref, k_own, *refs):
        sides = refs[:count], refs[count:2 * count]
        kx, up, down, right, diag, k_near, k_far, total, scratch = refs[2 * count:]
        matrix = pair_matrix(2 * nz, nz, 0.125)
        for i, (side, has) in enumerate(zip(sides, (place_ref[0] > 0, place_ref[1] > 0))):
            for (a, b, base), ref in zip(spans, side):
                total[a:b] = ref[0, a - base:b - base] + ref[1, a - base:b - base]
            near = restrict_planes(total[...], 0.0, scratch, matrix)
            k_near[i] = jnp.where(has, near, 0.0)
            last = side[-1]
            for rows, at in packed(nx, 2 * nz, last.shape[1] - ny // (2 * nx), ny):
                k_far[i, rows] = jnp.where(has, last[at], 0.0)

        def plane(i):
            if i == 0:
                return k_far[0]
            if i == 1:
                return k_near[0]
            if i < nx + 2:
                return k_own[i - 2]
            return k_near[1] if i == nx + 2 else k_far[1]

        for i in range(planes + 1):
            kx[i] = HALF_COARSE * (plane(i) + plane(i + 1))
        for p in range(planes):
            k = plane(p + 1)
            u, d, r, total = face_coefficients(
                k, pltpu.roll(k, 1, 0), pltpu.roll(k, ny - 1, 0), HALF_COARSE, 0, ny, ny, nz)
            up[p], down[p], right[p] = u, d, r
            diag[p] = 1.0 - (total + kx[p] + kx[p + 1])

    full = (planes, ny, nz)
    return call(
        body, [(planes + 1, ny, nz)] + [full] * 4, [place, own, *before, *after],
        [SMEM] + [VMEM] * (1 + 2 * count),
        [pltpu.VMEM((2, ny, nz), F32), pltpu.VMEM((2, ny, nz), F32),
         pltpu.VMEM((2 * ny, 2 * nz), F32), lane_scratch(2 * ny, nz)])


def sweep_step(place, own, on, off, coefficients, first, jumps=(), later=0):
    nx, ny, nz = own.shape

    def body(place_ref, d_own, d_on, d_off, kx, up, down, right, diag, *rest):
        even = place_ref[5] > 0
        live = place_ref[3] > 0 if first else True
        has_lo = jnp.logical_and(place_ref[0] > 0, live)
        has_hi = jnp.logical_and(place_ref[1] > 0, live)

        def step(v, i):
            c = v[1]
            total = diag[i] * c + kx[i] * v[0] + kx[i + 1] * v[2]
            total = total + up[i] * pltpu.roll(c, 1, 0) + down[i] * pltpu.roll(c, ny - 1, 0)
            return total + right[i] * pltpu.roll(c, nz - 1, 1) + pltpu.roll(right[i] * c, 1, 1)

        lo = [jnp.where(has_lo, jnp.where(even, d_off[nx - 2 + i], d_on[nx - 2 + i]), 0.0) for i in range(2)]
        hi = [jnp.where(has_hi, jnp.where(even, d_on[i], d_off[i]), 0.0) for i in range(2)]
        block = [jnp.where(live, d_own[i], 0.0) if first else d_own[i] for i in range(nx)]
        v = lo + block + hi
        w = [step(v[i:i + 3], i) for i in range(nx + 2)]
        w[0] = jnp.where(has_lo, w[0], 0.0)
        w[-1] = jnp.where(has_hi, w[-1], 0.0)
        for i in range(nx):
            e = step(w[i:i + 3], i + 1)
            if jumps:
                e = e + jnp.where(place_ref[2] >= later, joined(rest[0][i], rest[1][i]), 0.0)
            rest[-1][i] = e

    operands = [place, own, on, off, *coefficients]
    operands += jumps
    return call(body, [own.shape], operands, [SMEM] + [VMEM] * (len(operands) - 1))[0]


def jumps_of(moved, own, next_prior, own_prior):
    nx, rows, nz = moved.shape

    def body(a_ref, b_ref, next_ref, own_ref, out):
        for p in range(nx):
            out[p, :rows] = a_ref[p] - next_ref[p, :rows]
            out[p, rows:] = b_ref[p] - own_ref[p, rows:]

    return call(body, [own_prior.shape], [moved, own, next_prior, own_prior])[0]


def joined(upper, lower):
    rows = upper.shape[-2]
    row = lax.broadcasted_iota(jnp.int32, upper.shape, upper.ndim - 2)
    return jnp.where(row < rows // 2, upper, lower)


def finish(moved, own, prior, correction):
    nx, ny, nz = prior.shape
    rows = moved.shape[1]

    def body(moved_ref, own_ref, p_ref, e_ref, update, tail, out, wide, scratch, sems):
        parts = ((moved_ref, slice(0, rows)), (own_ref, slice(rows, ny)))
        spread = repeat_matrix(nz // 2, nz)
        copies = []
        for q in range(nx // 2):
            row = dot3(e_ref[q], spread)
            for b in range(nz // LANES):
                s = slice(b * LANES, (b + 1) * LANES)
                wide[b, pl.ds(0, ny // 2, 2), :] = row[:, s]
                wide[b, pl.ds(1, ny // 2, 2), :] = row[:, s]
            for p in (2 * q, 2 * q + 1):
                for ref, r in parts:
                    for b in range(nz // LANES):
                        s = slice(b * LANES, (b + 1) * LANES)
                        out[p, r, s] = (ref[p, :, s] + wide[b, r]) - p_ref[p, r, s]
                copies.append(pltpu.make_async_copy(out.at[p], update.at[p], sems.at[p]))
                copies[-1].start()
        matrix = pair_matrix(nz, nz // 2, 0.125)
        for q in range(nx // 2):
            for ref, r in parts:
                c = slice(r.start // 2, r.stop // 2)
                tail[q, c] = e_ref[q, c] + restrict_planes(ref[2 * q], ref[2 * q + 1], scratch, matrix)
        for c in copies:
            c.wait()

    return call(
        body, [prior.shape, correction.shape], [moved, own, prior, correction],
        scratch=[pltpu.VMEM(prior.shape, F32), lane_scratch(ny, nz), lane_scratch(rows, nz // 2),
                 pltpu.SemaphoreType.DMA((nx,))],
        out_specs=[HBM, VMEM])


def ring(block, axis, distance):
    size = lax.axis_size(axis)
    return lax.ppermute(block, axis, [(i, (i + distance) % size) for i in range(size)])


def from_sides(last, first):
    return ring(last, "space", 1), ring(first, "space", -1)


def swapped(block, axis, offset):
    size = lax.axis_size(axis)
    pairs = [(i % size, (i + 1) % size) for i in range(offset, size + offset, 2)]
    return lax.ppermute(block, axis, pairs + [(j, i) for i, j in pairs])


def shards(initial, prior, conductivity):
    t, times = lax.axis_index("tm"), lax.axis_size("tm")
    s, blocks = lax.axis_index("space"), lax.axis_size("space")
    own_prior = prior[0]
    home = times - 1
    place = jnp.stack([s > 0, s < blocks - 1, t, t == home, t == 0, s % 2 == 0]).astype(jnp.int32)
    ny = initial.shape[1]
    cut, wide = ny // 2, ny // 2 + OVERLAP
    windows = [(0, wide), (cut - OVERLAP, ny)]
    results = [(0, cut), (cut, ny)]

    down, up, lower_prior = first_messages(place, initial, own_prior, conductivity, wide, windows[1][0])
    before, after = ([x] for x in from_sides(up, down))
    received = ring(lower_prior, "tm", 1)
    down_2, up_2, cond, coarse_cond = second_messages(conductivity, wide, up)
    before_2, after_2 = from_sides(up_2, down_2)
    down_3, up_3 = third_messages(place, initial, received, windows[1][0])
    before_3, after_3 = from_sides(up_3, down_3)

    coefficients = prepare_fine(cond)
    cond_spans = [(0, wide, 0), (wide, ny, wide)]
    cond_before, cond_after = (before[0], before_2), (after[0], after_2)
    low, high = [[down], [down_3]], [[up], [up_3]]
    before, after = [before, [before_3]], [after, [after_3]]
    spans = [[(0, wide, -wide)], [(*windows[1], windows[1][0])]]
    started = [half_step(low[i], high[i], spans[i], windows[i], coefficients) for i in range(2)]
    own_coarse = restricted(own_prior)
    next_coarse = ring(own_coarse, "tm", -1)

    ghosts, middle = [], []
    for i in range(2):
        there = slice(0, i + 1)
        ghosts.append(ghost_coefficients(
            place, cond, cond_before[there], cond_after[there], cond_spans[there], windows[i]))
        middle.append(two_steps(
            place, low[i], high[i], spans[i], before[i], after[i], spans[i],
            started[i], windows[i], windows[i], coefficients, ghosts[i]))
    coarse_coef = coarse_coefficients(place, coarse_cond, cond_before, cond_after, cond_spans)
    sides = [from_sides(b, a) for a, b in middle]
    spans = [[(*w, w[0])] for w in windows]
    ended = []
    for i in range(2):
        a, b = middle[i]
        part = half_step([a], [b], spans[i], windows[i], coefficients, coarse_coef[:i])
        ended.append(two_steps(
            place, [a], [b], spans[i], [sides[i][0]], [sides[i][1]], spans[i],
            part, windows[i], results[i], coefficients, ghosts[i], True))
    (moved, moved_coarse), (own_fine, fine_coarse) = ended

    jump = jumps_of(moved_coarse, fine_coarse, next_coarse, own_coarse)
    lower = ring(jump[:, jump.shape[1] // 2:], "tm", -home)
    shifted = [jump] + [ring(jump, "tm", -j) for j in range(1, home)] + [jnp.concatenate([lower, lower], axis=1)]
    state = joined(shifted[0], shifted[1])
    for j in range(home):
        off, on = swapped(state, "space", 1), swapped(state, "space", 0)
        if j == 0:
            *_, moved = lax.optimization_barrier((on, off, lower, *shifted[2:home], moved))
            moved = ring(moved, "tm", 1)
        more = (shifted[j + 1:j + 3], home - j - 1) if j < home - 1 else ()
        state = sweep_step(place, state, on, off, coarse_coef, j == 0, *more)
    update, tail = finish(moved, own_fine, own_prior, state)
    return update[None], tail[None]


def solution(mesh):
    return jax.shard_map(
        shards,
        mesh=mesh,
        in_specs=(P("space", None, None), P("tm", "space", None, None), P("space", None, None)),
        out_specs=(P("tm", "space", None, None), P("tm", "space", None, None)),
        check_vma=False,
    )
```

```python
from typing import Any, NamedTuple

import jax
import jax.numpy as jnp
from jax import lax
from jax.experimental import pallas as pl
from jax.experimental.pallas import tpu as pltpu
from jax.sharding import PartitionSpec as P

FINE_RATE = 0.16
HALF_FINE = 0.5 * FINE_RATE
HALF_COARSE = 0.25 * FINE_RATE
TILE = 8
OVERLAP = 8
LANES = 128

VMEM = pl.BlockSpec(memory_space=pltpu.VMEM)
HBM = pl.BlockSpec(memory_space=pltpu.HBM)
F32 = jnp.float32


class Here(NamedTuple):
    t: Any
    first: Any
    last: Any
    has_lo: Any
    has_hi: Any
    even: Any


def here():
    t, s = lax.axis_index("tm"), lax.axis_index("space")
    times, blocks = lax.axis_size("tm"), lax.axis_size("space")
    return Here(t, t == 0, t == times - 1, s > 0, s < blocks - 1, lax.rem(s, 2) == 0)


def call(body, out_shapes, operands, specs=None, scratch=(), out_specs=None):
    operands = list(operands)
    specs = specs or [VMEM] * len(operands)
    operands = [
        pltpu.with_memory_space_constraint(x, pltpu.HBM) if spec is HBM else x for x, spec in zip(operands, specs)
    ]
    return pl.pallas_call(
        body,
        out_shape=[jax.ShapeDtypeStruct(s, F32) for s in out_shapes],
        in_specs=specs,
        out_specs=out_specs or [VMEM] * len(out_shapes),
        scratch_shapes=list(scratch),
        compiler_params=pltpu.CompilerParams(vmem_limit_bytes=8 * 1024 * 1024),
    )(*operands)


def lane_scratch(rows, columns):
    return pltpu.VMEM((columns // LANES, rows, LANES), F32)


def split3(x):
    hi = x.astype(jnp.bfloat16)
    rest = x - hi.astype(F32)
    mid = rest.astype(jnp.bfloat16)
    low = (rest - mid.astype(F32)).astype(jnp.bfloat16)
    return hi, mid, low


def dot3(x, m):
    parts = [jnp.dot(p, m, preferred_element_type=F32) for p in split3(x)]
    return parts[0] + (parts[1] + parts[2])


def pair_matrix(fine, coarse, value):
    rows = lax.broadcasted_iota(jnp.int32, (fine, coarse), 0)
    cols = lax.broadcasted_iota(jnp.int32, (fine, coarse), 1)
    return jnp.where((rows >> 1) == cols, value, 0.0).astype(jnp.bfloat16)


def repeat_matrix(coarse, fine):
    rows = lax.broadcasted_iota(jnp.int32, (coarse, fine), 0)
    cols = lax.broadcasted_iota(jnp.int32, (coarse, fine), 1)
    return jnp.where(rows == (cols >> 1), 1.0, 0.0).astype(jnp.bfloat16)


def restrict_planes(first, second, scratch, matrix):
    blocks, ny, _ = scratch.shape
    sums = dot3(first + second, matrix)
    parts = []
    for b in range(blocks):
        scratch[b] = sums[:, b * LANES:(b + 1) * LANES]
        parts.append(scratch[b, pl.ds(0, ny // 2, 2), :] + scratch[b, pl.ds(1, ny // 2, 2), :])
    return jnp.concatenate(parts, axis=1)


class Field:
    def __init__(self, pieces, edges):
        self.pieces, self.edges, self.moved = pieces, edges, {}

    def tile(self, a):
        for first, end, ref, index, base in self.pieces:
            if first <= a and a + TILE <= end:
                return ref[index + (slice(a - base, a - base + TILE),)]
        return None

    def rolled(self, a, shift):
        if (a, shift) not in self.moved:
            tile = self.tile(a)
            self.moved[a, shift] = None if tile is None else pltpu.roll(tile, shift, 0)
        return self.moved[a, shift]

    def neighbour(self, a, other, shift, edge):
        own, next_ = self.rolled(a, shift), self.rolled(other, shift)
        return own if next_ is None else jnp.where(edge, next_, own)

    def above(self, a):
        return self.neighbour(a, a - TILE, 1, self.edges[0])

    def below(self, a):
        return self.neighbour(a, a + TILE, TILE - 1, self.edges[1])


def edges(nz):
    row = lax.broadcasted_iota(jnp.int32, (TILE, nz), 0)
    return row == 0, row == TILE - 1


def fields(spans, refs, planes, nz):
    e = edges(nz)
    return [
        Field([(a, b, ref, (p,), base) for (a, b, base), ref in zip(spans, refs)], e)
        for p in range(planes)
    ]


def face_coefficients(k, above, below, half, a, size, ny, nz):
    row = lax.broadcasted_iota(jnp.int32, (size, nz), 0) + a
    col = lax.broadcasted_iota(jnp.int32, (size, nz), 1)
    up_face = half * (k + jnp.where(row == 0, 0.0, above))
    down_face = half * (k + jnp.where(row == ny - 1, 0.0, below))
    right = pltpu.roll(k, nz - 1, 1)
    left = pltpu.roll(k, 1, 1)
    right_face = half * (k + jnp.where(col == nz - 1, 0.0, right))
    left_face = half * (k + jnp.where(col == 0, 0.0, left))
    total = (up_face + down_face) + (right_face + left_face)
    return (
        jnp.where(row == 0, 0.0, up_face),
        jnp.where(row == ny - 1, 0.0, down_face),
        jnp.where(col == nz - 1, 0.0, right_face),
        total,
    )


def prepare_fine(cond):
    nx, ny, nz = cond.shape

    def body(k_ref, kx, up, down, right, diag):
        planes = fields([(0, ny, 0)], [k_ref], nx, nz)
        for p in range(nx):
            for a in range(0, ny, TILE):
                s = slice(a, a + TILE)
                k = k_ref[p, s]
                u, d, r, total = face_coefficients(
                    k, planes[p].above(a), planes[p].below(a), HALF_FINE, a, TILE, ny, nz)
                up[p, s], down[p, s], right[p, s] = u, d, r
                if p > 0:
                    total = total + kx[p - 1, s]
                if p < nx - 1:
                    face = HALF_FINE * (k + k_ref[p + 1, s])
                    kx[p, s] = face
                    total = total + face
                diag[p, s] = 1.0 - total
    full = (nx, ny, nz)
    return call(body, [(nx - 1, ny, nz), full, full, full, full], [cond])


def restricted(field):
    nx, ny, nz = field.shape

    def body(f_ref, out, scratch):
        matrix = pair_matrix(nz, nz // 2, 0.125)
        for q in range(nx // 2):
            out[q] = restrict_planes(f_ref[2 * q], f_ref[2 * q + 1], scratch, matrix)

    return call(
        body, [(nx // 2, ny // 2, nz // 2)], [field], scratch=[lane_scratch(ny, nz // 2)]
    )[0]


def packed(half, nz, at, count):
    step = count // (2 * half)
    return [
        (slice(i * step, (i + 1) * step),
         (i // 2, slice(at, at + step), slice(i % 2 * nz // 2, (i % 2 + 1) * nz // 2)))
        for i in range(2 * half)
    ]


def row_copies(source, out, base, rows, at, sems, first_sem):
    start, end = rows
    return [
        pltpu.make_async_copy(
            source.at[base + p, pl.ds(start, end - start)], out.at[p, pl.ds(at, end - start)], sems.at[first_sem + p])
        for p in range(out.shape[0])
    ]


def run(copies):
    for c in copies:
        c.start()
    for c in copies:
        c.wait()


def chosen(flag, body, this, other):
    pl.when(flag)(lambda: body(this))
    pl.when(jnp.logical_not(flag))(lambda: body(other))


def first_messages(initial, prior, cond, end):
    nx, ny, nz = cond.shape
    half = nx // 2

    def body(i_ref, p_ref, k_ref, down, up, sems):
        def copy(ref):
            copies = []
            for out, base in ((down, 0), (up, half)):
                for source, at in ((k_ref, 0), (ref, end)):
                    copies += row_copies(source, out, base, (0, end), at, sems, len(copies))
            run(copies)

        chosen(here().last, copy, i_ref, p_ref)

    return call(
        body, [(half, 2 * end, nz)] * 2, [initial, prior, cond], [HBM, HBM, HBM],
        [pltpu.SemaphoreType.DMA((4 * half,))])


def rows_from(field, start):
    nx, ny, nz = field.shape

    def body(ref, out, sems):
        run(row_copies(ref, out, 0, (start, ny), 0, sems, 0))

    return call(body, [(nx, ny - start, nz)], [field], [HBM], [pltpu.SemaphoreType.DMA((nx,))])[0]


def second_messages(cond, end, after):
    nx, ny, nz = cond.shape
    half, rows = nx // 2, ny - end
    extra = ny // 2 // (2 * half)

    def body(k_ref, after_ref, down, up, cond_out, coarse, scratch, sems):
        whole = [pltpu.make_async_copy(k_ref.at[p], cond_out.at[p], sems.at[p]) for p in range(nx)]
        run(whole)
        matrix = pair_matrix(nz, nz // 2, 0.125)
        for q in range(half):
            coarse[q] = restrict_planes(cond_out[2 * q], cond_out[2 * q + 1], scratch, matrix)
            down[q, :rows] = cond_out[q, end:]
            up[q, :rows] = cond_out[half + q, end:]
        for source, to in packed(half, nz, rows, ny // 2):
            down[to] = coarse[half - 1, source]
            up[to] = coarse[0, source]

    return call(
        body, [(half, rows + extra, nz)] * 2 + [(nx, ny, nz), (half, ny // 2, nz // 2)],
        [cond, after], [HBM, VMEM], [lane_scratch(ny, nz // 2), pltpu.SemaphoreType.DMA((nx,))])


def third_messages(initial, received, start, after):
    nx, ny, nz = initial.shape
    half = nx // 2

    def body(i_ref, r_ref, after_ref, down, up, sems):
        def copy(rows_of):
            ref, rows = rows_of
            run(row_copies(ref, down, 0, rows, 0, sems, 0) + row_copies(ref, up, half, rows, 0, sems, half))

        chosen(here().first, copy, (i_ref, (start, ny)), (r_ref, (0, ny - start)))

    return call(
        body, [(half, ny - start, nz)] * 2, [initial, received, after], [HBM, VMEM, VMEM],
        [pltpu.SemaphoreType.DMA((nx,))])


def ghost_coefficients(cond, before, after, spans, window):
    nx, ny, nz = cond.shape
    half, count = nx // 2, len(spans)
    w0, w1 = window

    def body(k_ref, *refs):
        me = here()
        lo = fields(spans, refs[:count], half, nz)
        hi = fields(spans, refs[count:2 * count], half, nz)
        kx, up, down, right, diag = refs[2 * count:]
        for side, near, far, inner, has in (
            (0, lo[half - 1], lo[half - 2], 0, me.has_lo),
            (1, hi[0], hi[1], nx - 1, me.has_hi),
        ):
            for a in range(w0, w1, TILE):
                s, d = slice(a, a + TILE), slice(a - w0, a - w0 + TILE)
                k = jnp.where(has, near.tile(a), 0.0)
                above, below = (jnp.where(has, x, 0.0) for x in (near.above(a), near.below(a)))
                u, v, r, total = face_coefficients(k, above, below, HALF_FINE, a, TILE, ny, nz)
                outer = HALF_FINE * (k + jnp.where(has, far.tile(a), 0.0))
                face = HALF_FINE * (k + k_ref[inner, s])
                kx[2 * side, d], kx[2 * side + 1, d] = outer, face
                up[side, d], down[side, d], right[side, d] = u, v, r
                diag[side, d] = 1.0 - ((total + outer) + face)

    rows = w1 - w0
    return call(
        body, [(4, rows, nz)] + [(2, rows, nz)] * 4, [cond, *before, *after],
        [VMEM] * (1 + 2 * count))


def row_step(v, up, down, right, diag, a):
    c = v.tile(a)
    nz = c.shape[1]
    total = diag * c
    total = total + up * v.above(a)
    total = total + down * v.below(a)
    total = total + right * pltpu.roll(c, nz - 1, 1)
    return c, total + pltpu.roll(right * c, 1, 1)


def half_step(low, high, spans, window, coefficients, ahead=()):
    half, nz = low[0].shape[0], low[0].shape[2]
    nx, ny, count = 2 * half, coefficients[1].shape[1], len(spans)
    w0, w1 = window

    def body(*refs):
        kx, up, down, right, diag = refs[2 * count:2 * count + 5]
        out = refs[-1]
        v = fields(spans, refs[:count], half, nz) + fields(spans, refs[count:2 * count], half, nz)
        for p in range(nx):
            for a in range(w0, w1, TILE):
                s = slice(a, a + TILE)
                _, total = row_step(v[p], up[p, s], down[p, s], right[p, s], diag[p, s], a)
                if p > 0:
                    total = total + kx[p - 1, s] * v[p - 1].tile(a)
                if p < nx - 1:
                    total = total + kx[p, s] * v[p + 1].tile(a)
                out[p, a - w0:a - w0 + TILE] = total

    return call(body, [(nx, w1 - w0, nz)], [*low, *high, *coefficients, *ahead])[0]


def two_steps(low, high, spans, before, after, side_spans, started, window, result, coefficients, ghosts, final=False):
    half, nz = low[0].shape[0], low[0].shape[2]
    nx, ny = 2 * half, coefficients[1].shape[1]
    n, m = len(spans), len(side_spans)
    (w0, w1), (r0, r1) = window, result
    counts = [n, n, m, m]

    def body(*refs):
        groups, at = [], 0
        for c in counts:
            groups.append(refs[at:at + c])
            at += c
        part, kx, up, down, right, diag, gx, gup, gdown, gright, gdiag, *rest = refs[at:]
        v = fields(spans, groups[0], half, nz) + fields(spans, groups[1], half, nz)
        lo = fields(side_spans, groups[2], half, nz)
        hi = fields(side_spans, groups[3], half, nz)
        has_lo, has_hi = here().has_lo, here().has_hi
        if final:
            out_ref, coarse_out, mid, scratch = rest
            out = [out_ref.at[p] for p in range(nx)]
        else:
            low_out, high_out, mid = rest
            out = [low_out.at[p] for p in range(half)] + [high_out.at[p] for p in range(half)]
        for a in range(w0, w1, TILE):
            s, d = slice(a, a + TILE), slice(a - w0, a - w0 + TILE)
            for side, near, far, has, own, ghost in (
                (0, lo[half - 1], lo[half - 2], has_lo, 0, 0),
                (1, hi[0], hi[1], has_hi, nx - 1, nx + 1),
            ):
                inner = v[own].tile(a)
                c, total = row_step(near, gup[side, d], gdown[side, d], gright[side, d], gdiag[side, d], a)
                total = total + gx[2 * side, d] * far.tile(a) + gx[2 * side + 1, d] * inner
                mid[ghost, d] = jnp.where(has, total, 0.0)
                mid[own + 1, d] = part[own, d] + gx[2 * side + 1, d] * (jnp.where(has, c, 0.0) - inner)
            for p in range(1, nx - 1):
                mid[p + 1, d] = part[p, d]
        w = fields([(w0, w1, w0)], [mid], nx + 2, nz)
        for p in range(nx):
            for a in range(r0, r1, TILE):
                s, d = slice(a, a + TILE), slice(a - w0, a - w0 + TILE)
                c, total = row_step(w[p + 1], up[p, s], down[p, s], right[p, s], diag[p, s], a)
                if p > 0:
                    total = total + kx[p - 1, s] * w[p].tile(a)
                else:
                    total = total + gx[1, d] * (w[p].tile(a) - c)
                if p < nx - 1:
                    total = total + kx[p, s] * w[p + 2].tile(a)
                else:
                    total = total + gx[3, d] * (w[p + 2].tile(a) - c)
                out[p][a - r0:a - r0 + TILE] = total
        if final:
            matrix = pair_matrix(nz, nz // 2, 0.125)
            for q in range(half):
                coarse_out[q] = restrict_planes(out[2 * q][...], out[2 * q + 1][...], scratch, matrix)

    operands = [*low, *high, *before, *after, started, *coefficients, *ghosts]
    scratch = [pltpu.VMEM((nx + 2, w1 - w0, nz), F32)]
    shapes = [(half, r1 - r0, nz)] * 2
    if final:
        scratch.append(lane_scratch(r1 - r0, nz // 2))
        shapes = [(nx, r1 - r0, nz), (half, (r1 - r0) // 2, nz // 2)]
    return call(body, shapes, operands, [VMEM] * len(operands), scratch)


def coarse_coefficients(own, before, after, spans):
    nx, ny, nz = own.shape
    planes, count = nx + 2, len(spans)

    def body(k_own, *refs):
        sides = refs[:count], refs[count:2 * count]
        kx, up, down, right, diag, k_near, k_far, total, scratch = refs[2 * count:]
        matrix = pair_matrix(2 * nz, nz, 0.125)
        for i, (side, has) in enumerate(zip(sides, (here().has_lo, here().has_hi))):
            for (a, b, base), ref in zip(spans, side):
                total[a:b] = ref[0, a - base:b - base] + ref[1, a - base:b - base]
            near = restrict_planes(total[...], 0.0, scratch, matrix)
            k_near[i] = jnp.where(has, near, 0.0)
            last = side[-1]
            for rows, at in packed(nx, 2 * nz, last.shape[1] - ny // (2 * nx), ny):
                k_far[i, rows] = jnp.where(has, last[at], 0.0)

        def plane(i):
            if i == 0:
                return k_far[0]
            if i == 1:
                return k_near[0]
            if i < nx + 2:
                return k_own[i - 2]
            return k_near[1] if i == nx + 2 else k_far[1]

        for i in range(planes + 1):
            kx[i] = HALF_COARSE * (plane(i) + plane(i + 1))
        for p in range(planes):
            k = plane(p + 1)
            u, d, r, total = face_coefficients(
                k, pltpu.roll(k, 1, 0), pltpu.roll(k, ny - 1, 0), HALF_COARSE, 0, ny, ny, nz)
            up[p], down[p], right[p] = u, d, r
            diag[p] = 1.0 - (total + kx[p] + kx[p + 1])

    full = (planes, ny, nz)
    return call(
        body, [(planes + 1, ny, nz)] + [full] * 4, [own, *before, *after],
        [VMEM] * (1 + 2 * count),
        [pltpu.VMEM((2, ny, nz), F32), pltpu.VMEM((2, ny, nz), F32),
         pltpu.VMEM((2 * ny, 2 * nz), F32), lane_scratch(2 * ny, nz)])


def sweep_step(own, on, off, coefficients, first, jumps=(), later=0):
    nx, ny, nz = own.shape

    def body(d_own, d_on, d_off, kx, up, down, right, diag, *rest):
        out, v_ref, w_ref = rest[-3:]
        me = here()
        even, has_lo, has_hi = me.even, me.has_lo, me.has_hi
        if first:
            has_lo, has_hi = (jnp.logical_and(x, me.last) for x in (has_lo, has_hi))
        tiles = [(a, slice(a, a + TILE)) for a in range(0, ny, TILE)]
        for a, s in tiles:
            for i in range(2):
                near = nx - 2 + i
                v_ref[i, s] = jnp.where(has_lo, jnp.where(even, d_off[near, s], d_on[near, s]), 0.0)
                v_ref[nx + 2 + i, s] = jnp.where(has_hi, jnp.where(even, d_on[i, s], d_off[i, s]), 0.0)
            for i in range(nx):
                v_ref[2 + i, s] = jnp.where(me.last, d_own[i, s], 0.0) if first else d_own[i, s]
        v = fields([(0, ny, 0)], [v_ref], nx + 4, nz)
        w = fields([(0, ny, 0)], [w_ref], nx + 2, nz)

        def step(planes, i, a, s):
            _, total = row_step(planes[i + 1], up[i, s], down[i, s], right[i, s], diag[i, s], a)
            return total + kx[i, s] * planes[i].tile(a) + kx[i + 1, s] * planes[i + 2].tile(a)

        for i in range(nx + 2):
            for a, s in tiles:
                total = step(v, i, a, s)
                if i == 0:
                    total = jnp.where(has_lo, total, 0.0)
                if i == nx + 1:
                    total = jnp.where(has_hi, total, 0.0)
                w_ref[i, s] = total
        for i in range(nx):
            for a, s in tiles:
                _, e = row_step(w[i + 1], up[i + 1, s], down[i + 1, s], right[i + 1, s], diag[i + 1, s], a)
                e = e + kx[i + 1, s] * w[i].tile(a) + kx[i + 2, s] * w[i + 2].tile(a)
                if jumps:
                    jump = rest[0 if a < ny // 2 else 1][i, s]
                    e = e + jnp.where(me.t >= later, jump, 0.0)
                out[i, s] = e

    operands = [own, on, off, *coefficients, *jumps]
    return call(
        body, [own.shape], operands, [VMEM] * len(operands),
        [pltpu.VMEM((nx + 4, ny, nz), F32), pltpu.VMEM((nx + 2, ny, nz), F32)])[0]


def joined(upper, lower):
    rows = upper.shape[-2]
    row = lax.broadcasted_iota(jnp.int32, upper.shape, upper.ndim - 2)
    return jnp.where(row < rows // 2, upper, lower)


def jumps_of(moved, own, next_prior, own_prior):
    nx, rows, nz = moved.shape

    def body(a_ref, b_ref, next_ref, own_ref, out):
        for p in range(nx):
            out[p, :rows] = a_ref[p] - next_ref[p, :rows]
            out[p, rows:] = b_ref[p] - own_ref[p, rows:]

    return call(body, [own_prior.shape], [moved, own, next_prior, own_prior])[0]


def finish(moved, own, prior, correction):
    nx, ny, nz = prior.shape
    rows = moved.shape[1]

    def body(moved_ref, own_ref, p_ref, e_ref, update, tail, out, wide, scratch, sems):
        parts = ((moved_ref, slice(0, rows)), (own_ref, slice(rows, ny)))
        spread = repeat_matrix(nz // 2, nz)
        copies = []
        for q in range(nx // 2):
            row = dot3(e_ref[q], spread)
            for b in range(nz // LANES):
                s = slice(b * LANES, (b + 1) * LANES)
                wide[b, pl.ds(0, ny // 2, 2), :] = row[:, s]
                wide[b, pl.ds(1, ny // 2, 2), :] = row[:, s]
            for p in (2 * q, 2 * q + 1):
                for ref, r in parts:
                    for b in range(nz // LANES):
                        s = slice(b * LANES, (b + 1) * LANES)
                        out[p, r, s] = (ref[p, :, s] + wide[b, r]) - p_ref[p, r, s]
                copies.append(pltpu.make_async_copy(out.at[p], update.at[p], sems.at[p]))
                copies[-1].start()
        matrix = pair_matrix(nz, nz // 2, 0.125)
        for q in range(nx // 2):
            for ref, r in parts:
                c = slice(r.start // 2, r.stop // 2)
                tail[q, c] = e_ref[q, c] + restrict_planes(ref[2 * q], ref[2 * q + 1], scratch, matrix)
        for c in copies:
            c.wait()

    return call(
        body, [prior.shape, correction.shape], [moved, own, prior, correction],
        scratch=[pltpu.VMEM(prior.shape, F32), lane_scratch(ny, nz), lane_scratch(rows, nz // 2),
                 pltpu.SemaphoreType.DMA((nx,))],
        out_specs=[HBM, VMEM])


def ring(block, axis, distance):
    size = lax.axis_size(axis)
    return lax.ppermute(block, axis, [(i, (i + distance) % size) for i in range(size)])


def from_sides(last, first):
    return ring(last, "space", 1), ring(first, "space", -1)


def swapped(block, axis, offset):
    size = lax.axis_size(axis)
    pairs = [(i % size, (i + 1) % size) for i in range(offset, size + offset, 2)]
    return lax.ppermute(block, axis, pairs + [(j, i) for i, j in pairs])


def shards(initial, prior, conductivity):
    t, times = lax.axis_index("tm"), lax.axis_size("tm")
    s, blocks = lax.axis_index("space"), lax.axis_size("space")
    own_prior = prior[0]
    home = times - 1
    ny = initial.shape[1]
    cut, wide = ny // 2, ny // 2 + OVERLAP
    windows = [(0, wide), (cut - OVERLAP, ny)]
    results = [(0, cut), (cut, ny)]

    down, up = first_messages(initial, own_prior, conductivity, wide)
    before, after = ([x] for x in from_sides(up, down))
    received = ring(rows_from(own_prior, windows[1][0]), "tm", 1)
    down_2, up_2, cond, coarse_cond = second_messages(conductivity, wide, up)
    before_2, after_2 = from_sides(up_2, down_2)
    down_3, up_3 = third_messages(initial, received, windows[1][0], before[0])
    before_3, after_3 = from_sides(up_3, down_3)

    coefficients = prepare_fine(cond)
    cond_spans = [(0, wide, 0), (wide, ny, wide)]
    cond_before, cond_after = (before[0], before_2), (after[0], after_2)
    low, high = [[down], [down_3]], [[up], [up_3]]
    before, after = [before, [before_3]], [after, [after_3]]
    spans = [[(0, wide, -wide)], [(*windows[1], windows[1][0])]]
    started = [half_step(low[i], high[i], spans[i], windows[i], coefficients) for i in range(2)]
    own_coarse = restricted(own_prior)
    next_coarse = ring(own_coarse, "tm", -1)

    ghosts, middle = [], []
    for i in range(2):
        there = slice(0, i + 1)
        ghosts.append(ghost_coefficients(
            cond, cond_before[there], cond_after[there], cond_spans[there], windows[i]))
        middle.append(two_steps(
            low[i], high[i], spans[i], before[i], after[i], spans[i],
            started[i], windows[i], windows[i], coefficients, ghosts[i]))
    coarse_coef = coarse_coefficients(coarse_cond, cond_before, cond_after, cond_spans)
    sides = [from_sides(b, a) for a, b in middle]
    spans = [[(*w, w[0])] for w in windows]
    ended = []
    for i in range(2):
        a, b = middle[i]
        part = half_step([a], [b], spans[i], windows[i], coefficients, coarse_coef[:i])
        ended.append(two_steps(
            [a], [b], spans[i], [sides[i][0]], [sides[i][1]], spans[i],
            part, windows[i], results[i], coefficients, ghosts[i], True))
    (moved, moved_coarse), (own_fine, fine_coarse) = ended

    jump = jumps_of(moved_coarse, fine_coarse, next_coarse, own_coarse)
    lower = ring(jump[:, jump.shape[1] // 2:], "tm", -home)
    shifted = [jump] + [ring(jump, "tm", -j) for j in range(1, home)] + [jnp.concatenate([lower, lower], axis=1)]
    state = joined(shifted[0], shifted[1])
    for j in range(home):
        off, on = swapped(state, "space", 1), swapped(state, "space", 0)
        if j == 0:
            *_, moved = lax.optimization_barrier((on, off, lower, *shifted[2:home], moved))
            moved = ring(moved, "tm", 1)
        more = (shifted[j + 1:j + 3], home - j - 1) if j < home - 1 else ()
        state = sweep_step(state, on, off, coarse_coef, j == 0, *more)
    update, tail = finish(moved, own_fine, own_prior, state)
    return update[None], tail[None]


def solution(mesh):
    return jax.shard_map(
        shards,
        mesh=mesh,
        in_specs=(P("space", None, None), P("tm", "space", None, None), P("space", None, None)),
        out_specs=(P("tm", "space", None, None), P("tm", "space", None, None)),
        check_vma=False,
    )
```

```python
from typing import Any, NamedTuple

import jax
import jax.numpy as jnp
from jax import lax
from jax.experimental import pallas as pl
from jax.experimental.pallas import tpu as pltpu
from jax.sharding import PartitionSpec as P

FINE_RATE = 0.16
HALF_FINE = 0.5 * FINE_RATE
HALF_COARSE = 0.25 * FINE_RATE
TILE = 8
OVERLAP = 8
CUT = (5, 8)
LANES = 128

VMEM = pl.BlockSpec(memory_space=pltpu.VMEM)
HBM = pl.BlockSpec(memory_space=pltpu.HBM)
F32 = jnp.float32


class Here(NamedTuple):
    t: Any
    first: Any
    last: Any
    has_lo: Any
    has_hi: Any
    even: Any


def here():
    t, s = lax.axis_index("tm"), lax.axis_index("space")
    times, blocks = lax.axis_size("tm"), lax.axis_size("space")
    return Here(t, t == 0, t == times - 1, s > 0, s < blocks - 1, lax.rem(s, 2) == 0)


def call(body, out_shapes, operands, specs=None, scratch=(), out_specs=None):
    operands = list(operands)
    specs = specs or [VMEM] * len(operands)
    operands = [
        pltpu.with_memory_space_constraint(x, pltpu.HBM) if spec is HBM else x for x, spec in zip(operands, specs)
    ]
    return pl.pallas_call(
        body,
        out_shape=[jax.ShapeDtypeStruct(s, F32) for s in out_shapes],
        in_specs=specs,
        out_specs=out_specs or [VMEM] * len(out_shapes),
        scratch_shapes=list(scratch),
        compiler_params=pltpu.CompilerParams(vmem_limit_bytes=8 * 1024 * 1024),
    )(*operands)


def lane_scratch(rows, columns):
    return pltpu.VMEM((columns // LANES, rows, LANES), F32)


def split3(x):
    hi = x.astype(jnp.bfloat16)
    rest = x - hi.astype(F32)
    mid = rest.astype(jnp.bfloat16)
    low = (rest - mid.astype(F32)).astype(jnp.bfloat16)
    return hi, mid, low


def dot3(x, m):
    parts = [jnp.dot(p, m, preferred_element_type=F32) for p in split3(x)]
    return parts[0] + (parts[1] + parts[2])


def pair_matrix(fine, coarse, value):
    rows = lax.broadcasted_iota(jnp.int32, (fine, coarse), 0)
    cols = lax.broadcasted_iota(jnp.int32, (fine, coarse), 1)
    return jnp.where((rows >> 1) == cols, value, 0.0).astype(jnp.bfloat16)


def repeat_matrix(coarse, fine):
    rows = lax.broadcasted_iota(jnp.int32, (coarse, fine), 0)
    cols = lax.broadcasted_iota(jnp.int32, (coarse, fine), 1)
    return jnp.where(rows == (cols >> 1), 1.0, 0.0).astype(jnp.bfloat16)


def restrict_planes(first, second, scratch, matrix):
    blocks, ny, _ = scratch.shape
    sums = dot3(first + second, matrix)
    parts = []
    for b in range(blocks):
        scratch[b] = sums[:, b * LANES:(b + 1) * LANES]
        parts.append(scratch[b, pl.ds(0, ny // 2, 2), :] + scratch[b, pl.ds(1, ny // 2, 2), :])
    return jnp.concatenate(parts, axis=1)


class Field:
    def __init__(self, pieces, edges):
        self.pieces, self.edges, self.moved = pieces, edges, {}

    def tile(self, a):
        for first, end, ref, index, base in self.pieces:
            if first <= a and a + TILE <= end:
                return ref[index + (slice(a - base, a - base + TILE),)]
        return None

    def rolled(self, a, shift):
        if (a, shift) not in self.moved:
            tile = self.tile(a)
            self.moved[a, shift] = None if tile is None else pltpu.roll(tile, shift, 0)
        return self.moved[a, shift]

    def neighbour(self, a, other, shift, edge):
        own, next_ = self.rolled(a, shift), self.rolled(other, shift)
        return own if next_ is None else jnp.where(edge, next_, own)

    def above(self, a):
        return self.neighbour(a, a - TILE, 1, self.edges[0])

    def below(self, a):
        return self.neighbour(a, a + TILE, TILE - 1, self.edges[1])


def edges(nz):
    row = lax.broadcasted_iota(jnp.int32, (TILE, nz), 0)
    return row == 0, row == TILE - 1


def fields(spans, refs, planes, nz):
    e = edges(nz)
    return [
        Field([(a, b, ref, (p,), base) for (a, b, base), ref in zip(spans, refs)], e)
        for p in range(planes)
    ]


def face_coefficients(k, above, below, half, a, size, ny, nz):
    row = lax.broadcasted_iota(jnp.int32, (size, nz), 0) + a
    col = lax.broadcasted_iota(jnp.int32, (size, nz), 1)
    up_face = half * (k + jnp.where(row == 0, 0.0, above))
    down_face = half * (k + jnp.where(row == ny - 1, 0.0, below))
    right = pltpu.roll(k, nz - 1, 1)
    left = pltpu.roll(k, 1, 1)
    right_face = half * (k + jnp.where(col == nz - 1, 0.0, right))
    left_face = half * (k + jnp.where(col == 0, 0.0, left))
    total = (up_face + down_face) + (right_face + left_face)
    return (
        jnp.where(row == 0, 0.0, up_face),
        jnp.where(row == ny - 1, 0.0, down_face),
        jnp.where(col == nz - 1, 0.0, right_face),
        total,
    )


def prepare_fine(cond):
    nx, ny, nz = cond.shape

    def body(k_ref, kx, up, down, right, diag):
        planes = fields([(0, ny, 0)], [k_ref], nx, nz)
        for p in range(nx):
            for a in range(0, ny, TILE):
                s = slice(a, a + TILE)
                k = k_ref[p, s]
                u, d, r, total = face_coefficients(
                    k, planes[p].above(a), planes[p].below(a), HALF_FINE, a, TILE, ny, nz)
                up[p, s], down[p, s], right[p, s] = u, d, r
                if p > 0:
                    total = total + kx[p - 1, s]
                if p < nx - 1:
                    face = HALF_FINE * (k + k_ref[p + 1, s])
                    kx[p, s] = face
                    total = total + face
                diag[p, s] = 1.0 - total
    full = (nx, ny, nz)
    return call(body, [(nx - 1, ny, nz), full, full, full, full], [cond])


def restricted(field):
    nx, ny, nz = field.shape

    def body(f_ref, out, scratch):
        matrix = pair_matrix(nz, nz // 2, 0.125)
        for q in range(nx // 2):
            out[q] = restrict_planes(f_ref[2 * q], f_ref[2 * q + 1], scratch, matrix)

    return call(
        body, [(nx // 2, ny // 2, nz // 2)], [field], scratch=[lane_scratch(ny, nz // 2)]
    )[0]


def row_copies(source, out, rows, at, sems, first_sem, planes):
    start, end = rows
    return [
        pltpu.make_async_copy(
            source.at[p, pl.ds(start, end - start)], out.at[i, pl.ds(at, end - start)], sems.at[first_sem + i])
        for i, p in enumerate(planes)
    ]


def run(copies):
    for c in copies:
        c.start()
    for c in copies:
        c.wait()


def chosen(flag, body, this, other):
    pl.when(flag)(lambda: body(this))
    pl.when(jnp.logical_not(flag))(lambda: body(other))


def first_block(initial, prior, cond, end):
    nx, ny, nz = cond.shape

    def body(i_ref, p_ref, k_hbm, k_ref, v_ref, down, up, sems):
        def copy(ref):
            run(row_copies(k_hbm, k_ref, (0, ny), 0, sems, 0, range(nx))
                + row_copies(ref, v_ref, (0, end), 0, sems, nx, range(nx)))

        chosen(here().last, copy, i_ref, p_ref)
        k = fields([(0, ny, 0)], [k_ref], nx, nz)
        v = fields([(0, end, 0)], [v_ref], nx, nz)
        for out, own, inner in ((down, 0, 1), (up, nx - 1, nx - 2)):
            for a in range(0, ny, TILE):
                own_k = k[own].tile(a)
                out[a:a + TILE] = own_k
                if a >= end:
                    continue
                u, d, r, total = face_coefficients(
                    own_k, k[own].above(a), k[own].below(a), HALF_FINE, a, TILE, ny, nz)
                face = HALF_FINE * (own_k + k[inner].tile(a))
                c, stepped = row_step(v[own], u, d, r, 1.0 - (total + face), a)
                out[ny + a:ny + a + TILE] = c
                out[ny + end + a:ny + end + a + TILE] = stepped + face * v[inner].tile(a)

    return call(
        body, [cond.shape, (nx, end, nz)] + [(ny + 2 * end, nz)] * 2, [initial, prior, cond], [HBM, HBM, HBM],
        [pltpu.SemaphoreType.DMA((2 * nx,))])


def rows_from(field, start):
    nx, ny, nz = field.shape

    def body(ref, out, sems):
        run(row_copies(ref, out, (start, ny), 0, sems, 0, range(nx)))

    return call(body, [(nx, ny - start, nz)], [field], [HBM], [pltpu.SemaphoreType.DMA((nx,))])[0]


def coarse_and_initial(cond, initial, start):
    nx, ny, nz = cond.shape

    def body(k_ref, i_ref, coarse, rows, scratch, sems):
        copies = row_copies(i_ref, rows, (start, ny), 0, sems, 0, range(nx))
        for c in copies:
            c.start()
        matrix = pair_matrix(nz, nz // 2, 0.125)
        for q in range(nx // 2):
            coarse[q] = restrict_planes(k_ref[2 * q], k_ref[2 * q + 1], scratch, matrix)
        for c in copies:
            c.wait()

    return call(
        body, [(nx // 2, ny // 2, nz // 2), (nx, ny - start, nz)], [cond, initial], [VMEM, HBM],
        [lane_scratch(ny, nz // 2), pltpu.SemaphoreType.DMA((nx,))])


def row_step(v, up, down, right, diag, a):
    c = v.tile(a)
    nz = c.shape[1]
    total = diag * c
    total = total + up * v.above(a)
    total = total + down * v.below(a)
    total = total + right * pltpu.roll(c, nz - 1, 1)
    return c, total + pltpu.roll(right * c, 1, 1)


def block_step(planes, p, coefficients, a):
    kx, up, down, right, diag = coefficients
    s = slice(a, a + TILE)
    c, total = row_step(planes[p], up[p, s], down[p, s], right[p, s], diag[p, s], a)
    if p > 0:
        total = total + kx[p - 1, s] * planes[p - 1].tile(a)
    if p < len(planes) - 1:
        total = total + kx[p, s] * planes[p + 1].tile(a)
    return c, total


def half_step(state, window, coefficients, ahead=()):
    nx, rows, nz = state.shape
    w0, w1 = window

    def body(v_ref, *refs):
        v, out = fields([(w0, w1, w0)], [v_ref], nx, nz), refs[-1]
        for p in range(nx):
            for a in range(w0, w1, TILE):
                out[p, a - w0:a - w0 + TILE] = block_step(v, p, refs[:5], a)[1]

    return call(body, [state.shape], [state, *coefficients, *ahead])[0]


def lower_start(initial, received, window, coefficients, coarse, after):
    nx, rows, nz = received.shape
    w0, w1 = window
    extra = coarse.shape[1] // 2

    def body(i_ref, r_ref, *refs):
        coarse_ref, _, state, part, down, up = refs[5:]
        first = here().first
        for p in range(nx):
            for a in range(0, rows, TILE):
                s = slice(a, a + TILE)
                state[p, s] = jnp.where(first, i_ref[p, s], r_ref[p, s])
        edge_messages(state, part, down, up, refs[:5], window)
        for out, q in ((down, 0), (up, coarse.shape[0] - 1)):
            for i in range(2):
                out[2 * rows:, i * nz // 2:(i + 1) * nz // 2] = coarse_ref[q, i * extra:(i + 1) * extra]

    return call(
        body, [received.shape] * 2 + [(2 * rows + extra, nz)] * 2,
        [initial, received, *coefficients, coarse, after])


def edge_messages(state, part, down, up, coefficients, window):
    nx, rows, nz = state.shape
    w0, w1 = window
    v = fields([(w0, w1, w0)], [state], nx, nz)
    for p in range(nx):
        out = down if p == 0 else up if p == nx - 1 else None
        if part is None and out is None:
            continue
        for a in range(w0, w1, TILE):
            d = slice(a - w0, a - w0 + TILE)
            c, total = block_step(v, p, coefficients, a)
            if part is not None:
                part[p, d] = total
            if out is not None:
                out[d] = c
                out[slice(rows + d.start, rows + d.stop)] = total


def two_steps(state, started, before, after, conds, cond, window, result, coefficients, final=False):
    nx, rows, nz = state.shape
    ny = cond.shape[1]
    (w0, w1), (r0, r1) = window, result
    sides = [before, after]

    def body(v_ref, part, k_ref, *refs):
        k_sides, messages, coef, rest = refs[:2], refs[2:6], refs[6:11], refs[11:]
        out, rest = rest[0], rest[1:]
        mid = rest[-2] if final else rest[-1]
        me = here()
        owns = ((0, 0, me.has_lo), (1, nx - 1, me.has_hi))

        def face(side, own, has, s):
            return HALF_FINE * (k_ref[own, s] + jnp.where(has, k_sides[side][s], 0.0))

        for side, own, has in owns:
            (_, v_at), (_, p_at) = sides[side]
            near, half_done = messages[2 * side:2 * side + 2]
            for a in range(w0, w1, TILE):
                s, d = slice(a, a + TILE), slice(a - w0, a - w0 + TILE)
                theirs = jnp.where(has, near[slice(v_at + d.start, v_at + d.stop)], 0.0)
                flow = face(side, own, has, s) * (theirs - v_ref[own, d])
                mid[2 + side, d] = part[own, d] + flow
                mid[side, d] = jnp.where(has, half_done[slice(p_at + d.start, p_at + d.stop)] - flow, 0.0)
        span = [(w0, w1, w0)]
        edge = fields(span, [mid], 4, nz)
        w = fields(span, [part], nx, nz)
        w[0], w[nx - 1] = edge[2], edge[3]
        for p in range(nx):
            for a in range(r0, r1, TILE):
                c, total = block_step(w, p, coef, a)
                for side, own, has in owns:
                    if p == own:
                        s = slice(a, a + TILE)
                        total = total + face(side, own, has, s) * (edge[side].tile(a) - c)
                out[p, a - r0:a - r0 + TILE] = total
        if final:
            matrix = pair_matrix(nz, nz // 2, 0.125)
            for q in range(nx // 2):
                rest[0][q] = restrict_planes(out[2 * q], out[2 * q + 1], rest[-1], matrix)
        else:
            edge_messages(out, None, rest[0], rest[1], coef, window)

    shape = (nx, r1 - r0, nz)
    scratch = [pltpu.VMEM((4, w1 - w0, nz), F32)]
    if final:
        shapes = [shape, (nx // 2, (r1 - r0) // 2, nz // 2)]
        scratch.append(lane_scratch(r1 - r0, nz // 2))
    else:
        shapes = [shape, (2 * rows, nz), (2 * rows, nz)]
    messages = [array for side in sides for array, _ in side]
    return call(body, shapes, [state, started, cond, *conds, *messages, *coefficients], scratch=scratch)


def coarse_coefficients(own, before, after, at):
    nx, ny, nz = own.shape

    def body(k_own, lo, hi, kx, up, down, right, diag):
        me = here()

        def side(ref, has):
            k = jnp.concatenate([ref[at:, :nz], ref[at:, nz:]], axis=0)
            return jnp.where(has, k, 0.0)

        planes = [side(lo, me.has_lo)] + [k_own[p] for p in range(nx)] + [side(hi, me.has_hi)]
        for i in range(nx + 1):
            kx[i] = HALF_COARSE * (planes[i] + planes[i + 1])
        for p in range(nx):
            k = k_own[p]
            u, d, r, total = face_coefficients(
                k, pltpu.roll(k, 1, 0), pltpu.roll(k, ny - 1, 0), HALF_COARSE, 0, ny, ny, nz)
            up[p], down[p], right[p] = u, d, r
            if p > 0:
                total = total + kx[p]
            if p < nx - 1:
                total = total + kx[p + 1]
            diag[p] = 1.0 - total

    full = (nx, ny, nz)
    return call(body, [(nx + 1, ny, nz)] + [full] * 4, [own, before, after])


def sweep_messages(state, part, on, off, coefficients):
    nx, ny, nz = state.shape
    kx, up, down, right, diag = coefficients
    even = here().even
    v = fields([(0, ny, 0)], [state], nx, nz)
    for a in range(0, ny, TILE):
        s = slice(a, a + TILE)
        both = []
        for p in range(nx):
            c, total = row_step(v[p], up[p, s], down[p, s], right[p, s], diag[p, s], a)
            if p > 0:
                total = total + kx[p, s] * v[p - 1].tile(a)
            if p < nx - 1:
                total = total + kx[p + 1, s] * v[p + 1].tile(a)
            part[p, s] = total
            both.append((c, total))
        for i in range(2):
            d = slice(i * ny + a, i * ny + a + TILE)
            on[d] = jnp.where(even, both[-1][i], both[0][i])
            off[d] = jnp.where(even, both[0][i], both[-1][i])


def sweep_start(upper, lower, cut, coefficients):
    nx, ny, nz = upper.shape

    def body(a_ref, b_ref, *refs):
        last = here().last
        state = refs[5]
        for p in range(nx):
            for a in range(0, ny, TILE):
                s = slice(a, a + TILE)
                state[p, s] = jnp.where(last, (a_ref if a < cut else b_ref)[p, s], 0.0)
        sweep_messages(*refs[5:], refs[:5])

    return call(body, [upper.shape] * 2 + [(2 * ny, nz)] * 2, [upper, lower, *coefficients])


def sweep_step(state, part, on, off, cut, coefficients, jumps=(), later=0):
    nx, ny, nz = state.shape

    def body(v_ref, part_ref, on_ref, off_ref, *refs):
        coef, rest = refs[:5], refs[5:]
        kx, up, down, right, diag = coef
        jump_refs, rest = rest[:len(jumps)], rest[len(jumps):]
        out, mid = rest[0], rest[-1]
        me = here()
        for a in range(0, ny, TILE):
            s = slice(a, a + TILE)
            for i, (own, has) in enumerate(((0, me.has_lo), (nx - 1, me.has_hi))):
                refs_of = (off_ref, on_ref) if i == 0 else (on_ref, off_ref)
                theirs, half_done = (
                    jnp.where(has, jnp.where(me.even, *(r[slice(j * ny + a, j * ny + a + TILE)] for r in refs_of)), 0.0)
                    for j in range(2)
                )
                flow = kx[i * nx, s] * (theirs - v_ref[own, s])
                mid[1 + own, s] = part_ref[own, s] + flow
                mid[i * (nx + 1), s] = jnp.where(has, half_done - flow, 0.0)
            for p in range(1, nx - 1):
                mid[1 + p, s] = part_ref[p, s]
        w = fields([(0, ny, 0)], [mid], nx + 2, nz)
        for p in range(nx):
            for a in range(0, ny, TILE):
                s = slice(a, a + TILE)
                c, e = row_step(w[p + 1], up[p, s], down[p, s], right[p, s], diag[p, s], a)
                for i, q in ((p, p), (p + 1, p + 2)):
                    other = w[q].tile(a)
                    e = e + kx[i, s] * (other - c if i in (0, nx) else other)
                if jumps:
                    jump = jump_refs[0 if a < cut else 1][p, s]
                    e = e + jnp.where(me.t >= later, jump, 0.0)
                out[p, s] = e
        if jumps:
            sweep_messages(out, *rest[1:4], coef)

    shapes = [state.shape]
    if jumps:
        shapes += [state.shape] + [on.shape] * 2
    return call(
        body, shapes, [state, part, on, off, *coefficients, *jumps], scratch=[pltpu.VMEM((nx + 2, ny, nz), F32)])


def jumps_of(moved, own, next_prior, own_prior):
    nx, rows, nz = moved.shape

    def body(a_ref, b_ref, next_ref, own_ref, out):
        for p in range(nx):
            out[p, :rows] = a_ref[p] - next_ref[p, :rows]
            out[p, rows:] = b_ref[p] - own_ref[p, rows:]

    return call(body, [own_prior.shape], [moved, own, next_prior, own_prior])[0]


def finish(moved, own, prior, correction):
    nx, ny, nz = prior.shape
    rows = moved.shape[1]

    def body(moved_ref, own_ref, p_ref, e_ref, update, tail, out, wide, upper, lower, sems):
        parts = ((moved_ref, slice(0, rows), upper), (own_ref, slice(rows, ny), lower))
        spread = repeat_matrix(nz // 2, nz)
        copies = []
        for q in range(nx // 2):
            row = dot3(e_ref[q], spread)
            for b in range(nz // LANES):
                s = slice(b * LANES, (b + 1) * LANES)
                wide[b, pl.ds(0, ny // 2, 2), :] = row[:, s]
                wide[b, pl.ds(1, ny // 2, 2), :] = row[:, s]
            for p in (2 * q, 2 * q + 1):
                for ref, r, _ in parts:
                    for b in range(nz // LANES):
                        s = slice(b * LANES, (b + 1) * LANES)
                        out[p, r, s] = (ref[p, :, s] + wide[b, r]) - p_ref[p, r, s]
                copies.append(pltpu.make_async_copy(out.at[p], update.at[p], sems.at[p]))
                copies[-1].start()
        matrix = pair_matrix(nz, nz // 2, 0.125)
        for q in range(nx // 2):
            for ref, r, scratch in parts:
                c = slice(r.start // 2, r.stop // 2)
                tail[q, c] = e_ref[q, c] + restrict_planes(ref[2 * q], ref[2 * q + 1], scratch, matrix)
        for c in copies:
            c.wait()

    return call(
        body, [prior.shape, correction.shape], [moved, own, prior, correction],
        scratch=[pltpu.VMEM(prior.shape, F32), lane_scratch(ny, nz), lane_scratch(rows, nz // 2),
                 lane_scratch(ny - rows, nz // 2), pltpu.SemaphoreType.DMA((nx,))],
        out_specs=[HBM, VMEM])


def ring(block, axis, distance):
    size = lax.axis_size(axis)
    return lax.ppermute(block, axis, [(i, (i + distance) % size) for i in range(size)])


def from_sides(last, first):
    return ring(last, "space", 1), ring(first, "space", -1)


def swapped(block, axis, offset):
    size = lax.axis_size(axis)
    pairs = [(i % size, (i + 1) % size) for i in range(offset, size + offset, 2)]
    return lax.ppermute(block, axis, pairs + [(j, i) for i, j in pairs])


def shards(initial, prior, conductivity):
    times = lax.axis_size("tm")
    own_prior = prior[0]
    home = times - 1
    ny = initial.shape[1]
    cut = ny * CUT[0] // CUT[1]
    wide = cut + OVERLAP
    windows = [(0, wide), (cut - OVERLAP, ny)]
    results = [(0, cut), (cut, ny)]
    start = windows[1][0]

    received = ring(rows_from(own_prior, start), "tm", 1)
    cond, upper, down, up = first_block(initial, own_prior, conductivity, wide)
    before, after = from_sides(up, down)
    coefficients = prepare_fine(cond)
    coarse_cond, initial_rows = coarse_and_initial(cond, initial, start)
    lower, lower_part, down, up = lower_start(initial_rows, received, windows[1], coefficients, coarse_cond, before)
    before_2, after_2 = from_sides(up, down)
    own_coarse = restricted(own_prior)
    next_coarse = ring(own_coarse, "tm", -1)

    conds = (before, after)
    rows = ny - start
    sides = [
        [[(x, at), (x, at + size)] for x in pair]
        for pair, at, size in ((conds, ny, wide), ((before_2, after_2), 0, rows))
    ]
    parts = [half_step(upper, windows[0], coefficients), lower_part]
    middle = [
        two_steps(state, parts[i], *sides[i], conds, cond, windows[i], windows[i], coefficients)
        for i, state in enumerate((upper, lower))
    ]
    coarse_coef = coarse_coefficients(coarse_cond, before_2, after_2, 2 * rows)
    received = [from_sides(up, down) for _, down, up in middle]
    ended = []
    for i, (state, _, _) in enumerate(middle):
        part = half_step(state, windows[i], coefficients, coarse_coef[:i])
        side = [[(x, 0), (x, x.shape[0] // 2)] for x in received[i]]
        ended.append(two_steps(state, part, *side, conds, cond, windows[i], results[i], coefficients, True))
    (moved, moved_coarse), (own_fine, fine_coarse) = ended

    jump = jumps_of(moved_coarse, fine_coarse, next_coarse, own_coarse)
    half_cut = cut // 2
    lower = ring(jump[:, half_cut:], "tm", -home)
    shifted = [jump] + [ring(jump, "tm", -j) for j in range(1, home)]
    shifted.append(jnp.concatenate([jump[:, :half_cut], lower], axis=1))
    sweep = sweep_start(shifted[0], shifted[1], half_cut, coarse_coef)
    for j in range(home):
        state, part, on, off = sweep
        off, on = swapped(off, "space", 1), swapped(on, "space", 0)
        if j == 0:
            *_, moved = lax.optimization_barrier((on, off, lower, *shifted[2:home], moved))
            moved = ring(moved, "tm", 1)
        more = (shifted[j + 1:j + 3], home - j - 1) if j < home - 1 else ()
        sweep = sweep_step(state, part, on, off, half_cut, coarse_coef, *more)
    update, tail = finish(moved, own_fine, own_prior, sweep[0])
    return update[None], tail[None]


def solution(mesh):
    return jax.shard_map(
        shards,
        mesh=mesh,
        in_specs=(P("space", None, None), P("tm", "space", None, None), P("space", None, None)),
        out_specs=(P("tm", "space", None, None), P("tm", "space", None, None)),
        check_vma=False,
    )
```

```python
from typing import Any, NamedTuple

import jax
import jax.numpy as jnp
from jax import lax
from jax.experimental import pallas as pl
from jax.experimental.pallas import tpu as pltpu
from jax.sharding import PartitionSpec as P

FINE_RATE = 0.16
HALF_FINE = 0.5 * FINE_RATE
HALF_COARSE = 0.25 * FINE_RATE
TILE = 8
OVERLAP = 8
CUT = (5, 8)
LANES = 128

VMEM = pl.BlockSpec(memory_space=pltpu.VMEM)
HBM = pl.BlockSpec(memory_space=pltpu.HBM)
F32 = jnp.float32


class Here(NamedTuple):
    t: Any
    first: Any
    last: Any
    has_lo: Any
    has_hi: Any
    even: Any


def here():
    t, s = lax.axis_index("tm"), lax.axis_index("space")
    times, blocks = lax.axis_size("tm"), lax.axis_size("space")
    return Here(t, t == 0, t == times - 1, s > 0, s < blocks - 1, lax.rem(s, 2) == 0)


def call(body, out_shapes, operands, specs=None, scratch=(), out_specs=None, aliases=None):
    operands = list(operands)
    specs = specs or [VMEM] * len(operands)
    operands = [
        pltpu.with_memory_space_constraint(x, pltpu.HBM) if spec is HBM else x for x, spec in zip(operands, specs)
    ]
    return pl.pallas_call(
        body,
        out_shape=[jax.ShapeDtypeStruct(s, F32) for s in out_shapes],
        in_specs=specs,
        out_specs=out_specs or [VMEM] * len(out_shapes),
        scratch_shapes=list(scratch),
        input_output_aliases=aliases or {},
        compiler_params=pltpu.CompilerParams(vmem_limit_bytes=8 * 1024 * 1024),
    )(*operands)


def lane_scratch(rows, columns):
    return pltpu.VMEM((columns // LANES, rows, LANES), F32)


def split3(x):
    hi = x.astype(jnp.bfloat16)
    rest = x - hi.astype(F32)
    mid = rest.astype(jnp.bfloat16)
    low = (rest - mid.astype(F32)).astype(jnp.bfloat16)
    return hi, mid, low


def dot3(x, m):
    parts = [jnp.dot(p, m, preferred_element_type=F32) for p in split3(x)]
    return parts[0] + (parts[1] + parts[2])


def pair_matrix(fine, coarse, value):
    rows = lax.broadcasted_iota(jnp.int32, (fine, coarse), 0)
    cols = lax.broadcasted_iota(jnp.int32, (fine, coarse), 1)
    return jnp.where((rows >> 1) == cols, value, 0.0).astype(jnp.bfloat16)


def repeat_matrix(coarse, fine):
    rows = lax.broadcasted_iota(jnp.int32, (coarse, fine), 0)
    cols = lax.broadcasted_iota(jnp.int32, (coarse, fine), 1)
    return jnp.where(rows == (cols >> 1), 1.0, 0.0).astype(jnp.bfloat16)


def restrict_planes(first, second, scratch, matrix):
    blocks, ny, _ = scratch.shape
    sums = dot3(first + second, matrix)
    parts = []
    for b in range(blocks):
        scratch[b] = sums[:, b * LANES:(b + 1) * LANES]
        parts.append(scratch[b, pl.ds(0, ny // 2, 2), :] + scratch[b, pl.ds(1, ny // 2, 2), :])
    return jnp.concatenate(parts, axis=1)


class Field:
    def __init__(self, pieces, edges):
        self.pieces, self.edges, self.moved = pieces, edges, {}

    def tile(self, a):
        for first, end, ref, index, base in self.pieces:
            if first <= a and a + TILE <= end:
                return ref[index + (slice(a - base, a - base + TILE),)]
        return None

    def rolled(self, a, shift):
        if (a, shift) not in self.moved:
            tile = self.tile(a)
            self.moved[a, shift] = None if tile is None else pltpu.roll(tile, shift, 0)
        return self.moved[a, shift]

    def neighbour(self, a, other, shift, edge):
        own, next_ = self.rolled(a, shift), self.rolled(other, shift)
        return own if next_ is None else jnp.where(edge, next_, own)

    def above(self, a):
        return self.neighbour(a, a - TILE, 1, self.edges[0])

    def below(self, a):
        return self.neighbour(a, a + TILE, TILE - 1, self.edges[1])


def edges(nz):
    row = lax.broadcasted_iota(jnp.int32, (TILE, nz), 0)
    return row == 0, row == TILE - 1


def fields(spans, refs, planes, nz):
    e = edges(nz)
    return [
        Field([(a, b, ref, (p,), base) for (a, b, base), ref in zip(spans, refs)], e)
        for p in range(planes)
    ]


def face_coefficients(k, above, below, half, a, size, ny, nz):
    row = lax.broadcasted_iota(jnp.int32, (size, nz), 0) + a
    col = lax.broadcasted_iota(jnp.int32, (size, nz), 1)
    up_face = half * (k + jnp.where(row == 0, 0.0, above))
    down_face = half * (k + jnp.where(row == ny - 1, 0.0, below))
    right = pltpu.roll(k, nz - 1, 1)
    left = pltpu.roll(k, 1, 1)
    right_face = half * (k + jnp.where(col == nz - 1, 0.0, right))
    left_face = half * (k + jnp.where(col == 0, 0.0, left))
    total = (up_face + down_face) + (right_face + left_face)
    return (
        jnp.where(row == 0, 0.0, up_face),
        jnp.where(row == ny - 1, 0.0, down_face),
        jnp.where(col == nz - 1, 0.0, right_face),
        total,
    )


def prepare_fine(cond):
    nx, ny, nz = cond.shape

    def body(k_ref, kx, up, down, right, diag):
        planes = fields([(0, ny, 0)], [k_ref], nx, nz)
        for p in range(nx):
            for a in range(0, ny, TILE):
                s = slice(a, a + TILE)
                k = k_ref[p, s]
                u, d, r, total = face_coefficients(
                    k, planes[p].above(a), planes[p].below(a), HALF_FINE, a, TILE, ny, nz)
                up[p, s], down[p, s], right[p, s] = u, d, r
                if p > 0:
                    total = total + kx[p - 1, s]
                if p < nx - 1:
                    face = HALF_FINE * (k + k_ref[p + 1, s])
                    kx[p, s] = face
                    total = total + face
                diag[p, s] = 1.0 - total
    full = (nx, ny, nz)
    return call(body, [(nx - 1, ny, nz), full, full, full, full], [cond])


def restricted(field):
    nx, ny, nz = field.shape

    def body(f_ref, out, scratch):
        matrix = pair_matrix(nz, nz // 2, 0.125)
        for q in range(nx // 2):
            out[q] = restrict_planes(f_ref[2 * q], f_ref[2 * q + 1], scratch, matrix)

    return call(
        body, [(nx // 2, ny // 2, nz // 2)], [field], scratch=[lane_scratch(ny, nz // 2)]
    )[0]


def row_copies(source, out, rows, at, sems, first_sem, planes):
    start, end = rows
    return [
        pltpu.make_async_copy(
            source.at[p, pl.ds(start, end - start)], out.at[i, pl.ds(at, end - start)], sems.at[first_sem + i])
        for i, p in enumerate(planes)
    ]


def run(copies):
    for c in copies:
        c.start()
    for c in copies:
        c.wait()


def chosen(flag, body, this, other):
    pl.when(flag)(lambda: body(this))
    pl.when(jnp.logical_not(flag))(lambda: body(other))


def first_block(initial, prior, cond, end):
    nx, ny, nz = cond.shape

    def body(i_ref, p_ref, k_hbm, k_ref, v_ref, down, up, sems):
        def copy(ref):
            run(row_copies(k_hbm, k_ref, (0, ny), 0, sems, 0, range(nx))
                + row_copies(ref, v_ref, (0, end), 0, sems, nx, range(nx)))

        chosen(here().last, copy, i_ref, p_ref)
        k = fields([(0, ny, 0)], [k_ref], nx, nz)
        v = fields([(0, end, 0)], [v_ref], nx, nz)
        for out, own, inner in ((down, 0, 1), (up, nx - 1, nx - 2)):
            for a in range(0, ny, TILE):
                own_k = k[own].tile(a)
                out[a:a + TILE] = own_k
                if a >= end:
                    continue
                u, d, r, total = face_coefficients(
                    own_k, k[own].above(a), k[own].below(a), HALF_FINE, a, TILE, ny, nz)
                face = HALF_FINE * (own_k + k[inner].tile(a))
                c, stepped = row_step(v[own], u, d, r, 1.0 - (total + face), a)
                out[ny + a:ny + a + TILE] = c
                out[ny + end + a:ny + end + a + TILE] = stepped + face * v[inner].tile(a)

    return call(
        body, [cond.shape, (nx, end, nz)] + [(ny + 2 * end, nz)] * 2, [initial, prior, cond], [HBM, HBM, HBM],
        [pltpu.SemaphoreType.DMA((2 * nx,))])


def rows_from(field, start):
    nx, ny, nz = field.shape

    def body(ref, out, sems):
        run(row_copies(ref, out, (start, ny), 0, sems, 0, range(nx)))

    return call(body, [(nx, ny - start, nz)], [field], [HBM], [pltpu.SemaphoreType.DMA((nx,))])[0]


def coarse_and_initial(cond, initial, start):
    nx, ny, nz = cond.shape

    def body(k_ref, i_ref, coarse, rows, scratch, sems):
        copies = row_copies(i_ref, rows, (start, ny), 0, sems, 0, range(nx))
        for c in copies:
            c.start()
        matrix = pair_matrix(nz, nz // 2, 0.125)
        for q in range(nx // 2):
            coarse[q] = restrict_planes(k_ref[2 * q], k_ref[2 * q + 1], scratch, matrix)
        for c in copies:
            c.wait()

    return call(
        body, [(nx // 2, ny // 2, nz // 2), (nx, ny - start, nz)], [cond, initial], [VMEM, HBM],
        [lane_scratch(ny, nz // 2), pltpu.SemaphoreType.DMA((nx,))])


def row_step(v, up, down, right, diag, a):
    c = v.tile(a)
    nz = c.shape[1]
    total = diag * c
    total = total + up * v.above(a)
    total = total + down * v.below(a)
    total = total + right * pltpu.roll(c, nz - 1, 1)
    return c, total + pltpu.roll(right * c, 1, 1)


def block_step(planes, p, coefficients, a):
    kx, up, down, right, diag = coefficients
    s = slice(a, a + TILE)
    c, total = row_step(planes[p], up[p, s], down[p, s], right[p, s], diag[p, s], a)
    if p > 0:
        total = total + kx[p - 1, s] * planes[p - 1].tile(a)
    if p < len(planes) - 1:
        total = total + kx[p, s] * planes[p + 1].tile(a)
    return c, total


def half_step(state, window, coefficients, ahead=()):
    nx, rows, nz = state.shape
    w0, w1 = window

    def body(v_ref, *refs):
        v, out = fields([(w0, w1, w0)], [v_ref], nx, nz), refs[-1]
        for p in range(nx):
            for a in range(w0, w1, TILE):
                out[p, a - w0:a - w0 + TILE] = block_step(v, p, refs[:5], a)[1]

    return call(body, [state.shape], [state, *coefficients, *ahead])[0]


def lower_start(initial, received, window, coefficients, coarse, after):
    nx, rows, nz = received.shape
    w0, w1 = window
    extra = coarse.shape[1] // 2

    def body(i_ref, r_ref, *refs):
        coarse_ref, _, state, part, down, up = refs[5:]
        first = here().first
        for p in range(nx):
            for a in range(0, rows, TILE):
                s = slice(a, a + TILE)
                state[p, s] = jnp.where(first, i_ref[p, s], r_ref[p, s])
        edge_messages(state, part, down, up, refs[:5], window)
        for out, q in ((down, 0), (up, coarse.shape[0] - 1)):
            for i in range(2):
                out[2 * rows:, i * nz // 2:(i + 1) * nz // 2] = coarse_ref[q, i * extra:(i + 1) * extra]

    return call(
        body, [received.shape] * 2 + [(2 * rows + extra, nz)] * 2,
        [initial, received, *coefficients, coarse, after])


def edge_messages(state, part, down, up, coefficients, window):
    nx, rows, nz = state.shape
    w0, w1 = window
    v = fields([(w0, w1, w0)], [state], nx, nz)
    for p in range(nx):
        out = down if p == 0 else up if p == nx - 1 else None
        if part is None and out is None:
            continue
        for a in range(w0, w1, TILE):
            d = slice(a - w0, a - w0 + TILE)
            c, total = block_step(v, p, coefficients, a)
            if part is not None:
                part[p, d] = total
            if out is not None:
                out[d] = c
                out[slice(rows + d.start, rows + d.stop)] = total


def two_steps(state, started, before, after, conds, cond, window, result, coefficients, final=False):
    nx, rows, nz = state.shape
    ny = cond.shape[1]
    (w0, w1), (r0, r1) = window, result
    sides = [before, after]

    def body(v_ref, part, k_ref, *refs):
        k_sides, messages, coef, rest = refs[:2], refs[2:6], refs[6:11], refs[11:]
        out, rest = rest[0], rest[1:]
        mid = rest[-2] if final else rest[-1]
        me = here()
        owns = ((0, 0, me.has_lo), (1, nx - 1, me.has_hi))

        def face(side, own, has, s):
            return HALF_FINE * (k_ref[own, s] + jnp.where(has, k_sides[side][s], 0.0))

        for side, own, has in owns:
            (_, v_at), (_, p_at) = sides[side]
            near, half_done = messages[2 * side:2 * side + 2]
            for a in range(w0, w1, TILE):
                s, d = slice(a, a + TILE), slice(a - w0, a - w0 + TILE)
                theirs = jnp.where(has, near[slice(v_at + d.start, v_at + d.stop)], 0.0)
                flow = face(side, own, has, s) * (theirs - v_ref[own, d])
                mid[2 + side, d] = part[own, d] + flow
                mid[side, d] = jnp.where(has, half_done[slice(p_at + d.start, p_at + d.stop)] - flow, 0.0)
        span = [(w0, w1, w0)]
        edge = fields(span, [mid], 4, nz)
        w = fields(span, [part], nx, nz)
        w[0], w[nx - 1] = edge[2], edge[3]
        for p in range(nx):
            for a in range(r0, r1, TILE):
                c, total = block_step(w, p, coef, a)
                for side, own, has in owns:
                    if p == own:
                        s = slice(a, a + TILE)
                        total = total + face(side, own, has, s) * (edge[side].tile(a) - c)
                out[p, a - r0:a - r0 + TILE] = total
        if final:
            matrix = pair_matrix(nz, nz // 2, 0.125)
            for q in range(nx // 2):
                rest[0][q] = restrict_planes(out[2 * q], out[2 * q + 1], rest[-1], matrix)
        else:
            edge_messages(out, None, rest[0], rest[1], coef, window)

    shape = (nx, r1 - r0, nz)
    scratch = [pltpu.VMEM((4, w1 - w0, nz), F32)]
    if final:
        shapes = [shape, (nx // 2, (r1 - r0) // 2, nz // 2)]
        scratch.append(lane_scratch(r1 - r0, nz // 2))
    else:
        shapes = [shape, (2 * rows, nz), (2 * rows, nz)]
    messages = [array for side in sides for array, _ in side]
    return call(body, shapes, [state, started, cond, *conds, *messages, *coefficients], scratch=scratch)


def coarse_coefficients(own, before, after, at):
    nx, ny, nz = own.shape

    def body(k_own, lo, hi, kx, up, down, right, diag):
        me = here()

        def side(ref, has):
            k = jnp.concatenate([ref[at:, :nz], ref[at:, nz:]], axis=0)
            return jnp.where(has, k, 0.0)

        planes = [side(lo, me.has_lo)] + [k_own[p] for p in range(nx)] + [side(hi, me.has_hi)]
        for i in range(nx + 1):
            kx[i] = HALF_COARSE * (planes[i] + planes[i + 1])
        for p in range(nx):
            k = k_own[p]
            u, d, r, total = face_coefficients(
                k, pltpu.roll(k, 1, 0), pltpu.roll(k, ny - 1, 0), HALF_COARSE, 0, ny, ny, nz)
            up[p], down[p], right[p] = u, d, r
            if p > 0:
                total = total + kx[p]
            if p < nx - 1:
                total = total + kx[p + 1]
            diag[p] = 1.0 - total

    full = (nx, ny, nz)
    return call(body, [(nx + 1, ny, nz)] + [full] * 4, [own, before, after])


def sweep_messages(state, part, on, off, coefficients):
    nx, ny, nz = state.shape
    kx, up, down, right, diag = coefficients
    even = here().even
    v = fields([(0, ny, 0)], [state], nx, nz)
    for a in range(0, ny, TILE):
        s = slice(a, a + TILE)
        both = []
        for p in range(nx):
            c, total = row_step(v[p], up[p, s], down[p, s], right[p, s], diag[p, s], a)
            if p > 0:
                total = total + kx[p, s] * v[p - 1].tile(a)
            if p < nx - 1:
                total = total + kx[p + 1, s] * v[p + 1].tile(a)
            part[p, s] = total
            both.append((c, total))
        for i in range(2):
            d = slice(i * ny + a, i * ny + a + TILE)
            on[d] = jnp.where(even, both[-1][i], both[0][i])
            off[d] = jnp.where(even, both[0][i], both[-1][i])


def sweep_start(upper, lower, cut, coefficients):
    nx, ny, nz = upper.shape

    def body(a_ref, b_ref, *refs):
        last = here().last
        state = refs[5]
        for p in range(nx):
            for a in range(0, ny, TILE):
                s = slice(a, a + TILE)
                state[p, s] = jnp.where(last, (a_ref if a < cut else b_ref)[p, s], 0.0)
        sweep_messages(*refs[5:], refs[:5])

    return call(body, [upper.shape] * 2 + [(2 * ny, nz)] * 2, [upper, lower, *coefficients])


def sweep_step(state, part, on, off, cut, coefficients, jumps=(), later=0):
    nx, ny, nz = state.shape

    def body(v_ref, part_ref, on_ref, off_ref, *refs):
        coef, rest = refs[:5], refs[5:]
        kx, up, down, right, diag = coef
        jump_refs, rest = rest[:len(jumps)], rest[len(jumps):]
        out, mid = rest[0], rest[-1]
        me = here()
        for a in range(0, ny, TILE):
            s = slice(a, a + TILE)
            for i, (own, has) in enumerate(((0, me.has_lo), (nx - 1, me.has_hi))):
                refs_of = (off_ref, on_ref) if i == 0 else (on_ref, off_ref)
                theirs, half_done = (
                    jnp.where(has, jnp.where(me.even, *(r[slice(j * ny + a, j * ny + a + TILE)] for r in refs_of)), 0.0)
                    for j in range(2)
                )
                flow = kx[i * nx, s] * (theirs - v_ref[own, s])
                mid[1 + own, s] = part_ref[own, s] + flow
                mid[i * (nx + 1), s] = jnp.where(has, half_done - flow, 0.0)
            for p in range(1, nx - 1):
                mid[1 + p, s] = part_ref[p, s]
        w = fields([(0, ny, 0)], [mid], nx + 2, nz)
        for p in range(nx):
            for a in range(0, ny, TILE):
                s = slice(a, a + TILE)
                c, e = row_step(w[p + 1], up[p, s], down[p, s], right[p, s], diag[p, s], a)
                for i, q in ((p, p), (p + 1, p + 2)):
                    other = w[q].tile(a)
                    e = e + kx[i, s] * (other - c if i in (0, nx) else other)
                if jumps:
                    jump = jump_refs[0 if a < cut else 1][p, s]
                    e = e + jnp.where(me.t >= later, jump, 0.0)
                out[p, s] = e
        if jumps:
            sweep_messages(out, *rest[1:4], coef)

    shapes = [state.shape]
    if jumps:
        shapes += [state.shape] + [on.shape] * 2
    return call(
        body, shapes, [state, part, on, off, *coefficients, *jumps], scratch=[pltpu.VMEM((nx + 2, ny, nz), F32)])


def jumps_of(moved, own, next_prior, own_prior):
    nx, rows, nz = moved.shape

    def body(a_ref, b_ref, next_ref, own_ref, out):
        for p in range(nx):
            out[p, :rows] = a_ref[p] - next_ref[p, :rows]
            out[p, rows:] = b_ref[p] - own_ref[p, rows:]

    return call(body, [own_prior.shape], [moved, own, next_prior, own_prior])[0]


def prolonged(e_ref, rows, q, spread, wide):
    row = dot3(e_ref[q, rows], spread)
    count = row.shape[0]
    for b in range(wide.shape[0]):
        s = slice(b * LANES, (b + 1) * LANES)
        wide[b, pl.ds(0, count, 2), :] = row[:, s]
        wide[b, pl.ds(1, count, 2), :] = row[:, s]


def finish_lower(fine, coarse, prior, correction):
    nx, ny, nz = prior.shape
    rows = fine.shape[1]
    cut = ny - rows

    def body(f_ref, c_ref, p_ref, e_ref, update, tail, rest, out, tail_out, upper, lower, sems):
        spread = repeat_matrix(nz // 2, nz)
        copies = []
        for q in range(nx // 2):
            tail_out[q] = e_ref[q, cut // 2:] + c_ref[q]
            copies.append(pltpu.make_async_copy(
                tail_out.at[q], tail.at[q, pl.ds(cut // 2, rows // 2)], sems.at[nx + q]))
            copies[-1].start()
        for q in range(nx // 2):
            prolonged(e_ref, slice(cut // 2, ny // 2), q, spread, lower)
            for p in (2 * q, 2 * q + 1):
                for b in range(nz // LANES):
                    s = slice(b * LANES, (b + 1) * LANES)
                    out[p, :, s] = (f_ref[p, :, s] + lower[b]) - p_ref[p, cut:, s]
                copies.append(pltpu.make_async_copy(out.at[p], update.at[p, pl.ds(cut, rows)], sems.at[p]))
                copies[-1].start()
        for q in range(nx // 2):
            prolonged(e_ref, slice(0, cut // 2), q, spread, upper)
            for p in (2 * q, 2 * q + 1):
                for b in range(nz // LANES):
                    s = slice(b * LANES, (b + 1) * LANES)
                    rest[p, :, s] = upper[b] - p_ref[p, :cut, s]
        for c in copies:
            c.wait()

    return call(
        body, [prior.shape, correction.shape, (nx, cut, nz)], [fine, coarse, prior, correction],
        scratch=[pltpu.VMEM(fine.shape, F32), pltpu.VMEM(coarse.shape, F32), lane_scratch(cut, nz),
                 lane_scratch(rows, nz), pltpu.SemaphoreType.DMA((nx + nx // 2,))],
        out_specs=[HBM, HBM, VMEM])


def finish_upper(fine, correction, rest, update, tail):
    nx, rows, nz = fine.shape

    def body(f_ref, e_ref, rest_ref, *refs):
        update, tail, out, tail_out, scratch, sems = refs[2:]
        copies = []
        for p in range(nx):
            for a in range(0, rows, TILE):
                s = slice(a, a + TILE)
                out[p, s] = f_ref[p, s] + rest_ref[p, s]
            copies.append(pltpu.make_async_copy(out.at[p], update.at[p, pl.ds(0, rows)], sems.at[p]))
            copies[-1].start()
        matrix = pair_matrix(nz, nz // 2, 0.125)
        for q in range(nx // 2):
            tail_out[q] = e_ref[q, :rows // 2] + restrict_planes(f_ref[2 * q], f_ref[2 * q + 1], scratch, matrix)
            copies.append(pltpu.make_async_copy(tail_out.at[q], tail.at[q, pl.ds(0, rows // 2)], sems.at[nx + q]))
            copies[-1].start()
        for c in copies:
            c.wait()

    return call(
        body, [update.shape, tail.shape], [fine, correction, rest, update, tail],
        [VMEM] * 3 + [HBM] * 2,
        [pltpu.VMEM(fine.shape, F32), pltpu.VMEM((nx // 2, rows // 2, nz // 2), F32), lane_scratch(rows, nz // 2),
         pltpu.SemaphoreType.DMA((nx + nx // 2,))],
        [HBM, HBM], {3: 0, 4: 1})


def ring(block, axis, distance):
    size = lax.axis_size(axis)
    return lax.ppermute(block, axis, [(i, (i + distance) % size) for i in range(size)])


def from_sides(last, first):
    return ring(last, "space", 1), ring(first, "space", -1)


def swapped(block, axis, offset):
    size = lax.axis_size(axis)
    pairs = [(i % size, (i + 1) % size) for i in range(offset, size + offset, 2)]
    return lax.ppermute(block, axis, pairs + [(j, i) for i, j in pairs])


def shards(initial, prior, conductivity):
    times = lax.axis_size("tm")
    own_prior = prior[0]
    home = times - 1
    ny = initial.shape[1]
    cut = ny * CUT[0] // CUT[1]
    wide = cut + OVERLAP
    windows = [(0, wide), (cut - OVERLAP, ny)]
    results = [(0, cut), (cut, ny)]
    start = windows[1][0]

    received = ring(rows_from(own_prior, start), "tm", 1)
    cond, upper, down, up = first_block(initial, own_prior, conductivity, wide)
    before, after = from_sides(up, down)
    coefficients = prepare_fine(cond)
    coarse_cond, initial_rows = coarse_and_initial(cond, initial, start)
    lower, lower_part, down, up = lower_start(initial_rows, received, windows[1], coefficients, coarse_cond, before)
    before_2, after_2 = from_sides(up, down)
    own_coarse = restricted(own_prior)
    next_coarse = ring(own_coarse, "tm", -1)

    conds = (before, after)
    rows = ny - start
    sides = [
        [[(x, at), (x, at + size)] for x in pair]
        for pair, at, size in ((conds, ny, wide), ((before_2, after_2), 0, rows))
    ]
    parts = [half_step(upper, windows[0], coefficients), lower_part]
    middle = [
        two_steps(state, parts[i], *sides[i], conds, cond, windows[i], windows[i], coefficients)
        for i, state in enumerate((upper, lower))
    ]
    coarse_coef = coarse_coefficients(coarse_cond, before_2, after_2, 2 * rows)
    received = [from_sides(up, down) for _, down, up in middle]
    ended = []
    for i, (state, _, _) in enumerate(middle):
        part = half_step(state, windows[i], coefficients, coarse_coef[:i])
        side = [[(x, 0), (x, x.shape[0] // 2)] for x in received[i]]
        ended.append(two_steps(state, part, *side, conds, cond, windows[i], results[i], coefficients, True))
    (moved, moved_coarse), (own_fine, fine_coarse) = ended

    jump = jumps_of(moved_coarse, fine_coarse, next_coarse, own_coarse)
    half_cut = cut // 2
    lower = ring(jump[:, half_cut:], "tm", -home)
    shifted = [jump] + [ring(jump, "tm", -j) for j in range(1, home)]
    shifted.append(jnp.concatenate([jump[:, :half_cut], lower], axis=1))
    sweep = sweep_start(shifted[0], shifted[1], half_cut, coarse_coef)
    for j in range(home):
        state, part, on, off = sweep
        off, on = swapped(off, "space", 1), swapped(on, "space", 0)
        if j == 0:
            *_, moved = lax.optimization_barrier((on, off, lower, *shifted[2:home], moved))
            moved = ring(moved, "tm", 1)
        more = (shifted[j + 1:j + 3], home - j - 1) if j < home - 1 else ()
        sweep = sweep_step(state, part, on, off, half_cut, coarse_coef, *more)
    update, tail, rest = finish_lower(own_fine, fine_coarse, own_prior, sweep[0])
    update, tail = finish_upper(moved, sweep[0], rest, update, tail)
    return update[None], tail[None]


def solution(mesh):
    return jax.shard_map(
        shards,
        mesh=mesh,
        in_specs=(P("space", None, None), P("tm", "space", None, None), P("space", None, None)),
        out_specs=(P("tm", "space", None, None), P("tm", "space", None, None)),
        check_vma=False,
    )
```

```python
from typing import Any, NamedTuple

import jax
import jax.numpy as jnp
from jax import lax
from jax.experimental import pallas as pl
from jax.experimental.pallas import tpu as pltpu
from jax.sharding import PartitionSpec as P

FINE_RATE = 0.16
HALF_FINE = 0.5 * FINE_RATE
HALF_COARSE = 0.25 * FINE_RATE
TILE = 8
OVERLAP = 8
CUT = (5, 8)
LANES = 128

VMEM = pl.BlockSpec(memory_space=pltpu.VMEM)
HBM = pl.BlockSpec(memory_space=pltpu.HBM)
F32 = jnp.float32


class Here(NamedTuple):
    t: Any
    first: Any
    last: Any
    has_lo: Any
    has_hi: Any
    even: Any


def here():
    t, s = lax.axis_index("tm"), lax.axis_index("space")
    times, blocks = lax.axis_size("tm"), lax.axis_size("space")
    return Here(t, t == 0, t == times - 1, s > 0, s < blocks - 1, lax.rem(s, 2) == 0)


def call(body, out_shapes, operands, specs=None, scratch=(), out_specs=None, aliases=None):
    operands = list(operands)
    specs = specs or [VMEM] * len(operands)
    operands = [
        pltpu.with_memory_space_constraint(x, pltpu.HBM) if spec is HBM else x for x, spec in zip(operands, specs)
    ]
    return pl.pallas_call(
        body,
        out_shape=[jax.ShapeDtypeStruct(s, F32) for s in out_shapes],
        in_specs=specs,
        out_specs=out_specs or [VMEM] * len(out_shapes),
        scratch_shapes=list(scratch),
        input_output_aliases=aliases or {},
        compiler_params=pltpu.CompilerParams(vmem_limit_bytes=8 * 1024 * 1024),
    )(*operands)


def lane_scratch(rows, columns):
    return pltpu.VMEM((columns // LANES, rows, LANES), F32)


def split3(x):
    hi = x.astype(jnp.bfloat16)
    rest = x - hi.astype(F32)
    mid = rest.astype(jnp.bfloat16)
    low = (rest - mid.astype(F32)).astype(jnp.bfloat16)
    return hi, mid, low


def dot3(x, m):
    parts = [jnp.dot(p, m, preferred_element_type=F32) for p in split3(x)]
    return parts[0] + (parts[1] + parts[2])


def pair_matrix(fine, coarse, value):
    rows = lax.broadcasted_iota(jnp.int32, (fine, coarse), 0)
    cols = lax.broadcasted_iota(jnp.int32, (fine, coarse), 1)
    return jnp.where((rows >> 1) == cols, value, 0.0).astype(jnp.bfloat16)


def repeat_matrix(coarse, fine):
    rows = lax.broadcasted_iota(jnp.int32, (coarse, fine), 0)
    cols = lax.broadcasted_iota(jnp.int32, (coarse, fine), 1)
    return jnp.where(rows == (cols >> 1), 1.0, 0.0).astype(jnp.bfloat16)


def restrict_planes(first, second, scratch, matrix):
    blocks, ny, _ = scratch.shape
    sums = dot3(first + second, matrix)
    parts = []
    for b in range(blocks):
        scratch[b] = sums[:, b * LANES:(b + 1) * LANES]
        parts.append(scratch[b, pl.ds(0, ny // 2, 2), :] + scratch[b, pl.ds(1, ny // 2, 2), :])
    return jnp.concatenate(parts, axis=1)


class Field:
    def __init__(self, pieces, edges):
        self.pieces, self.edges, self.moved = pieces, edges, {}

    def tile(self, a):
        for first, end, ref, index, base in self.pieces:
            if first <= a and a + TILE <= end:
                return ref[index + (slice(a - base, a - base + TILE),)]
        return None

    def rolled(self, a, shift):
        if (a, shift) not in self.moved:
            tile = self.tile(a)
            self.moved[a, shift] = None if tile is None else pltpu.roll(tile, shift, 0)
        return self.moved[a, shift]

    def neighbour(self, a, other, shift, edge):
        own, next_ = self.rolled(a, shift), self.rolled(other, shift)
        return own if next_ is None else jnp.where(edge, next_, own)

    def above(self, a):
        return self.neighbour(a, a - TILE, 1, self.edges[0])

    def below(self, a):
        return self.neighbour(a, a + TILE, TILE - 1, self.edges[1])


def edges(nz):
    row = lax.broadcasted_iota(jnp.int32, (TILE, nz), 0)
    return row == 0, row == TILE - 1


def fields(spans, refs, planes, nz):
    e = edges(nz)
    return [
        Field([(a, b, ref, (p,), base) for (a, b, base), ref in zip(spans, refs)], e)
        for p in range(planes)
    ]


def face_coefficients(k, above, below, half, a, size, ny, nz):
    row = lax.broadcasted_iota(jnp.int32, (size, nz), 0) + a
    col = lax.broadcasted_iota(jnp.int32, (size, nz), 1)
    up_face = half * (k + jnp.where(row == 0, 0.0, above))
    down_face = half * (k + jnp.where(row == ny - 1, 0.0, below))
    right = pltpu.roll(k, nz - 1, 1)
    left = pltpu.roll(k, 1, 1)
    right_face = half * (k + jnp.where(col == nz - 1, 0.0, right))
    left_face = half * (k + jnp.where(col == 0, 0.0, left))
    total = (up_face + down_face) + (right_face + left_face)
    return (
        jnp.where(row == 0, 0.0, up_face),
        jnp.where(row == ny - 1, 0.0, down_face),
        jnp.where(col == nz - 1, 0.0, right_face),
        total,
    )


def prepare_fine(cond):
    nx, ny, nz = cond.shape

    def body(k_ref, kx, up, down, right, diag):
        planes = fields([(0, ny, 0)], [k_ref], nx, nz)
        for p in range(nx):
            for a in range(0, ny, TILE):
                s = slice(a, a + TILE)
                k = k_ref[p, s]
                u, d, r, total = face_coefficients(
                    k, planes[p].above(a), planes[p].below(a), HALF_FINE, a, TILE, ny, nz)
                up[p, s], down[p, s], right[p, s] = u, d, r
                if p > 0:
                    total = total + kx[p - 1, s]
                if p < nx - 1:
                    face = HALF_FINE * (k + k_ref[p + 1, s])
                    kx[p, s] = face
                    total = total + face
                diag[p, s] = 1.0 - total
    full = (nx, ny, nz)
    return call(body, [(nx - 1, ny, nz), full, full, full, full], [cond])


def restricted(field):
    nx, ny, nz = field.shape

    def body(f_ref, out, scratch):
        matrix = pair_matrix(nz, nz // 2, 0.125)
        for q in range(nx // 2):
            out[q] = restrict_planes(f_ref[2 * q], f_ref[2 * q + 1], scratch, matrix)

    return call(
        body, [(nx // 2, ny // 2, nz // 2)], [field], scratch=[lane_scratch(ny, nz // 2)]
    )[0]


def row_copies(source, out, rows, at, sems, first_sem, planes):
    start, end = rows
    return [
        pltpu.make_async_copy(
            source.at[p, pl.ds(start, end - start)], out.at[i, pl.ds(at, end - start)], sems.at[first_sem + i])
        for i, p in enumerate(planes)
    ]


def run(copies):
    for c in copies:
        c.start()
    for c in copies:
        c.wait()


def chosen(flag, body, this, other):
    pl.when(flag)(lambda: body(this))
    pl.when(jnp.logical_not(flag))(lambda: body(other))


def first_block(initial, prior, cond, end):
    nx, ny, nz = cond.shape

    def body(i_ref, p_ref, k_hbm, k_ref, v_ref, down, up, sems):
        def copy(ref):
            run(row_copies(k_hbm, k_ref, (0, ny), 0, sems, 0, range(nx))
                + row_copies(ref, v_ref, (0, end), 0, sems, nx, range(nx)))

        chosen(here().last, copy, i_ref, p_ref)
        k = fields([(0, ny, 0)], [k_ref], nx, nz)
        v = fields([(0, end, 0)], [v_ref], nx, nz)
        for out, own, inner in ((down, 0, 1), (up, nx - 1, nx - 2)):
            for a in range(0, ny, TILE):
                own_k = k[own].tile(a)
                out[a:a + TILE] = own_k
                if a >= end:
                    continue
                u, d, r, total = face_coefficients(
                    own_k, k[own].above(a), k[own].below(a), HALF_FINE, a, TILE, ny, nz)
                face = HALF_FINE * (own_k + k[inner].tile(a))
                c, stepped = row_step(v[own], u, d, r, 1.0 - (total + face), a)
                out[ny + a:ny + a + TILE] = c
                out[ny + end + a:ny + end + a + TILE] = stepped + face * v[inner].tile(a)

    return call(
        body, [cond.shape, (nx, end, nz)] + [(ny + 2 * end, nz)] * 2, [initial, prior, cond], [HBM, HBM, HBM],
        [pltpu.SemaphoreType.DMA((2 * nx,))])


def rows_from(field, start):
    nx, ny, nz = field.shape

    def body(ref, out, sems):
        run(row_copies(ref, out, (start, ny), 0, sems, 0, range(nx)))

    return call(body, [(nx, ny - start, nz)], [field], [HBM], [pltpu.SemaphoreType.DMA((nx,))])[0]


def coarse_and_initial(cond, initial, start):
    nx, ny, nz = cond.shape

    def body(k_ref, i_ref, coarse, rows, scratch, sems):
        copies = row_copies(i_ref, rows, (start, ny), 0, sems, 0, range(nx))
        for c in copies:
            c.start()
        matrix = pair_matrix(nz, nz // 2, 0.125)
        for q in range(nx // 2):
            coarse[q] = restrict_planes(k_ref[2 * q], k_ref[2 * q + 1], scratch, matrix)
        for c in copies:
            c.wait()

    return call(
        body, [(nx // 2, ny // 2, nz // 2), (nx, ny - start, nz)], [cond, initial], [VMEM, HBM],
        [lane_scratch(ny, nz // 2), pltpu.SemaphoreType.DMA((nx,))])


def row_step(v, up, down, right, diag, a):
    c = v.tile(a)
    nz = c.shape[1]
    total = diag * c
    total = total + up * v.above(a)
    total = total + down * v.below(a)
    total = total + right * pltpu.roll(c, nz - 1, 1)
    return c, total + pltpu.roll(right * c, 1, 1)


def block_step(planes, p, coefficients, a):
    kx, up, down, right, diag = coefficients
    s = slice(a, a + TILE)
    c, total = row_step(planes[p], up[p, s], down[p, s], right[p, s], diag[p, s], a)
    if p > 0:
        total = total + kx[p - 1, s] * planes[p - 1].tile(a)
    if p < len(planes) - 1:
        total = total + kx[p, s] * planes[p + 1].tile(a)
    return c, total


def half_step(state, window, coefficients, ahead=()):
    nx, rows, nz = state.shape
    w0, w1 = window

    def body(v_ref, *refs):
        v, out = fields([(w0, w1, w0)], [v_ref], nx, nz), refs[-1]
        for p in range(nx):
            for a in range(w0, w1, TILE):
                out[p, a - w0:a - w0 + TILE] = block_step(v, p, refs[:5], a)[1]

    return call(body, [state.shape], [state, *coefficients, *ahead])[0]


def lower_start(initial, received, window, coefficients, coarse, after):
    nx, rows, nz = received.shape
    w0, w1 = window
    extra = coarse.shape[1] // 2

    def body(i_ref, r_ref, *refs):
        coarse_ref, _, state, part, down, up = refs[5:]
        first = here().first
        for p in range(nx):
            for a in range(0, rows, TILE):
                s = slice(a, a + TILE)
                state[p, s] = jnp.where(first, i_ref[p, s], r_ref[p, s])
        edge_messages(state, part, down, up, refs[:5], window)
        for out, q in ((down, 0), (up, coarse.shape[0] - 1)):
            for i in range(2):
                out[2 * rows:, i * nz // 2:(i + 1) * nz // 2] = coarse_ref[q, i * extra:(i + 1) * extra]

    return call(
        body, [received.shape] * 2 + [(2 * rows + extra, nz)] * 2,
        [initial, received, *coefficients, coarse, after])


def edge_messages(state, part, down, up, coefficients, window):
    nx, rows, nz = state.shape
    w0, w1 = window
    v = fields([(w0, w1, w0)], [state], nx, nz)
    for p in range(nx):
        out = down if p == 0 else up if p == nx - 1 else None
        if part is None and out is None:
            continue
        for a in range(w0, w1, TILE):
            d = slice(a - w0, a - w0 + TILE)
            c, total = block_step(v, p, coefficients, a)
            if part is not None:
                part[p, d] = total
            if out is not None:
                out[d] = c
                out[slice(rows + d.start, rows + d.stop)] = total


def two_steps(state, started, before, after, conds, cond, window, result, coefficients, final=False):
    nx, rows, nz = state.shape
    ny = cond.shape[1]
    (w0, w1), (r0, r1) = window, result
    sides = [before, after]

    def body(v_ref, part, k_ref, *refs):
        k_sides, messages, coef, rest = refs[:2], refs[2:6], refs[6:11], refs[11:]
        out, rest = rest[0], rest[1:]
        mid = rest[-2] if final else rest[-1]
        me = here()
        owns = ((0, 0, me.has_lo), (1, nx - 1, me.has_hi))

        def face(side, own, has, s):
            return HALF_FINE * (k_ref[own, s] + jnp.where(has, k_sides[side][s], 0.0))

        for side, own, has in owns:
            (_, v_at), (_, p_at) = sides[side]
            near, half_done = messages[2 * side:2 * side + 2]
            for a in range(w0, w1, TILE):
                s, d = slice(a, a + TILE), slice(a - w0, a - w0 + TILE)
                theirs = jnp.where(has, near[slice(v_at + d.start, v_at + d.stop)], 0.0)
                flow = face(side, own, has, s) * (theirs - v_ref[own, d])
                mid[2 + side, d] = part[own, d] + flow
                mid[side, d] = jnp.where(has, half_done[slice(p_at + d.start, p_at + d.stop)] - flow, 0.0)
        span = [(w0, w1, w0)]
        edge = fields(span, [mid], 4, nz)
        w = fields(span, [part], nx, nz)
        w[0], w[nx - 1] = edge[2], edge[3]
        for p in range(nx):
            for a in range(r0, r1, TILE):
                c, total = block_step(w, p, coef, a)
                for side, own, has in owns:
                    if p == own:
                        s = slice(a, a + TILE)
                        total = total + face(side, own, has, s) * (edge[side].tile(a) - c)
                out[p, a - r0:a - r0 + TILE] = total
        if final:
            matrix = pair_matrix(nz, nz // 2, 0.125)
            for q in range(nx // 2):
                rest[0][q] = restrict_planes(out[2 * q], out[2 * q + 1], rest[-1], matrix)
        else:
            edge_messages(out, None, rest[0], rest[1], coef, window)

    shape = (nx, r1 - r0, nz)
    scratch = [pltpu.VMEM((4, w1 - w0, nz), F32)]
    if final:
        shapes = [shape, (nx // 2, (r1 - r0) // 2, nz // 2)]
        scratch.append(lane_scratch(r1 - r0, nz // 2))
    else:
        shapes = [shape, (2 * rows, nz), (2 * rows, nz)]
    messages = [array for side in sides for array, _ in side]
    return call(body, shapes, [state, started, cond, *conds, *messages, *coefficients], scratch=scratch)


def coarse_coefficients(own, before, after, at):
    nx, ny, nz = own.shape

    def body(k_own, lo, hi, kx, up, down, right, diag):
        me = here()

        def side(ref, has):
            k = jnp.concatenate([ref[at:, :nz], ref[at:, nz:]], axis=0)
            return jnp.where(has, k, 0.0)

        planes = [side(lo, me.has_lo)] + [k_own[p] for p in range(nx)] + [side(hi, me.has_hi)]
        for i in range(nx + 1):
            kx[i] = HALF_COARSE * (planes[i] + planes[i + 1])
        for p in range(nx):
            k = k_own[p]
            u, d, r, total = face_coefficients(
                k, pltpu.roll(k, 1, 0), pltpu.roll(k, ny - 1, 0), HALF_COARSE, 0, ny, ny, nz)
            up[p], down[p], right[p] = u, d, r
            if p > 0:
                total = total + kx[p]
            if p < nx - 1:
                total = total + kx[p + 1]
            diag[p] = 1.0 - total

    full = (nx, ny, nz)
    return call(body, [(nx + 1, ny, nz)] + [full] * 4, [own, before, after])


def sweep_messages(state, part, on, off, coefficients):
    nx, ny, nz = state.shape
    kx, up, down, right, diag = coefficients
    even = here().even
    v = fields([(0, ny, 0)], [state], nx, nz)
    for a in range(0, ny, TILE):
        s = slice(a, a + TILE)
        both = []
        for p in range(nx):
            c, total = row_step(v[p], up[p, s], down[p, s], right[p, s], diag[p, s], a)
            if p > 0:
                total = total + kx[p, s] * v[p - 1].tile(a)
            if p < nx - 1:
                total = total + kx[p + 1, s] * v[p + 1].tile(a)
            part[p, s] = total
            both.append((c, total))
        for i in range(2):
            d = slice(i * ny + a, i * ny + a + TILE)
            on[d] = jnp.where(even, both[-1][i], both[0][i])
            off[d] = jnp.where(even, both[0][i], both[-1][i])


def sweep_start(upper, lower, cut, coefficients):
    nx, ny, nz = upper.shape

    def body(a_ref, b_ref, *refs):
        last = here().last
        state = refs[5]
        for p in range(nx):
            for a in range(0, ny, TILE):
                s = slice(a, a + TILE)
                state[p, s] = jnp.where(last, (a_ref if a < cut else b_ref)[p, s], 0.0)
        sweep_messages(*refs[5:], refs[:5])

    return call(body, [upper.shape] * 2 + [(2 * ny, nz)] * 2, [upper, lower, *coefficients])


def sweep_step(state, part, on, off, cut, coefficients, jumps=(), later=0):
    nx, ny, nz = state.shape

    def body(v_ref, part_ref, on_ref, off_ref, *refs):
        coef, rest = refs[:5], refs[5:]
        kx, up, down, right, diag = coef
        jump_refs, rest = rest[:len(jumps)], rest[len(jumps):]
        out, mid = rest[0], rest[-1]
        me = here()
        for a in range(0, ny, TILE):
            s = slice(a, a + TILE)
            for i, (own, has) in enumerate(((0, me.has_lo), (nx - 1, me.has_hi))):
                refs_of = (off_ref, on_ref) if i == 0 else (on_ref, off_ref)
                theirs, half_done = (
                    jnp.where(has, jnp.where(me.even, *(r[slice(j * ny + a, j * ny + a + TILE)] for r in refs_of)), 0.0)
                    for j in range(2)
                )
                flow = kx[i * nx, s] * (theirs - v_ref[own, s])
                mid[1 + own, s] = part_ref[own, s] + flow
                mid[i * (nx + 1), s] = jnp.where(has, half_done - flow, 0.0)
            for p in range(1, nx - 1):
                mid[1 + p, s] = part_ref[p, s]
        w = fields([(0, ny, 0)], [mid], nx + 2, nz)
        for p in range(nx):
            for a in range(0, ny, TILE):
                s = slice(a, a + TILE)
                c, e = row_step(w[p + 1], up[p, s], down[p, s], right[p, s], diag[p, s], a)
                for i, q in ((p, p), (p + 1, p + 2)):
                    other = w[q].tile(a)
                    e = e + kx[i, s] * (other - c if i in (0, nx) else other)
                if jumps:
                    jump = jump_refs[0 if a < cut else 1][p, s]
                    e = e + jnp.where(me.t >= later, jump, 0.0)
                out[p, s] = e
        if jumps:
            sweep_messages(out, *rest[1:4], coef)

    shapes = [state.shape]
    if jumps:
        shapes += [state.shape] + [on.shape] * 2
    return call(
        body, shapes, [state, part, on, off, *coefficients, *jumps], scratch=[pltpu.VMEM((nx + 2, ny, nz), F32)])


def jumps_of(moved, own, next_prior, own_prior):
    nx, rows, nz = moved.shape

    def body(a_ref, b_ref, next_ref, own_ref, out):
        for p in range(nx):
            out[p, :rows] = a_ref[p] - next_ref[p, :rows]
            out[p, rows:] = b_ref[p] - own_ref[p, rows:]

    return call(body, [own_prior.shape], [moved, own, next_prior, own_prior])[0]


def prolonged(e_ref, rows, q, spread, wide):
    row = dot3(e_ref[q, rows], spread)
    count = row.shape[0]
    for b in range(wide.shape[0]):
        s = slice(b * LANES, (b + 1) * LANES)
        wide[b, pl.ds(0, count, 2), :] = row[:, s]
        wide[b, pl.ds(1, count, 2), :] = row[:, s]


def finish_lower(fine, coarse, prior, correction):
    nx, ny, nz = prior.shape
    rows = fine.shape[1]
    cut = ny - rows

    def body(f_ref, c_ref, p_ref, e_ref, update, tail, rest, out, tail_out, upper, lower, sems):
        spread = repeat_matrix(nz // 2, nz)
        copies = []
        for q in range(nx // 2):
            tail_out[q] = e_ref[q, cut // 2:] + c_ref[q]
            copies.append(pltpu.make_async_copy(
                tail_out.at[q], tail.at[q, pl.ds(cut // 2, rows // 2)], sems.at[nx + q]))
            copies[-1].start()
        for q in range(nx // 2):
            prolonged(e_ref, slice(cut // 2, ny // 2), q, spread, lower)
            for p in (2 * q, 2 * q + 1):
                for b in range(nz // LANES):
                    s = slice(b * LANES, (b + 1) * LANES)
                    out[p, :, s] = (f_ref[p, :, s] + lower[b]) - p_ref[p, cut:, s]
                copies.append(pltpu.make_async_copy(out.at[p], update.at[p, pl.ds(cut, rows)], sems.at[p]))
                copies[-1].start()
        for q in range(nx // 2):
            prolonged(e_ref, slice(0, cut // 2), q, spread, upper)
            for p in (2 * q, 2 * q + 1):
                for b in range(nz // LANES):
                    s = slice(b * LANES, (b + 1) * LANES)
                    rest[p, :, s] = upper[b] - p_ref[p, :cut, s]
        for c in copies:
            c.wait()

    return call(
        body, [prior.shape, correction.shape, (nx, cut, nz)], [fine, coarse, prior, correction],
        scratch=[pltpu.VMEM(fine.shape, F32), pltpu.VMEM(coarse.shape, F32), lane_scratch(cut, nz),
                 lane_scratch(rows, nz), pltpu.SemaphoreType.DMA((nx + nx // 2,))],
        out_specs=[HBM, HBM, VMEM])


def finish_upper(fine_first, fine, correction, rest, update, tail):
    nx, rows, nz = fine.shape

    def body(first_ref, other_ref, e_ref, rest_ref, *refs):
        update, tail, out, tail_out, f_ref, scratch, sems = refs[2:]
        first = here().first
        copies = []
        for p in range(nx):
            for a in range(0, rows, TILE):
                s = slice(a, a + TILE)
                f = jnp.where(first, first_ref[p, s], other_ref[p, s])
                f_ref[p, s] = f
                out[p, s] = f + rest_ref[p, s]
            copies.append(pltpu.make_async_copy(out.at[p], update.at[p, pl.ds(0, rows)], sems.at[p]))
            copies[-1].start()
        matrix = pair_matrix(nz, nz // 2, 0.125)
        for q in range(nx // 2):
            tail_out[q] = e_ref[q, :rows // 2] + restrict_planes(f_ref[2 * q], f_ref[2 * q + 1], scratch, matrix)
            copies.append(pltpu.make_async_copy(tail_out.at[q], tail.at[q, pl.ds(0, rows // 2)], sems.at[nx + q]))
            copies[-1].start()
        for c in copies:
            c.wait()

    return call(
        body, [update.shape, tail.shape], [fine_first, fine, correction, rest, update, tail],
        [VMEM] * 4 + [HBM] * 2,
        [pltpu.VMEM(fine.shape, F32), pltpu.VMEM((nx // 2, rows // 2, nz // 2), F32), pltpu.VMEM(fine.shape, F32),
         lane_scratch(rows, nz // 2), pltpu.SemaphoreType.DMA((nx + nx // 2,))],
        [HBM, HBM], {4: 0, 5: 1})


def ring(block, axis, distance):
    size = lax.axis_size(axis)
    return lax.ppermute(block, axis, [(i, (i + distance) % size) for i in range(size)])


def from_sides(last, first):
    return ring(last, "space", 1), ring(first, "space", -1)


def swapped(block, axis, offset):
    size = lax.axis_size(axis)
    pairs = [(i % size, (i + 1) % size) for i in range(offset, size + offset, 2)]
    return lax.ppermute(block, axis, pairs + [(j, i) for i, j in pairs])


def shards(initial, prior, conductivity):
    times = lax.axis_size("tm")
    own_prior = prior[0]
    home = times - 1
    ny = initial.shape[1]
    cut = ny * CUT[0] // CUT[1]
    wide = cut + OVERLAP
    windows = [(0, wide), (cut - OVERLAP, ny)]
    results = [(0, cut), (cut, ny)]
    start = windows[1][0]

    received = ring(rows_from(own_prior, start), "tm", 1)
    cond, upper, down, up = first_block(initial, own_prior, conductivity, wide)
    before, after = from_sides(up, down)
    coefficients = prepare_fine(cond)
    coarse_cond, initial_rows = coarse_and_initial(cond, initial, start)
    lower, lower_part, down, up = lower_start(initial_rows, received, windows[1], coefficients, coarse_cond, before)
    before_2, after_2 = from_sides(up, down)
    own_coarse = restricted(own_prior)
    next_coarse = ring(own_coarse, "tm", -1)

    conds = (before, after)
    rows = ny - start
    sides = [
        [[(x, at), (x, at + size)] for x in pair]
        for pair, at, size in ((conds, ny, wide), ((before_2, after_2), 0, rows))
    ]
    parts = [half_step(upper, windows[0], coefficients), lower_part]
    middle = [
        two_steps(state, parts[i], *sides[i], conds, cond, windows[i], windows[i], coefficients)
        for i, state in enumerate((upper, lower))
    ]
    coarse_coef = coarse_coefficients(coarse_cond, before_2, after_2, 2 * rows)
    received = [from_sides(up, down) for _, down, up in middle]
    ended = []
    for i, (state, _, _) in enumerate(middle):
        part = half_step(state, windows[i], coefficients, coarse_coef[:i])
        side = [[(x, 0), (x, x.shape[0] // 2)] for x in received[i]]
        ended.append(two_steps(state, part, *side, conds, cond, windows[i], results[i], coefficients, True))
    (moved, moved_coarse), (own_fine, fine_coarse) = ended

    jump = jumps_of(moved_coarse, fine_coarse, next_coarse, own_coarse)
    half_cut = cut // 2
    lower = ring(jump[:, half_cut:], "tm", -home)
    shifted = [jump] + [ring(jump, "tm", -j) for j in range(1, home)]
    shifted.append(jnp.concatenate([jump[:, :half_cut], lower], axis=1))
    sweep = sweep_start(shifted[0], shifted[1], half_cut, coarse_coef)
    _, early = lax.optimization_barrier((sweep[0], moved))
    moved_first = lax.ppermute(early, "tm", [(home, 0)])
    for j in range(home):
        state, part, on, off = sweep
        off, on = swapped(off, "space", 1), swapped(on, "space", 0)
        if j == 0:
            *_, moved = lax.optimization_barrier((on, off, lower, *shifted[2:home], moved))
            moved = lax.ppermute(moved, "tm", [(i, i + 1) for i in range(home)])
        more = (shifted[j + 1:j + 3], home - j - 1) if j < home - 1 else ()
        sweep = sweep_step(state, part, on, off, half_cut, coarse_coef, *more)
    update, tail, rest = finish_lower(own_fine, fine_coarse, own_prior, sweep[0])
    update, tail = finish_upper(moved_first, moved, sweep[0], rest, update, tail)
    return update[None], tail[None]


def solution(mesh):
    return jax.shard_map(
        shards,
        mesh=mesh,
        in_specs=(P("space", None, None), P("tm", "space", None, None), P("space", None, None)),
        out_specs=(P("tm", "space", None, None), P("tm", "space", None, None)),
        check_vma=False,
    )
```

```python
from typing import Any, NamedTuple

import jax
import jax.numpy as jnp
from jax import lax
from jax.experimental import pallas as pl
from jax.experimental.pallas import tpu as pltpu
from jax.sharding import PartitionSpec as P

FINE_RATE = 0.16
HALF_FINE = 0.5 * FINE_RATE
HALF_COARSE = 0.25 * FINE_RATE
TILE = 8
OVERLAP = 8
CUT = (5, 8)
LANES = 128

VMEM = pl.BlockSpec(memory_space=pltpu.VMEM)
HBM = pl.BlockSpec(memory_space=pltpu.HBM)
F32 = jnp.float32


class Here(NamedTuple):
    t: Any
    first: Any
    last: Any
    has_lo: Any
    has_hi: Any
    even: Any


def here():
    t, s = lax.axis_index("tm"), lax.axis_index("space")
    times, blocks = lax.axis_size("tm"), lax.axis_size("space")
    return Here(t, t == 0, t == times - 1, s > 0, s < blocks - 1, lax.rem(s, 2) == 0)


def call(body, out_shapes, operands, specs=None, scratch=(), out_specs=None, aliases=None):
    operands = list(operands)
    specs = specs or [VMEM] * len(operands)
    operands = [
        pltpu.with_memory_space_constraint(x, pltpu.HBM) if spec is HBM else x for x, spec in zip(operands, specs)
    ]
    return pl.pallas_call(
        body,
        out_shape=[jax.ShapeDtypeStruct(s, F32) for s in out_shapes],
        in_specs=specs,
        out_specs=out_specs or [VMEM] * len(out_shapes),
        scratch_shapes=list(scratch),
        input_output_aliases=aliases or {},
        compiler_params=pltpu.CompilerParams(vmem_limit_bytes=8 * 1024 * 1024),
    )(*operands)


def lane_scratch(rows, columns):
    return pltpu.VMEM((columns // LANES, rows, LANES), F32)


def split3(x):
    hi = x.astype(jnp.bfloat16)
    rest = x - hi.astype(F32)
    mid = rest.astype(jnp.bfloat16)
    low = (rest - mid.astype(F32)).astype(jnp.bfloat16)
    return hi, mid, low


def dot3(x, m):
    parts = [jnp.dot(p, m, preferred_element_type=F32) for p in split3(x)]
    return parts[0] + (parts[1] + parts[2])


def pair_matrix(fine, coarse, value):
    rows = lax.broadcasted_iota(jnp.int32, (fine, coarse), 0)
    cols = lax.broadcasted_iota(jnp.int32, (fine, coarse), 1)
    return jnp.where((rows >> 1) == cols, value, 0.0).astype(jnp.bfloat16)


def repeat_matrix(coarse, fine):
    rows = lax.broadcasted_iota(jnp.int32, (coarse, fine), 0)
    cols = lax.broadcasted_iota(jnp.int32, (coarse, fine), 1)
    return jnp.where(rows == (cols >> 1), 1.0, 0.0).astype(jnp.bfloat16)


def restrict_planes(first, second, scratch, matrix):
    blocks, ny, _ = scratch.shape
    sums = dot3(first + second, matrix)
    parts = []
    for b in range(blocks):
        scratch[b] = sums[:, b * LANES:(b + 1) * LANES]
        parts.append(scratch[b, pl.ds(0, ny // 2, 2), :] + scratch[b, pl.ds(1, ny // 2, 2), :])
    return jnp.concatenate(parts, axis=1)


class Field:
    def __init__(self, pieces, edges):
        self.pieces, self.edges, self.moved = pieces, edges, {}

    def tile(self, a):
        for first, end, ref, index, base in self.pieces:
            if first <= a and a + TILE <= end:
                return ref[index + (slice(a - base, a - base + TILE),)]
        return None

    def rolled(self, a, shift):
        if (a, shift) not in self.moved:
            tile = self.tile(a)
            self.moved[a, shift] = None if tile is None else pltpu.roll(tile, shift, 0)
        return self.moved[a, shift]

    def neighbour(self, a, other, shift, edge):
        own, next_ = self.rolled(a, shift), self.rolled(other, shift)
        return own if next_ is None else jnp.where(edge, next_, own)

    def above(self, a):
        return self.neighbour(a, a - TILE, 1, self.edges[0])

    def below(self, a):
        return self.neighbour(a, a + TILE, TILE - 1, self.edges[1])


def edges(nz):
    row = lax.broadcasted_iota(jnp.int32, (TILE, nz), 0)
    return row == 0, row == TILE - 1


def fields(spans, refs, planes, nz):
    e = edges(nz)
    return [
        Field([(a, b, ref, (p,), base) for (a, b, base), ref in zip(spans, refs)], e)
        for p in range(planes)
    ]


def face_coefficients(k, above, below, half, a, size, ny, nz):
    row = lax.broadcasted_iota(jnp.int32, (size, nz), 0) + a
    col = lax.broadcasted_iota(jnp.int32, (size, nz), 1)
    up_face = half * (k + jnp.where(row == 0, 0.0, above))
    down_face = half * (k + jnp.where(row == ny - 1, 0.0, below))
    right = pltpu.roll(k, nz - 1, 1)
    left = pltpu.roll(k, 1, 1)
    right_face = half * (k + jnp.where(col == nz - 1, 0.0, right))
    left_face = half * (k + jnp.where(col == 0, 0.0, left))
    total = (up_face + down_face) + (right_face + left_face)
    return (
        jnp.where(row == 0, 0.0, up_face),
        jnp.where(row == ny - 1, 0.0, down_face),
        jnp.where(col == nz - 1, 0.0, right_face),
        total,
    )


def prepare_fine(cond):
    nx, ny, nz = cond.shape

    def body(k_ref, kx, up, down, right, diag):
        planes = fields([(0, ny, 0)], [k_ref], nx, nz)
        for p in range(nx):
            for a in range(0, ny, TILE):
                s = slice(a, a + TILE)
                k = k_ref[p, s]
                u, d, r, total = face_coefficients(
                    k, planes[p].above(a), planes[p].below(a), HALF_FINE, a, TILE, ny, nz)
                up[p, s], down[p, s], right[p, s] = u, d, r
                if p > 0:
                    total = total + kx[p - 1, s]
                if p < nx - 1:
                    face = HALF_FINE * (k + k_ref[p + 1, s])
                    kx[p, s] = face
                    total = total + face
                diag[p, s] = 1.0 - total
    full = (nx, ny, nz)
    return call(body, [(nx - 1, ny, nz), full, full, full, full], [cond])


def restricted(field):
    nx, ny, nz = field.shape

    def body(f_ref, out, scratch):
        matrix = pair_matrix(nz, nz // 2, 0.125)
        for q in range(nx // 2):
            out[q] = restrict_planes(f_ref[2 * q], f_ref[2 * q + 1], scratch, matrix)

    return call(
        body, [(nx // 2, ny // 2, nz // 2)], [field], scratch=[lane_scratch(ny, nz // 2)]
    )[0]


def row_copies(source, out, rows, at, sems, first_sem, planes):
    start, end = rows
    return [
        pltpu.make_async_copy(
            source.at[p, pl.ds(start, end - start)], out.at[i, pl.ds(at, end - start)], sems.at[first_sem + i])
        for i, p in enumerate(planes)
    ]


def run(copies):
    for c in copies:
        c.start()
    for c in copies:
        c.wait()


def chosen(flag, body, this, other):
    pl.when(flag)(lambda: body(this))
    pl.when(jnp.logical_not(flag))(lambda: body(other))


def first_block(initial, prior, cond, end):
    nx, ny, nz = cond.shape

    def body(i_ref, p_ref, k_hbm, k_ref, v_ref, down, up, sems):
        k = fields([(0, ny, 0)], [k_ref], nx, nz)
        v = fields([(0, end, 0)], [v_ref], nx, nz)

        def message(out, own, inner):
            for a in range(0, ny, TILE):
                own_k = k[own].tile(a)
                out[a:a + TILE] = own_k
                if a >= end:
                    continue
                u, d, r, total = face_coefficients(
                    own_k, k[own].above(a), k[own].below(a), HALF_FINE, a, TILE, ny, nz)
                face = HALF_FINE * (own_k + k[inner].tile(a))
                c, stepped = row_step(v[own], u, d, r, 1.0 - (total + face), a)
                out[ny + a:ny + a + TILE] = c
                out[ny + end + a:ny + end + a + TILE] = stepped + face * v[inner].tile(a)

        def copy(ref):
            for x in k + v:
                x.moved.clear()
            conds = row_copies(k_hbm, k_ref, (0, ny), 0, sems, 0, range(nx))
            states = row_copies(ref, v_ref, (0, end), 0, sems, nx, range(nx))
            groups = [conds[:2] + states[:2], conds[2:] + states[2:]]
            for c in groups[0] + groups[1]:
                c.start()
            for c in groups[0]:
                c.wait()
            message(down, 0, 1)
            for c in groups[1]:
                c.wait()
            message(up, nx - 1, nx - 2)

        chosen(here().last, copy, i_ref, p_ref)

    return call(
        body, [cond.shape, (nx, end, nz)] + [(ny + 2 * end, nz)] * 2, [initial, prior, cond], [HBM, HBM, HBM],
        [pltpu.SemaphoreType.DMA((2 * nx,))])


def rows_from(field, start):
    nx, ny, nz = field.shape

    def body(ref, out, sems):
        run(row_copies(ref, out, (start, ny), 0, sems, 0, range(nx)))

    return call(body, [(nx, ny - start, nz)], [field], [HBM], [pltpu.SemaphoreType.DMA((nx,))])[0]


def coarse_and_initial(cond, initial, start):
    nx, ny, nz = cond.shape

    def body(k_ref, i_ref, coarse, rows, scratch, sems):
        copies = row_copies(i_ref, rows, (start, ny), 0, sems, 0, range(nx))
        for c in copies:
            c.start()
        matrix = pair_matrix(nz, nz // 2, 0.125)
        for q in range(nx // 2):
            coarse[q] = restrict_planes(k_ref[2 * q], k_ref[2 * q + 1], scratch, matrix)
        for c in copies:
            c.wait()

    return call(
        body, [(nx // 2, ny // 2, nz // 2), (nx, ny - start, nz)], [cond, initial], [VMEM, HBM],
        [lane_scratch(ny, nz // 2), pltpu.SemaphoreType.DMA((nx,))])


def row_step(v, up, down, right, diag, a):
    c = v.tile(a)
    nz = c.shape[1]
    total = diag * c
    total = total + up * v.above(a)
    total = total + down * v.below(a)
    total = total + right * pltpu.roll(c, nz - 1, 1)
    return c, total + pltpu.roll(right * c, 1, 1)


def block_step(planes, p, coefficients, a):
    kx, up, down, right, diag = coefficients
    s = slice(a, a + TILE)
    c, total = row_step(planes[p], up[p, s], down[p, s], right[p, s], diag[p, s], a)
    if p > 0:
        total = total + kx[p - 1, s] * planes[p - 1].tile(a)
    if p < len(planes) - 1:
        total = total + kx[p, s] * planes[p + 1].tile(a)
    return c, total


def half_step(state, window, coefficients, ahead=()):
    nx, rows, nz = state.shape
    w0, w1 = window

    def body(v_ref, *refs):
        v, out = fields([(w0, w1, w0)], [v_ref], nx, nz), refs[-1]
        for p in range(nx):
            for a in range(w0, w1, TILE):
                out[p, a - w0:a - w0 + TILE] = block_step(v, p, refs[:5], a)[1]

    return call(body, [state.shape], [state, *coefficients, *ahead])[0]


def lower_start(initial, received, window, coefficients, coarse, after):
    nx, rows, nz = received.shape
    w0, w1 = window
    extra = coarse.shape[1] // 2

    def body(i_ref, r_ref, *refs):
        coarse_ref, _, state, part, down, up = refs[5:]
        first = here().first
        for p in range(nx):
            for a in range(0, rows, TILE):
                s = slice(a, a + TILE)
                state[p, s] = jnp.where(first, i_ref[p, s], r_ref[p, s])
        edge_messages(state, part, down, up, refs[:5], window)
        for out, q in ((down, 0), (up, coarse.shape[0] - 1)):
            for i in range(2):
                out[2 * rows:, i * nz // 2:(i + 1) * nz // 2] = coarse_ref[q, i * extra:(i + 1) * extra]

    return call(
        body, [received.shape] * 2 + [(2 * rows + extra, nz)] * 2,
        [initial, received, *coefficients, coarse, after])


def edge_messages(state, part, down, up, coefficients, window):
    nx, rows, nz = state.shape
    w0, w1 = window
    v = fields([(w0, w1, w0)], [state], nx, nz)
    for p in range(nx):
        out = down if p == 0 else up if p == nx - 1 else None
        if part is None and out is None:
            continue
        for a in range(w0, w1, TILE):
            d = slice(a - w0, a - w0 + TILE)
            c, total = block_step(v, p, coefficients, a)
            if part is not None:
                part[p, d] = total
            if out is not None:
                out[d] = c
                out[slice(rows + d.start, rows + d.stop)] = total


def two_steps(state, started, before, after, conds, cond, window, result, coefficients, final=False):
    nx, rows, nz = state.shape
    ny = cond.shape[1]
    (w0, w1), (r0, r1) = window, result
    sides = [before, after]

    def body(v_ref, part, k_ref, *refs):
        k_sides, messages, coef, rest = refs[:2], refs[2:6], refs[6:11], refs[11:]
        out, rest = rest[0], rest[1:]
        mid = rest[-2] if final else rest[-1]
        me = here()
        owns = ((0, 0, me.has_lo), (1, nx - 1, me.has_hi))

        def face(side, own, has, s):
            return HALF_FINE * (k_ref[own, s] + jnp.where(has, k_sides[side][s], 0.0))

        for side, own, has in owns:
            (_, v_at), (_, p_at) = sides[side]
            near, half_done = messages[2 * side:2 * side + 2]
            for a in range(w0, w1, TILE):
                s, d = slice(a, a + TILE), slice(a - w0, a - w0 + TILE)
                theirs = jnp.where(has, near[slice(v_at + d.start, v_at + d.stop)], 0.0)
                flow = face(side, own, has, s) * (theirs - v_ref[own, d])
                mid[2 + side, d] = part[own, d] + flow
                mid[side, d] = jnp.where(has, half_done[slice(p_at + d.start, p_at + d.stop)] - flow, 0.0)
        span = [(w0, w1, w0)]
        edge = fields(span, [mid], 4, nz)
        w = fields(span, [part], nx, nz)
        w[0], w[nx - 1] = edge[2], edge[3]
        for p in range(nx):
            for a in range(r0, r1, TILE):
                c, total = block_step(w, p, coef, a)
                for side, own, has in owns:
                    if p == own:
                        s = slice(a, a + TILE)
                        total = total + face(side, own, has, s) * (edge[side].tile(a) - c)
                out[p, a - r0:a - r0 + TILE] = total
        if final:
            matrix = pair_matrix(nz, nz // 2, 0.125)
            for q in range(nx // 2):
                rest[0][q] = restrict_planes(out[2 * q], out[2 * q + 1], rest[-1], matrix)
        else:
            edge_messages(out, None, rest[0], rest[1], coef, window)

    shape = (nx, r1 - r0, nz)
    scratch = [pltpu.VMEM((4, w1 - w0, nz), F32)]
    if final:
        shapes = [shape, (nx // 2, (r1 - r0) // 2, nz // 2)]
        scratch.append(lane_scratch(r1 - r0, nz // 2))
    else:
        shapes = [shape, (2 * rows, nz), (2 * rows, nz)]
    messages = [array for side in sides for array, _ in side]
    return call(body, shapes, [state, started, cond, *conds, *messages, *coefficients], scratch=scratch)


def coarse_coefficients(own, before, after, at):
    nx, ny, nz = own.shape

    def body(k_own, lo, hi, kx, up, down, right, diag):
        me = here()

        def side(ref, has):
            k = jnp.concatenate([ref[at:, :nz], ref[at:, nz:]], axis=0)
            return jnp.where(has, k, 0.0)

        planes = [side(lo, me.has_lo)] + [k_own[p] for p in range(nx)] + [side(hi, me.has_hi)]
        for i in range(nx + 1):
            kx[i] = HALF_COARSE * (planes[i] + planes[i + 1])
        for p in range(nx):
            k = k_own[p]
            u, d, r, total = face_coefficients(
                k, pltpu.roll(k, 1, 0), pltpu.roll(k, ny - 1, 0), HALF_COARSE, 0, ny, ny, nz)
            up[p], down[p], right[p] = u, d, r
            if p > 0:
                total = total + kx[p]
            if p < nx - 1:
                total = total + kx[p + 1]
            diag[p] = 1.0 - total

    full = (nx, ny, nz)
    return call(body, [(nx + 1, ny, nz)] + [full] * 4, [own, before, after])


def sweep_messages(state, part, on, off, coefficients):
    nx, ny, nz = state.shape
    kx, up, down, right, diag = coefficients
    even = here().even
    v = fields([(0, ny, 0)], [state], nx, nz)
    for a in range(0, ny, TILE):
        s = slice(a, a + TILE)
        both = []
        for p in range(nx):
            c, total = row_step(v[p], up[p, s], down[p, s], right[p, s], diag[p, s], a)
            if p > 0:
                total = total + kx[p, s] * v[p - 1].tile(a)
            if p < nx - 1:
                total = total + kx[p + 1, s] * v[p + 1].tile(a)
            part[p, s] = total
            both.append((c, total))
        for i in range(2):
            d = slice(i * ny + a, i * ny + a + TILE)
            on[d] = jnp.where(even, both[-1][i], both[0][i])
            off[d] = jnp.where(even, both[0][i], both[-1][i])


def sweep_start(upper, lower, cut, coefficients):
    nx, ny, nz = upper.shape

    def body(a_ref, b_ref, *refs):
        last = here().last
        state = refs[5]
        for p in range(nx):
            for a in range(0, ny, TILE):
                s = slice(a, a + TILE)
                state[p, s] = jnp.where(last, (a_ref if a < cut else b_ref)[p, s], 0.0)
        sweep_messages(*refs[5:], refs[:5])

    return call(body, [upper.shape] * 2 + [(2 * ny, nz)] * 2, [upper, lower, *coefficients])


def sweep_step(state, part, on, off, cut, coefficients, jumps=(), later=0):
    nx, ny, nz = state.shape

    def body(v_ref, part_ref, on_ref, off_ref, *refs):
        coef, rest = refs[:5], refs[5:]
        kx, up, down, right, diag = coef
        jump_refs, rest = rest[:len(jumps)], rest[len(jumps):]
        out, mid = rest[0], rest[-1]
        me = here()
        for a in range(0, ny, TILE):
            s = slice(a, a + TILE)
            for i, (own, has) in enumerate(((0, me.has_lo), (nx - 1, me.has_hi))):
                refs_of = (off_ref, on_ref) if i == 0 else (on_ref, off_ref)
                theirs, half_done = (
                    jnp.where(has, jnp.where(me.even, *(r[slice(j * ny + a, j * ny + a + TILE)] for r in refs_of)), 0.0)
                    for j in range(2)
                )
                flow = kx[i * nx, s] * (theirs - v_ref[own, s])
                mid[1 + own, s] = part_ref[own, s] + flow
                mid[i * (nx + 1), s] = jnp.where(has, half_done - flow, 0.0)
            for p in range(1, nx - 1):
                mid[1 + p, s] = part_ref[p, s]
        w = fields([(0, ny, 0)], [mid], nx + 2, nz)
        for p in range(nx):
            for a in range(0, ny, TILE):
                s = slice(a, a + TILE)
                c, e = row_step(w[p + 1], up[p, s], down[p, s], right[p, s], diag[p, s], a)
                for i, q in ((p, p), (p + 1, p + 2)):
                    other = w[q].tile(a)
                    e = e + kx[i, s] * (other - c if i in (0, nx) else other)
                if jumps:
                    jump = jump_refs[0 if a < cut else 1][p, s]
                    e = e + jnp.where(me.t >= later, jump, 0.0)
                out[p, s] = e
        if jumps:
            sweep_messages(out, *rest[1:4], coef)

    shapes = [state.shape]
    if jumps:
        shapes += [state.shape] + [on.shape] * 2
    return call(
        body, shapes, [state, part, on, off, *coefficients, *jumps], scratch=[pltpu.VMEM((nx + 2, ny, nz), F32)])


def jumps_of(moved, own, next_prior, own_prior):
    nx, rows, nz = moved.shape

    def body(a_ref, b_ref, next_ref, own_ref, out):
        for p in range(nx):
            out[p, :rows] = a_ref[p] - next_ref[p, :rows]
            out[p, rows:] = b_ref[p] - own_ref[p, rows:]

    return call(body, [own_prior.shape], [moved, own, next_prior, own_prior])[0]


def prolonged(e_ref, rows, q, spread, wide):
    row = dot3(e_ref[q, rows], spread)
    count = row.shape[0]
    for b in range(wide.shape[0]):
        s = slice(b * LANES, (b + 1) * LANES)
        wide[b, pl.ds(0, count, 2), :] = row[:, s]
        wide[b, pl.ds(1, count, 2), :] = row[:, s]


def finish_lower(fine, coarse, prior, correction):
    nx, ny, nz = prior.shape
    rows = fine.shape[1]
    cut = ny - rows

    def body(f_ref, c_ref, p_ref, e_ref, update, tail, rest, out, tail_out, upper, lower, sems):
        spread = repeat_matrix(nz // 2, nz)
        copies = []
        for q in range(nx // 2):
            tail_out[q] = e_ref[q, cut // 2:] + c_ref[q]
            copies.append(pltpu.make_async_copy(
                tail_out.at[q], tail.at[q, pl.ds(cut // 2, rows // 2)], sems.at[nx + q]))
            copies[-1].start()
        for q in range(nx // 2):
            prolonged(e_ref, slice(cut // 2, ny // 2), q, spread, lower)
            for p in (2 * q, 2 * q + 1):
                for b in range(nz // LANES):
                    s = slice(b * LANES, (b + 1) * LANES)
                    out[p, :, s] = (f_ref[p, :, s] + lower[b]) - p_ref[p, cut:, s]
                copies.append(pltpu.make_async_copy(out.at[p], update.at[p, pl.ds(cut, rows)], sems.at[p]))
                copies[-1].start()
        for q in range(nx // 2):
            prolonged(e_ref, slice(0, cut // 2), q, spread, upper)
            for p in (2 * q, 2 * q + 1):
                for b in range(nz // LANES):
                    s = slice(b * LANES, (b + 1) * LANES)
                    rest[p, :, s] = upper[b] - p_ref[p, :cut, s]
        for c in copies:
            c.wait()

    return call(
        body, [prior.shape, correction.shape, (nx, cut, nz)], [fine, coarse, prior, correction],
        scratch=[pltpu.VMEM(fine.shape, F32), pltpu.VMEM(coarse.shape, F32), lane_scratch(cut, nz),
                 lane_scratch(rows, nz), pltpu.SemaphoreType.DMA((nx + nx // 2,))],
        out_specs=[HBM, HBM, VMEM])


def finish_upper(fine_first, fine, correction, rest, update, tail):
    nx, rows, nz = fine.shape

    def body(first_ref, other_ref, e_ref, rest_ref, *refs):
        update, tail, out, tail_out, f_ref, scratch, sems = refs[2:]
        first = here().first
        copies = []
        for p in range(nx):
            for a in range(0, rows, TILE):
                s = slice(a, a + TILE)
                f = jnp.where(first, first_ref[p, s], other_ref[p, s])
                f_ref[p, s] = f
                out[p, s] = f + rest_ref[p, s]
            copies.append(pltpu.make_async_copy(out.at[p], update.at[p, pl.ds(0, rows)], sems.at[p]))
            copies[-1].start()
        matrix = pair_matrix(nz, nz // 2, 0.125)
        for q in range(nx // 2):
            tail_out[q] = e_ref[q, :rows // 2] + restrict_planes(f_ref[2 * q], f_ref[2 * q + 1], scratch, matrix)
            copies.append(pltpu.make_async_copy(tail_out.at[q], tail.at[q, pl.ds(0, rows // 2)], sems.at[nx + q]))
            copies[-1].start()
        for c in copies:
            c.wait()

    return call(
        body, [update.shape, tail.shape], [fine_first, fine, correction, rest, update, tail],
        [VMEM] * 4 + [HBM] * 2,
        [pltpu.VMEM(fine.shape, F32), pltpu.VMEM((nx // 2, rows // 2, nz // 2), F32), pltpu.VMEM(fine.shape, F32),
         lane_scratch(rows, nz // 2), pltpu.SemaphoreType.DMA((nx + nx // 2,))],
        [HBM, HBM], {4: 0, 5: 1})


def ring(block, axis, distance):
    size = lax.axis_size(axis)
    return lax.ppermute(block, axis, [(i, (i + distance) % size) for i in range(size)])


def from_sides(last, first):
    return ring(last, "space", 1), ring(first, "space", -1)


def swapped(block, axis, offset):
    size = lax.axis_size(axis)
    pairs = [(i % size, (i + 1) % size) for i in range(offset, size + offset, 2)]
    return lax.ppermute(block, axis, pairs + [(j, i) for i, j in pairs])


def shards(initial, prior, conductivity):
    times = lax.axis_size("tm")
    own_prior = prior[0]
    home = times - 1
    ny = initial.shape[1]
    cut = ny * CUT[0] // CUT[1]
    wide = cut + OVERLAP
    windows = [(0, wide), (cut - OVERLAP, ny)]
    results = [(0, cut), (cut, ny)]
    start = windows[1][0]

    received = ring(rows_from(own_prior, start), "tm", 1)
    cond, upper, down, up = first_block(initial, own_prior, conductivity, wide)
    before, after = from_sides(up, down)
    coefficients = prepare_fine(cond)
    coarse_cond, initial_rows = coarse_and_initial(cond, initial, start)
    lower, lower_part, down, up = lower_start(initial_rows, received, windows[1], coefficients, coarse_cond, before)
    before_2, after_2 = from_sides(up, down)
    own_coarse = restricted(own_prior)
    next_coarse = ring(own_coarse, "tm", -1)

    conds = (before, after)
    rows = ny - start
    sides = [
        [[(x, at), (x, at + size)] for x in pair]
        for pair, at, size in ((conds, ny, wide), ((before_2, after_2), 0, rows))
    ]
    parts = [half_step(upper, windows[0], coefficients), lower_part]
    middle = [
        two_steps(state, parts[i], *sides[i], conds, cond, windows[i], windows[i], coefficients)
        for i, state in enumerate((upper, lower))
    ]
    coarse_coef = coarse_coefficients(coarse_cond, before_2, after_2, 2 * rows)
    received = [from_sides(up, down) for _, down, up in middle]
    ended = []
    for i, (state, _, _) in enumerate(middle):
        part = half_step(state, windows[i], coefficients, coarse_coef[:i])
        side = [[(x, 0), (x, x.shape[0] // 2)] for x in received[i]]
        ended.append(two_steps(state, part, *side, conds, cond, windows[i], results[i], coefficients, True))
    (moved, moved_coarse), (own_fine, fine_coarse) = ended

    jump = jumps_of(moved_coarse, fine_coarse, next_coarse, own_coarse)
    half_cut = cut // 2
    lower = ring(jump[:, half_cut:], "tm", -home)
    shifted = [jump] + [ring(jump, "tm", -j) for j in range(1, home)]
    shifted.append(jnp.concatenate([jump[:, :half_cut], lower], axis=1))
    sweep = sweep_start(shifted[0], shifted[1], half_cut, coarse_coef)
    _, early = lax.optimization_barrier((sweep[0], moved))
    moved_first = lax.ppermute(early, "tm", [(home, 0)])
    for j in range(home):
        state, part, on, off = sweep
        off, on = swapped(off, "space", 1), swapped(on, "space", 0)
        if j == 0:
            *_, moved = lax.optimization_barrier((on, off, lower, *shifted[2:home], moved))
            moved = lax.ppermute(moved, "tm", [(i, i + 1) for i in range(home)])
        more = (shifted[j + 1:j + 3], home - j - 1) if j < home - 1 else ()
        sweep = sweep_step(state, part, on, off, half_cut, coarse_coef, *more)
    update, tail, rest = finish_lower(own_fine, fine_coarse, own_prior, sweep[0])
    update, tail = finish_upper(moved_first, moved, sweep[0], rest, update, tail)
    return update[None], tail[None]


def solution(mesh):
    return jax.shard_map(
        shards,
        mesh=mesh,
        in_specs=(P("space", None, None), P("tm", "space", None, None), P("space", None, None)),
        out_specs=(P("tm", "space", None, None), P("tm", "space", None, None)),
        check_vma=False,
    )
```
